32 devices in a mesh: rows: 4 (over x, core), blk: 4 (over z), hd: 2 (over y).
Axes of the slice: x: 2, y: 2, z: 4, core: 2. Of those that a mesh axis runs over, the one named last changes fastest.
Arguments:
- tokens: bfloat16 [16, 1536, 512], P('rows', ('blk', 'hd')), may hold values from -6 to 6
- w_qkv: bfloat16 [512, 1536], P(('rows', 'blk', 'hd')), may hold values from -0.25 to 0.25
- w_gate: bfloat16 [512, 8], P(('rows', 'blk', 'hd')), may hold values from -0.25 to 0.25
- gate_bias: float32 [8], P('hd'), may hold values from 3 to 13
- w_out: bfloat16 [512, 512], P(('rows', 'blk', 'hd')), may hold values from -1 to 1
- w_up: bfloat16 [512, 2048], P(('rows', 'blk', 'hd')), may hold values from -0.25 to 0.25
- up_bias: bfloat16 [2048], P(('rows', 'blk', 'hd')), may hold values from -3 to 3
- w_down: bfloat16 [2048, 512], P(('rows', 'blk', 'hd')), may hold values from -0.125 to 0.125
- down_bias: bfloat16 [512], P(('rows', 'blk', 'hd')), may hold values from -3 to 3
- pre_gain: bfloat16 [512], P(('rows', 'blk', 'hd')), may hold values from 0.5 to 1.5
- pre_shift: bfloat16 [512], P(('rows', 'blk', 'hd')), may hold values from -3 to 3
- mid_gain: bfloat16 [512], P(('rows', 'blk', 'hd')), may hold values from 0.5 to 1.5
- mid_shift: bfloat16 [512], P(('rows', 'blk', 'hd')), may hold values from -3 to 3
- feature_map: bfloat16 [8, 64, 128], P('hd'), may hold values from -4 to 4
- state_init: float32 [16, 8, 256, 64], P('rows', 'hd'), may hold values from -3 to 3
- keysum_init: float32 [16, 8, 256], P('rows', 'hd'), may hold values from -0.2 to 0.2
- out_cot: bfloat16 [16, 1536, 512], P('rows', ('blk', 'hd')), may hold values from -6 to 6
- state_cot: float32 [16, 8, 256, 64], P('rows', 'hd'), may hold values from -6 to 6
- keysum_cot: float32 [16, 8, 256], P('rows', 'hd'), may hold values from -6 to 6
Outputs:
- output: bfloat16 [16, 1536, 512], P('rows', ('blk', 'hd'))
- tokens_grad: bfloat16 [16, 1536, 512], P('rows', ('blk', 'hd'))
- qkv_grad: float32 [512, 1536], P(('rows', 'blk', 'hd'))
- gate_grad: float32 [512, 8], P(('rows', 'blk', 'hd'))
- gatebias_grad: float32 [8], P('hd')
- outproj_grad: float32 [512, 512], P(('rows', 'blk', 'hd'))
- up_grad: float32 [512, 2048], P(('rows', 'blk', 'hd'))
- upbias_grad: float32 [2048], P(('rows', 'blk', 'hd'))
- down_grad: float32 [2048, 512], P(('rows', 'blk', 'hd'))
- downbias_grad: float32 [512], P(('rows', 'blk', 'hd'))
- pregain_grad: float32 [512], P(('rows', 'blk', 'hd'))
- preshift_grad: float32 [512], P(('rows', 'blk', 'hd'))
- midgain_grad: float32 [512], P(('rows', 'blk', 'hd'))
- midshift_grad: float32 [512], P(('rows', 'blk', 'hd'))
- state_final: float32 [16, 8, 256, 64], P('rows', 'hd')
- keysum_final: float32 [16, 8, 256], P('rows', 'hd')
- state_grad: float32 [16, 8, 256, 64], P('rows', 'hd')
- keysum_grad: float32 [16, 8, 256], P('rows', 'hd')
The draws below stay inside these ranges and needn't reach their ends.
All inputs are finite; a program needn't handle non-finite values.
Results may differ from the reference program's by a relative error of at most 0.014.
The reference program's roundings to bfloat16 on the way count: a program that leaves them out, or rounds other values in their place, can miss the bound.
Values may be sent and summed in bfloat16 or wider, within the bound.
No kernel may reach another device: no remote copies, remote signals or barrier semaphores. Data moves between devices by JAX's collectives and lax.ppermute only.
A program may use at most 192 MiB of HBM per device.

```python
import math
import jax
import jax.numpy as jnp
from jax import lax

D = 512
HEADS = 8
HEAD_DIM = 64
RAND_FEATS = 128
FF = 2048
FEAT_DIM = 256
TILE = 128
LENGTH = 1536
NSEQ = 16


def draw_gate_bias(key, part):
    key = jax.random.fold_in(key, 7)
    first, second, third = jax.random.split(key, 3)
    share = 0.5
    quick = jax.random.uniform(first, (HEADS,), jnp.float32) < share
    fast = jnp.log(32.0) + jnp.log(1.5) * jax.random.uniform(second, (HEADS,), jnp.float32)
    slow = jnp.log(1.0 * LENGTH) + 2.0 * jax.random.uniform(third, (HEADS,), jnp.float32)
    return jnp.where(quick, fast, slow).astype(jnp.float32)


def draw_keysum_init(key, part):
    key = jax.random.fold_in(key, 11)
    first, second = jax.random.split(key)
    sine = jnp.clip(0.03 * jax.random.normal(first, (NSEQ, HEADS, RAND_FEATS), jnp.float32), -0.15, 0.15)
    cosine = 0.12 * jax.random.uniform(second, (NSEQ, HEADS, RAND_FEATS), jnp.float32, 0.5, 1.5)
    return jnp.concatenate([sine, cosine], axis=-1)


def levels(key, extent, shards, least, largest):
    level = 1.0
    for axis_at, shards_of in shards:
        steps = jax.random.uniform(jax.random.fold_in(jax.random.fold_in(key, 6), axis_at), (shards_of,), jnp.float32, least / len(shards), largest / len(shards))
        level = level * jnp.repeat(jnp.exp(steps), extent[axis_at] // shards_of).reshape((-1,) + (1,) * (len(extent) - 1 - axis_at))
    return level


def gaussian(own_key, extent, scale, bound, cuts=(), held_as=jnp.bfloat16):
    factor_of = levels(own_key, extent, cuts, -0.22, 0.18) if cuts else 1.0
    entries = jax.random.normal(own_key, extent, jnp.float32) * scale * factor_of
    return jnp.minimum(jnp.maximum(entries, -bound), bound).astype(held_as)


def setup_inputs(seed: int = 0) -> dict:
    seeds = jax.random.split(jax.random.key(seed), 20)
    return {
        "tokens": gaussian(seeds[0], (NSEQ, LENGTH, D), 1.0, 6.0, ((0, 4), (1, 8))),
        "w_qkv": gaussian(seeds[1], (D, 3 * D), D ** -0.5, 0.25, ((0, 32),)),
        "w_gate": gaussian(seeds[2], (D, HEADS), D ** -0.5, 0.25, ((0, 32),)),
        "gate_bias": draw_gate_bias(jax.random.fold_in(seeds[19], 71), 0),
        "w_out": gaussian(seeds[4], (D, D), (D // 16) ** -0.5, 1.0, ((0, 32),)),
        "w_up": gaussian(seeds[5], (D, FF), D ** -0.5, 0.25, ((0, 32),)),
        "up_bias": gaussian(seeds[6], (FF,), 0.5, 3.0, ((0, 32),)),
        "w_down": gaussian(seeds[7], (FF, D), FF ** -0.5, 0.125, ((0, 32),)),
        "down_bias": gaussian(seeds[8], (D,), 0.5, 3.0, ((0, 32),)),
        "pre_gain": jnp.clip(1.0 + 0.1 * jax.random.normal(seeds[9], (D,), jnp.float32), 0.5, 1.5).astype(jnp.bfloat16),
        "pre_shift": gaussian(seeds[10], (D,), 0.5, 3.0, ((0, 32),)),
        "mid_gain": jnp.clip(1.0 + 0.1 * jax.random.normal(seeds[11], (D,), jnp.float32), 0.5, 1.5).astype(jnp.bfloat16),
        "mid_shift": gaussian(seeds[12], (D,), 0.5, 3.0, ((0, 32),)),
        "feature_map": gaussian(seeds[13], (HEADS, HEAD_DIM, RAND_FEATS), 1.0, 4.0, ((0, 2),)),
        "state_init": gaussian(seeds[14], (NSEQ, HEADS, FEAT_DIM, HEAD_DIM), 0.5, 3.0, ((0, 4), (1, 2)), jnp.float32),
        "keysum_init": draw_keysum_init(jax.random.fold_in(seeds[19], 71), 0),
        "out_cot": gaussian(seeds[16], (NSEQ, LENGTH, D), 1.0, 6.0, ((0, 4), (1, 8))),
        "state_cot": gaussian(seeds[17], (NSEQ, HEADS, FEAT_DIM, HEAD_DIM), 1.0, 6.0, ((0, 4), (1, 2)), jnp.float32),
        "keysum_cot": gaussian(seeds[18], (NSEQ, HEADS, FEAT_DIM), 1.0, 6.0, ((0, 4), (1, 2)), jnp.float32),
    }


@jax.custom_vjp
def low(v):
    return lax.optimization_barrier(v.astype(jnp.bfloat16)).astype(jnp.float32)

@jax.custom_vjp
def low_back(v):
    return v

def low_keep(v):
    return (low(v), None)

def low_pass(kept, grad):
    return (grad,)

def back_keep(v):
    return (v, None)

def back_low(kept, grad):
    return (low(grad),)
low.defvjp(low_keep, low_pass)
low_back.defvjp(back_keep, back_low)
HIGH = lax.Precision.HIGHEST

def layer_norm(values, gain, shift):
    average = lax.optimization_barrier(jnp.mean(values, axis=-1, keepdims=True))
    centered = values - average
    variance = lax.optimization_barrier(jnp.mean(centered * centered, axis=-1, keepdims=True))
    return centered * lax.rsqrt(variance + 1e-05) * gain + shift

def unit_rows(values):
    return values * lax.rsqrt(lax.optimization_barrier(jnp.sum(values * values, axis=-1, keepdims=True)) + 1e-06)

def waves(angles):
    scale = 1.0 / math.sqrt(angles.shape[-1])
    return jnp.concatenate([jnp.sin(angles), jnp.cos(angles)], axis=-1) * scale

def smooth(values):
    return jax.nn.gelu(values, approximate=False)

def tile_step(carry, inputs):
    state, keysum = carry
    query_feat, key_feat, values, keep, fresh = inputs
    width = keep.shape[0]
    running = jnp.cumsum(keep, axis=0)
    lower = jnp.arange(width)[:, None] >= jnp.arange(width)[None, :]
    gaps = running.T[:, :, None] - running.T[:, None, :]
    weights = jnp.where(lower, jnp.exp(jnp.where(lower, gaps, 0.0)), 0.0) * fresh.T[:, None, :]
    scores = jnp.einsum('thf,jhf->htj', query_feat, key_feat, precision=HIGH) * weights
    decay = jnp.exp(running)
    numer = jnp.einsum('htj,jhe->the', scores, values, precision=HIGH)
    numer = numer + decay[:, :, None] * jnp.einsum('thf,hfe->the', query_feat, state, precision=HIGH)
    denom = lax.optimization_barrier(jnp.sum(scores, axis=-1)).T + decay * jnp.einsum('thf,hf->th', query_feat, keysum, precision=HIGH)
    floor = jax.nn.softplus(4.0 * denom) * 0.25 + 0.1
    mixed = numer / floor[:, :, None]
    tail = jnp.exp(running[-1][None, :] - running) * fresh
    carry_decay = jnp.exp(running[-1])
    new_state = carry_decay[:, None, None] * state + jnp.einsum('jhf,jhe->hfe', key_feat * tail[:, :, None], values, precision=HIGH)
    new_keysum = carry_decay[:, None] * keysum + jnp.einsum('jhf,jh->hf', key_feat, tail, precision=HIGH)
    return ((new_state, new_keysum), mixed)

def recurrence(query_feat, key_feat, values, keep, fresh, state, keysum):
    length = query_feat.shape[0]
    count = length // TILE

    def split(array):
        return array.reshape((count, TILE) + array.shape[1:])
    carry, mixed = lax.scan(jax.checkpoint(tile_step), (state, keysum), (split(query_feat), split(key_feat), split(values), split(keep), split(fresh)))
    return (mixed.reshape((length,) + mixed.shape[2:]), carry)

def forward(tokens, state, keysum, w_qkv, w_gate, gate_bias, w_out, w_up, up_bias, w_down, down_bias, pre_gain, pre_shift, mid_gain, mid_shift, feature_map):
    length = tokens.shape[0]
    normed = low(layer_norm(tokens, pre_gain, pre_shift))
    packed = low(low_back(jnp.dot(normed, w_qkv, precision=HIGH)))
    gate_raw = low(low_back(jnp.dot(normed, w_gate, precision=HIGH)))
    packed = packed.reshape(length, HEADS, 3, HEAD_DIM)
    query = packed[:, :, 0]
    key_raw = packed[:, :, 1]
    values = packed[:, :, 2]
    query_angle = low_back(jnp.einsum('lhe,hem->lhm', low(unit_rows(query)), feature_map, precision=HIGH))
    key_angle = low_back(jnp.einsum('lhe,hem->lhm', low(unit_rows(key_raw)), feature_map, precision=HIGH))
    query_feat = low(waves(query_angle))
    key_feat = low(waves(key_angle))
    logit = gate_raw + gate_bias
    keep = jax.nn.log_sigmoid(logit)
    fresh = jax.nn.sigmoid(-logit)
    mixed, (final_state, final_keysum) = recurrence(query_feat, key_feat, values, keep, fresh, state, keysum)
    mixed = low(low_back(mixed.reshape(length, D)))
    attended = tokens + low_back(jnp.dot(mixed, w_out, precision=HIGH))
    hidden = low(layer_norm(attended, mid_gain, mid_shift))
    before = low_back(jnp.dot(hidden, w_up, precision=HIGH) + up_bias)
    active = low(smooth(before))
    result = attended + jnp.dot(active, w_down, precision=HIGH) + down_bias
    return (result, final_state, final_keysum)

def reference(tokens, w_qkv, w_gate, gate_bias, w_out, w_up, up_bias, w_down, down_bias, pre_gain, pre_shift, mid_gain, mid_shift, feature_map, state_init, keysum_init, out_cot, state_cot, keysum_cot):
    params = (w_qkv.astype(jnp.float32), w_gate.astype(jnp.float32), gate_bias.astype(jnp.float32), w_out.astype(jnp.float32), w_up.astype(jnp.float32), up_bias.astype(jnp.float32), w_down.astype(jnp.float32), down_bias.astype(jnp.float32), pre_gain.astype(jnp.float32), pre_shift.astype(jnp.float32), mid_gain.astype(jnp.float32), mid_shift.astype(jnp.float32))
    directions = feature_map.astype(jnp.float32)

    def local(seq_tokens, seq_state, seq_keysum, *weights):
        return forward(seq_tokens, seq_state, seq_keysum, *weights, directions)

    def one(total, item):
        seq_tokens, seq_state, seq_keysum, seq_cot, seq_state_cot, seq_keysum_cot = item
        outs, pullback = jax.vjp(local, seq_tokens.astype(jnp.float32), seq_state, seq_keysum, *params)
        grads = pullback((seq_cot.astype(jnp.float32), seq_state_cot, seq_keysum_cot))
        total = tuple((acc + grad for acc, grad in zip(total, grads[3:])))
        return (total, (outs[0].astype(jnp.bfloat16), grads[0].astype(jnp.bfloat16), outs[1], outs[2], grads[1], grads[2]))
    zeros = tuple((jnp.zeros(param.shape, jnp.float32) for param in params))
    total, stacked = lax.scan(one, zeros, (tokens, state_init, keysum_init, out_cot, state_cot, keysum_cot))
    output, tokens_grad, state_final, keysum_final, state_grad, keysum_grad = stacked
    return (output, tokens_grad, total[0], total[1], total[2], total[3], total[4], total[5], total[6], total[7], total[8], total[9], total[10], total[11], state_final, keysum_final, state_grad, keysum_grad)
```

```python
import functools
import math

import jax
import jax.numpy as jnp
from jax import lax
from jax.experimental import pallas as pl
from jax.experimental.pallas import tpu as pltpu
from jax.sharding import PartitionSpec as P

ALL = ("rows", "blk", "hd")
BOTH = ("blk", "hd")
F32 = jnp.float32
BF16 = jnp.bfloat16
AUG = 16
ROWS = 8


def flip(x, axis, size, bit):
    return lax.ppermute(x, axis, [(i, i ^ bit) for i in range(size)])


def ordered(parts, me):
    parts = list(parts)
    bit = 1
    while bit < len(parts):
        there = (me & bit) != 0
        parts = [jnp.where(there, parts[i ^ bit], parts[i]) for i in range(len(parts))]
        bit *= 2
    return parts


def swap_pieces(x, axis, size, group, me):
    parts = [lax.dynamic_index_in_dim(x, me, 0, False)]
    for k in range(1, group):
        parts.append(flip(lax.dynamic_index_in_dim(x, me ^ k, 0, False), axis, size, k))
    return ordered(parts, me)


def bits_of(sizes):
    found = []
    for axis in ALL:
        bit = sizes[axis] // 2
        while bit:
            found.append((axis, sizes[axis], bit))
            bit //= 2
    return found


def gather_order(sizes):
    order = [b for b in bits_of(sizes) if b[0] == "blk"]
    order += [b for b in bits_of(sizes) if b[0] == "hd"]
    order += [b for b in bits_of(sizes) if b[0] == "rows"]
    return order


def gather_all(x, sizes):
    bits = bits_of(sizes)
    cur = x.reshape((1,) * len(bits) + x.shape)
    for entry in gather_order(sizes):
        axis, size, bit = entry
        dim = bits.index(entry)
        got = flip(cur, axis, size, bit)
        there = (lax.axis_index(axis) & bit) != 0
        cur = jnp.where(
            there,
            jnp.concatenate([got, cur], axis=dim),
            jnp.concatenate([cur, got], axis=dim),
        )
    return cur.reshape((-1,) + x.shape[1:])


def scatter_sum(x, sizes):
    bits = bits_of(sizes)
    cur = x.reshape((2,) * len(bits) + x.shape[1:])
    for entry in reversed(gather_order(sizes)):
        axis, size, bit = entry
        dim = bits.index(entry)
        mine = ((lax.axis_index(axis) & bit) != 0).astype(jnp.int32)
        got = flip(lax.dynamic_index_in_dim(cur, 1 - mine, dim, True), axis, size, bit)
        own = lax.dynamic_index_in_dim(cur, mine, dim, True)
        cur = (own.astype(F32) + got.astype(F32)).astype(BF16)
    return cur.reshape(x.shape[1:]).astype(F32)


def sum_all(x, sizes):
    for axis, size, bit in bits_of(sizes):
        x = x + flip(x, axis, size, bit)
    return x


def dot(a, b, contract):
    return lax.dot_general(a, b, ((contract[:1], contract[1:]), ((), ())), preferred_element_type=F32)


def sine_cosine(x):
    turns = jnp.round(x * (1.0 / math.pi))
    rest = x - turns * 3.140625
    rest = rest - turns * 9.67502593994140625e-4
    rest = rest - turns * 1.50995788317e-7
    half = turns * 0.5
    odd = half - jnp.floor(half)
    sign = 1.0 - 4.0 * odd
    sq = rest * rest
    sine = sq * (-2.5052108385e-8) + 2.7557319224e-6
    sine = sine * sq - 1.9841269841e-4
    sine = sine * sq + 8.3333333333e-3
    sine = sine * sq - 1.6666666667e-1
    sine = rest + rest * (sq * sine)
    cosine = sq * 2.0876756988e-9 - 2.7557319224e-7
    cosine = cosine * sq + 2.4801587302e-5
    cosine = cosine * sq - 1.3888888889e-3
    cosine = cosine * sq + 4.1666666667e-2
    cosine = cosine * sq - 0.5
    cosine = cosine * sq + 1.0
    return sine * sign, cosine * sign


def lanes(x, width):
    return jnp.concatenate([x] * (width // x.shape[1]), axis=1) if width > x.shape[1] else x


def augmented(v, ones):
    width = v.shape[1]
    place = lax.broadcasted_iota(jnp.int32, (AUG, width), 0)
    extra = jnp.where(place == 0, ones, 0.0)
    return jnp.concatenate([v.astype(F32), extra], axis=0)


def lower_mask(c):
    return lax.broadcasted_iota(jnp.int32, (c, c), 0) <= lax.broadcasted_iota(jnp.int32, (c, c), 1)


def gate_kernel(tile, raw_ref, bias_ref, out_ref):
    logit = raw_ref[...].astype(F32) + bias_ref[...]
    heads, width = logit.shape
    small = jnp.log1p(jnp.exp(-jnp.abs(logit)))
    keep = jnp.minimum(logit, 0.0) - small
    slow = jnp.minimum(-logit, 0.0) - small
    place = lax.broadcasted_iota(jnp.int32, (heads, width), 1)

    def sums(x, within):
        at = lax.rem(place, within)
        step = 1
        while step < within:
            x = x + jnp.where(at >= step, pltpu.roll(x, step, 1), 0.0)
            step *= 2
        return x

    running = sums(keep, tile)
    whole = running
    offset = jnp.zeros((heads, 1), F32)
    for at in range(0, width, tile):
        whole = jnp.where((place >= at) & (place < at + tile), running + offset, whole)
        offset = offset + running[:, at + tile - 1 : at + tile]
    out_ref[0] = running
    out_ref[1] = slow - running
    out_ref[2] = whole
    out_ref[3] = jnp.exp(slow)
    out_ref[4] = jnp.exp(keep)
    out_ref[5] = jnp.broadcast_to(offset, (heads, width))
    out_ref[6] = keep
    out_ref[7] = slow


def features(unit, fmt, scale):
    sine, cosine = sine_cosine(dot(fmt, unit, (1, 0)))
    return (jnp.concatenate([sine, cosine], axis=0) * scale).astype(BF16)


def forward_kernel(tile, qkv_ref, fmt_ref, rows_ref, col_ref, qf_ref, kf_ref, nu_ref, state_ref):
    width = qkv_ref.shape[-1]
    fmt = fmt_ref[0]
    scale = 1.0 / math.sqrt(fmt.shape[0])
    mask = lower_mask(tile)
    state = None
    for at in range(0, width, tile):
        here = pl.ds(at, tile)
        query = qkv_ref[0, 0, :, here].astype(F32)
        key = qkv_ref[1, 0, :, here].astype(F32)
        query = (query * lax.rsqrt(jnp.sum(query * query, axis=0, keepdims=True) + 1e-06)).astype(BF16)
        key = (key * lax.rsqrt(jnp.sum(key * key, axis=0, keepdims=True) + 1e-06)).astype(BF16)
        qf = features(query, fmt, scale)
        kf = features(key, fmt, scale)
        qf_ref[0, :, here] = qf
        kf_ref[0, :, here] = kf
        running = rows_ref[0, 0:1, here]
        lead = rows_ref[0, 1:2, here]
        last = running[:, tile - 1 : tile]
        values = augmented(qkv_ref[2, 0, :, here], 1.0)
        weights = jnp.where(mask, jnp.exp(running + lanes(col_ref[0, here, :], tile)), 0.0)
        scores = (dot(kf, qf, (0, 0)) * weights).astype(BF16)
        numer = dot(values.astype(BF16), scores, (1, 0))
        if state is not None:
            numer = numer + jnp.exp(running) * dot(state.astype(BF16), qf, (1, 0))
        nu_ref[0, :, here] = numer[: nu_ref.shape[1]]
        tail = (values * jnp.exp(last + lead)).astype(BF16)
        new = dot(tail, kf, (1, 1))
        state = new if state is None else jnp.exp(last) * state + new
    state_ref[0] = state


def enter_kernel(state_ref, qf_ref, rows_ref, nu_ref, mixed_ref, total_ref):
    state = state_ref[0]
    high = state.astype(BF16)
    rest = (state - high.astype(F32)).astype(BF16)
    qf = qf_ref[0]
    rows = nu_ref.shape[1]
    extra = (dot(high, qf, (1, 0)) + dot(rest, qf, (1, 0)))[:rows]
    total = nu_ref[0] + jnp.exp(rows_ref[0, 2:3, :]) * extra
    total_ref[0] = total
    size = mixed_ref.shape[1]
    denom = total[size : size + 1]
    floor = softplus(4.0 * denom) * 0.25 + 0.1
    mixed_ref[0] = (total[:size] / floor).astype(BF16)


def softplus(x):
    return jnp.maximum(x, 0.0) + jnp.log1p(jnp.exp(-jnp.abs(x)))


def leave_kernel(grad_ref, total_ref, qf_ref, rows_ref, a_ref, back_ref):
    grad = grad_ref[0].astype(F32)
    size = grad.shape[0]
    numer = total_ref[0, :size]
    denom = total_ref[0, size : size + 1]
    inverse = 1.0 / (softplus(4.0 * denom) * 0.25 + 0.1)
    inner = jnp.sum(grad * numer, axis=0, keepdims=True)
    by_denom = -inner * jax.nn.sigmoid(4.0 * denom) * inverse * inverse
    whole = augmented(grad * inverse, by_denom)
    a_ref[0] = whole.astype(BF16)
    back_ref[0] = dot((whole * jnp.exp(rows_ref[0, 2:3, :])).astype(BF16), qf_ref[0], (1, 1))


def unit_back(raw, unit_grad):
    inverse = lax.rsqrt(jnp.sum(raw * raw, axis=0, keepdims=True) + 1e-06)
    inner = jnp.sum(raw * unit_grad, axis=0, keepdims=True)
    return inverse * (unit_grad - raw * (inner * inverse * inverse))


def angle_back(feat, grad):
    half = feat.shape[0] // 2
    feat = feat.astype(F32)
    return (grad[:half] * feat[half:] - grad[half:] * feat[:half]).astype(BF16)


def backward_kernel(
    tile, qkv_ref, fm_ref, rows_ref, col_ref, qf_ref, kf_ref, a_ref, state_ref, back_ref, out_ref, logit_ref
):
    width = qkv_ref.shape[-1]
    size = qkv_ref.shape[2]
    fm = fm_ref[0]
    mask = lower_mask(tile)
    spots = list(range(0, width, tile))
    states = [state_ref[0]]
    for at in spots:
        here = pl.ds(at, tile)
        last = rows_ref[0, 0:1, at + tile - 1 : at + tile]
        values = augmented(qkv_ref[2, 0, :, here], 1.0)
        tail = (values * jnp.exp(last + rows_ref[0, 1:2, here])).astype(BF16)
        states.append(jnp.exp(last) * states[-1] + dot(tail, kf_ref[0, :, here], (1, 1)))
    back = back_ref[0]
    ones = jnp.ones((AUG, tile), BF16)

    def whole_sum(x):
        return jnp.sum(jnp.sum(x, axis=0, keepdims=True), axis=1, keepdims=True)

    pieces = []
    for index in reversed(range(len(spots))):
        at = spots[index]
        here = pl.ds(at, tile)
        running = rows_ref[0, 0:1, here]
        lead = rows_ref[0, 1:2, here]
        last = running[:, tile - 1 : tile]
        decay = jnp.exp(running)
        tail = jnp.exp(last + lead)
        qf = qf_ref[0, :, here]
        kf = kf_ref[0, :, here]
        a = a_ref[0, :, here]
        values = augmented(qkv_ref[2, 0, :, here], 1.0).astype(BF16)
        state = states[index].astype(BF16)
        low_back = back.astype(BF16)
        weights = jnp.where(mask, jnp.exp(running + lanes(col_ref[0, here, :], tile)), 0.0)
        alike = dot(kf, qf, (0, 0))
        scores = (alike * weights).astype(BF16)
        pairs = dot(values, a, (0, 0)) * weights
        terms = (pairs * alike).astype(BF16)
        pairs = pairs.astype(BF16)
        from_state = decay * dot(state, a, (0, 0))
        from_back = tail * dot(low_back, values, (0, 0))
        query_feat = dot(kf, pairs, (1, 0)) + from_state
        key_feat = dot(qf, pairs, (1, 1)) + from_back
        by_query = dot(ones, terms, (1, 0))[:1]
        by_key = dot(ones, terms, (1, 1))[:1]
        state_term = jnp.sum(qf.astype(F32) * from_state, axis=0, keepdims=True)
        back_term = jnp.sum(kf.astype(F32) * from_back, axis=0, keepdims=True)
        through = jnp.exp(last) * whole_sum(back * states[index])
        constant = jnp.sum(back_term, axis=1, keepdims=True) + through
        pieces.append((by_query - by_key + state_term - back_term, by_key + back_term, constant))
        value = dot(a[:size], scores, (1, 1)) + tail * dot(low_back[:size], kf, (1, 0))
        query_unit = dot(fm, angle_back(qf, query_feat), (1, 0))
        key_unit = dot(fm, angle_back(kf, key_feat), (1, 0))
        out_ref[0, 0, :, here] = unit_back(qkv_ref[0, 0, :, here].astype(F32), query_unit).astype(BF16)
        out_ref[1, 0, :, here] = unit_back(qkv_ref[1, 0, :, here].astype(F32), key_unit).astype(BF16)
        out_ref[2, 0, :, here] = value.astype(BF16)
        back = jnp.exp(last) * back + dot((a.astype(F32) * decay).astype(BF16), qf, (1, 1))
    place = lax.broadcasted_iota(jnp.int32, (ROWS, tile), 0)
    sums = jnp.zeros((ROWS, tile), F32)
    for index, piece in enumerate(pieces[::-1]):
        sums = jnp.where(place == index, piece[0], sums)
    place = lax.broadcasted_iota(jnp.int32, (ROWS, tile), 1)
    step = 1
    while step < tile:
        sums = sums + jnp.where(place < tile - step, pltpu.roll(sums, tile - step, 1), 0.0)
        step *= 2
    for index, (_, by_key, constant) in enumerate(pieces[::-1]):
        here = pl.ds(spots[index], tile)
        keep_grad = sums[index : index + 1] + constant
        logit = keep_grad * rows_ref[0, 3:4, here] - by_key * rows_ref[0, 4:5, here]
        logit_ref[0, :, here] = jnp.broadcast_to(logit, (ROWS, tile))


def per_head(kernel, outs, *arrays, flops=1e9):
    heads = arrays[0][0].shape[arrays[0][1]]

    def spec(shape, at):
        block = tuple(1 if i == at else n for i, n in enumerate(shape))
        return pl.BlockSpec(block, lambda h, at=at, n=len(shape): tuple(h if i == at else 0 for i in range(n)))

    nbytes = sum(a.size * a.dtype.itemsize for a, _ in arrays)
    nbytes += sum(math.prod(s) * jnp.dtype(d).itemsize for s, d, _ in outs)
    return pl.pallas_call(
        kernel,
        grid=(heads,),
        in_specs=[spec(a.shape, at) for a, at in arrays],
        out_specs=[spec(s, at) for s, _, at in outs],
        out_shape=[jax.ShapeDtypeStruct(s, d) for s, d, _ in outs],
        compiler_params=pltpu.CompilerParams(vmem_limit_bytes=48 * 2**20),
        cost_estimate=pl.CostEstimate(flops=int(flops), bytes_accessed=int(nbytes), transcendentals=0),
    )(*[a for a, _ in arrays])


def norm_parts(x):
    average = jnp.mean(x, axis=0, keepdims=True)
    centered = x - average
    inverse = lax.rsqrt(jnp.mean(centered * centered, axis=0, keepdims=True) + 1e-05)
    return centered * inverse, inverse


def norm_back(hat, inverse, gain, grad):
    scaled = grad * gain
    first = jnp.mean(scaled, axis=0, keepdims=True)
    second = jnp.mean(scaled * hat, axis=0, keepdims=True)
    return (scaled - first - hat * second) * inverse


def product(spec, a, b):
    return jnp.einsum(spec, a, b, preferred_element_type=F32)


def local(
    tokens, w_qkv, w_gate, gate_bias, w_out, w_up, up_bias, w_down, down_bias, pre_gain, pre_shift,
    mid_gain, mid_shift, feature_map, state_init, keysum_init, out_cot, state_cot, keysum_cot,
):
    sizes = {axis: lax.axis_size(axis) for axis in ALL}
    count_hd, count_blk = sizes["hd"], sizes["blk"]
    devices = sizes["rows"] * count_blk * count_hd
    both = count_blk * count_hd
    seqs, part, width = tokens.shape
    own_heads, head_dim, rand = feature_map.shape
    heads = own_heads * count_hd
    feat = 2 * rand
    hidden_size = w_up.shape[1]
    length = seqs * part
    tile = 256 if length % 256 == 0 else 128
    shard = w_qkv.shape[0]
    aug = head_dim + AUG
    place_hd, place_blk = lax.axis_index("hd"), lax.axis_index("blk")
    place = place_blk * count_hd + place_hd
    member, chunk = place % seqs, place // seqs
    chunks = both // seqs

    def to_chunk(x):
        return jnp.stack(swap_pieces(x, BOTH, both, seqs, member)).reshape(length, width)

    def from_chunk(x):
        return jnp.stack(swap_pieces(x.reshape(seqs, part, width), BOTH, both, seqs, member))

    columns = w_qkv.reshape(shard, heads, 3, head_dim).transpose(0, 2, 1, 3).reshape(shard, 3 * width)
    per_row = hidden_size // width
    small = jnp.concatenate(
        [w_gate, up_bias.reshape(shard, per_row)]
        + [v.reshape(shard, 1) for v in (down_bias, pre_gain, pre_shift, mid_gain, mid_shift)],
        axis=1,
    )
    n_small = small.shape[1]
    small = jnp.pad(small, ((0, 0), (0, -n_small % 128)))
    first = gather_all(jnp.concatenate([columns, small], axis=1), sizes)
    full_qkv = first[:, : 3 * width]
    full_small = first[:, 3 * width :]
    full_gate = full_small[:, :heads]
    full_up_bias = full_small[:, heads : heads + per_row].reshape(hidden_size, 1).astype(F32)
    vectors = [full_small[:, heads + per_row + i : heads + per_row + i + 1].astype(F32) for i in range(5)]
    full_down_bias, gain_1, shift_1, gain_2, shift_2 = vectors
    x = to_chunk(tokens).T.astype(F32)

    fm = jnp.stack(ordered([feature_map] + [flip(feature_map, "hd", count_hd, k) for k in range(1, count_hd)], place_hd))
    fm = fm.reshape(heads, head_dim, rand)
    fmt = fm.transpose(0, 2, 1)
    bias = jnp.broadcast_to(gate_bias[:, None], (own_heads, 128))
    bias = jnp.stack(ordered([bias] + [flip(bias, "hd", count_hd, k) for k in range(1, count_hd)], place_hd))
    bias = bias.reshape(heads, 128)[:, :1]

    def lines(state, keysum):
        lead = state.shape[:-3]
        n = state.shape[-3]
        rows = jnp.swapaxes(state, -1, -2).reshape(lead + (n * head_dim, feat))
        return jnp.concatenate([rows, keysum], axis=-2)

    def unlines(rows, n):
        lead = rows.shape[:-2]
        return rows[..., : n * head_dim, :].reshape(lead + (n, head_dim, feat)), rows[..., n * head_dim :, :]

    def stacked(state, keysum):
        zeros = jnp.zeros((heads, AUG - 1, feat), F32)
        return jnp.concatenate([state.astype(F32), keysum.astype(F32)[:, None], zeros], axis=1)

    def flat(x):
        return jnp.concatenate([x[:, :head_dim].reshape(heads * head_dim, feat), x[:, head_dim]], axis=0)

    def unflat(rows):
        return stacked(*unlines(rows, heads))

    begin, end = lines(state_init, keysum_init), lines(state_cot, keysum_cot)
    offers = []
    for other in range(count_hd):
        spot = place_blk * count_hd + other
        pick = lambda a: lax.dynamic_index_in_dim(a, spot % seqs, 0, False)
        offers.append(jnp.where(spot // seqs == 0, pick(begin), pick(end)))
    edges = [unlines(e, own_heads) for e in swap_pieces(jnp.stack(offers), "hd", count_hd, count_hd, place_hd)]
    edge = stacked(jnp.concatenate([e[0] for e in edges]), jnp.concatenate([e[1] for e in edges]))

    def hop(x, forward):
        pairs = [(i, i + seqs) for i in range(both - seqs)]
        pairs = pairs if forward else [(b, a) for a, b in pairs]
        return unflat(lax.ppermute(flat(x).astype(BF16), BOTH, pairs).astype(F32))

    hat_1, inverse_1 = norm_parts(x)
    normed = (hat_1 * gain_1 + shift_1).astype(BF16)
    packed = product("dc,dt->ct", full_qkv, normed).astype(BF16).reshape(3, heads, head_dim, length)
    raw = product("dh,dt->ht", full_gate, normed).astype(BF16)
    gates = pl.pallas_call(
        functools.partial(gate_kernel, tile),
        out_shape=jax.ShapeDtypeStruct((8, heads, length), F32),
    )(raw, bias)
    col = jnp.broadcast_to(gates[1][:, :, None], (heads, length, 128))
    decay = jnp.exp(gates[5][:, :1])[:, :, None]
    rows = gates.transpose(1, 0, 2)

    qf, kf, partial_nu, chunk_state = per_head(
        functools.partial(forward_kernel, tile),
        [
            ((heads, feat, length), BF16, 0),
            ((heads, feat, length), BF16, 0),
            ((heads, head_dim + 8, length), F32, 0),
            ((heads, aug, feat), F32, 0),
        ],
        (packed, 1), (fmt, 0), (rows, 0), (col, 0), flops=6e9,
    )
    at_start = chunk == 0
    at_end = chunk == chunks - 1
    entering = edge
    for _ in range(chunks - 1):
        entering = jnp.where(at_start, edge, hop(chunk_state + decay * entering, True))
    leaving = chunk_state + decay * entering
    mixed, total_nu = per_head(
        enter_kernel,
        [((heads, head_dim, length), BF16, 0), ((heads, head_dim + 8, length), F32, 0)],
        (entering, 0), (qf, 0), (rows, 0), (partial_nu, 0),
    )
    mixed = mixed.reshape(width, length)

    second = gather_all(jnp.concatenate([w_out, w_up, w_down.reshape(shard, hidden_size)], axis=1), sizes)
    full_out = second[:, :width]
    full_up = second[:, width : width + hidden_size]
    full_down = second[:, width + hidden_size :].reshape(hidden_size, width)
    cot = to_chunk(out_cot).T

    attended = x + product("io,it->ot", full_out, mixed)
    hat_2, inverse_2 = norm_parts(attended)
    hidden = (hat_2 * gain_2 + shift_2).astype(BF16)
    before = product("df,dt->ft", full_up, hidden) + full_up_bias
    cumulative = 0.5 + 0.5 * lax.erf(before * math.sqrt(0.5))
    density = jnp.exp(-0.5 * before * before) * (1.0 / math.sqrt(2.0 * math.pi))
    active = (before * cumulative).astype(BF16)
    result = attended + product("fo,ft->ot", full_down, active) + full_down_bias
    output = from_chunk(result.astype(BF16).T)

    cot_full = cot.astype(F32)
    down_bias_grad = jnp.sum(cot_full, axis=1)
    down_grad = product("ft,ot->fo", active, cot)
    before_grad = (product("fo,ot->ft", full_down, cot) * (cumulative + before * density)).astype(BF16)
    up_bias_grad = jnp.sum(before_grad.astype(F32), axis=1)
    up_grad = product("dt,ft->df", hidden, before_grad)
    hidden_grad = product("df,ft->dt", full_up, before_grad)
    gain_2_grad = jnp.sum(hidden_grad * hat_2, axis=1)
    shift_2_grad = jnp.sum(hidden_grad, axis=1)
    attended_grad = cot_full + norm_back(hat_2, inverse_2, gain_2, hidden_grad)
    attended_low = attended_grad.astype(BF16)
    out_grad = product("it,ot->io", mixed, attended_low)
    mixed_grad = product("io,ot->it", full_out, attended_low).astype(BF16).reshape(heads, head_dim, length)

    a, chunk_back = per_head(
        leave_kernel,
        [((heads, aug, length), BF16, 0), ((heads, aug, feat), F32, 0)],
        (mixed_grad, 0), (total_nu, 0), (qf, 0), (rows, 0),
    )
    back = edge
    for _ in range(chunks - 1):
        back = jnp.where(at_end, edge, hop(chunk_back + decay * back, False))
    starting = chunk_back + decay * back
    packed_grad, logit_grad = per_head(
        functools.partial(backward_kernel, tile),
        [((3, heads, head_dim, length), BF16, 1), ((heads, ROWS, length), F32, 0)],
        (packed, 1), (fm, 0), (rows, 0), (col, 0), (qf, 0), (kf, 0), (a, 0), (entering, 0), (back, 0),
        flops=6e9,
    )
    packed_grad = packed_grad.reshape(3 * width, length)
    logit_grad = logit_grad[:, 0]
    gate_low = logit_grad.astype(BF16)
    bias_grad = jnp.sum(logit_grad, axis=1)

    qkv_grad = product("dt,ct->dc", normed, packed_grad)
    gate_grad = product("dt,ht->dh", normed, gate_low)
    normed_grad = product("dc,ct->dt", full_qkv, packed_grad) + product("dh,ht->dt", full_gate, gate_low)
    gain_1_grad = jnp.sum(normed_grad * hat_1, axis=1)
    shift_1_grad = jnp.sum(normed_grad, axis=1)
    token_grad = attended_grad + norm_back(hat_1, inverse_1, gain_1, normed_grad)
    token_grad = from_chunk(token_grad.astype(BF16).T)

    ends = flat(jnp.where(at_start, starting, leaving))
    state_part, keysum_part = unlines(ends.astype(BF16), heads)
    offers = jnp.concatenate(
        [state_part.reshape(count_hd, own_heads * head_dim, feat), keysum_part.reshape(count_hd, own_heads, feat)], axis=1
    )
    ends = jnp.stack(swap_pieces(offers, "hd", count_hd, count_hd, place_hd))
    ends = ordered([ends] + [flip(ends, "blk", count_blk, k) for k in range(1, count_blk)], place_blk)
    ends = jnp.stack(ends).reshape((both,) + offers.shape[1:]).astype(F32)

    def finished(rows):
        state, keysum = unlines(rows, own_heads)
        return jnp.swapaxes(state, -1, -2), keysum

    state_start, keysum_start = finished(ends[:seqs])
    state_final, keysum_final = finished(ends[both - seqs :])

    pieces = jnp.concatenate(
        [
            down_grad.astype(BF16).reshape(devices, -1),
            up_grad.astype(BF16).reshape(devices, -1),
        ],
        axis=1,
    )
    early = scatter_sum(pieces.reshape(devices, -1, width), sizes).reshape(-1)
    n_down = hidden_size * width // devices
    down_own = early[:n_down].reshape(-1, width)
    up_own = early[n_down:].reshape(shard, hidden_size)
    grad_small = jnp.concatenate(
        [gate_grad, up_bias_grad.reshape(width, per_row)]
        + [v[:, None] for v in (down_bias_grad, gain_1_grad, shift_1_grad, gain_2_grad, shift_2_grad)],
        axis=1,
    )
    grad_small = jnp.pad(grad_small, ((0, 0), (0, -n_small % 128)))
    late = jnp.concatenate([qkv_grad, out_grad, grad_small], axis=1).astype(BF16)
    late = scatter_sum(late.reshape(devices, shard, -1), sizes)
    qkv_own = late[:, : 3 * width].reshape(shard, 3, heads, head_dim).transpose(0, 2, 1, 3).reshape(shard, 3 * width)
    out_own = late[:, 3 * width : 4 * width]
    own_small = late[:, 4 * width :]
    gate_own = own_small[:, :heads]
    up_bias_own = own_small[:, heads : heads + per_row].reshape(-1)
    down_bias_own, gain_1_own, shift_1_own, gain_2_own, shift_2_own = (
        own_small[:, heads + per_row + i] for i in range(5)
    )
    bias_sum = sum_all(jnp.broadcast_to(bias_grad[:, None], (heads, 128)), sizes)[:, 0]
    bias_own = lax.dynamic_slice_in_dim(bias_sum, place_hd * own_heads, own_heads)
    return (
        output, token_grad, qkv_own, gate_own, bias_own, out_own, up_own, up_bias_own, down_own, down_bias_own,
        gain_1_own, shift_1_own, gain_2_own, shift_2_own, state_final, keysum_final, state_start, keysum_start,
    )


def solution(mesh):
    by_tokens = P("rows", ("blk", "hd"), None)
    by_rows = P(ALL, None)
    by_entry = P(ALL)
    by_head = P("hd")
    by_state = P("rows", "hd", None, None)
    by_keysum = P("rows", "hd", None)
    in_specs = (
        by_tokens, by_rows, by_rows, by_head, by_rows, by_rows, by_entry, by_rows, by_entry, by_entry, by_entry,
        by_entry, by_entry, P("hd", None, None), by_state, by_keysum, by_tokens, by_state, by_keysum,
    )
    out_specs = (
        by_tokens, by_tokens, by_rows, by_rows, by_head, by_rows, by_rows, by_entry, by_rows, by_entry,
        by_entry, by_entry, by_entry, by_entry, by_state, by_keysum, by_state, by_keysum,
    )
    return jax.shard_map(local, mesh=mesh, in_specs=in_specs, out_specs=out_specs, check_vma=False)
```

```python
import functools
import math

import jax
import jax.numpy as jnp
from jax import lax
from jax.experimental import pallas as pl
from jax.experimental.pallas import tpu as pltpu
from jax.sharding import PartitionSpec as P

ALL = ("rows", "blk", "hd")
BOTH = ("blk", "hd")
F32 = jnp.float32
BF16 = jnp.bfloat16
AUG = 16
ROWS = 8


def after(x, *others):
    return lax.optimization_barrier((x,) + others)[0]


class Trip:
    def __init__(self, own, sends, finish):
        self.own, self.sends, self.finish = own, sends, finish

    def messages(self):
        return [send[0] for send in self.sends]

    def land(self, *others):
        got = [lax.ppermute(*send) for send in self.sends]
        if others:
            got = after(got, *others)
        return self.finish([self.own] + got)


def departed(x, *trips):
    return after(x, [trip.messages() for trip in trips])


def landed(trips, *others):
    return [trip.land(*others) for trip in trips]


def turned(size, bit):
    return [(i, i ^ bit) for i in range(size)]


def ordered(parts, me):
    parts = list(parts)
    bit = 1
    while bit < len(parts):
        there = (me & bit) != 0
        parts = [jnp.where(there, parts[i ^ bit], parts[i]) for i in range(len(parts))]
        bit *= 2
    return parts


def pieces_trip(x, axis, size, group, me):
    sends = [(lax.dynamic_index_in_dim(x, me ^ k, 0, False), axis, turned(size, k)) for k in range(1, group)]
    own = lax.dynamic_index_in_dim(x, me, 0, False)
    return Trip(own, sends, lambda parts: jnp.stack(ordered(parts, me)))


def copies_trip(x, axis, size, me):
    sends = [(x, axis, turned(size, k)) for k in range(1, size)]
    return Trip(x, sends, lambda parts: jnp.stack(ordered(parts, me)))


def bits_of(sizes):
    found = []
    for axis in ALL:
        bit = sizes[axis] // 2
        while bit:
            found.append((axis, bit))
            bit //= 2
    return found


def routes(sizes):
    own = lambda axis: [[b] for b in bits_of(sizes) if b[0] == axis]
    z = [[b for b in bits_of(sizes) if b[0] == "blk"]]
    y, x = own("hd"), own("rows")
    return z + y + x[:1] + x[1:], z + x[:1] + y + x[1:]


def partners(step, sizes):
    axis, low = step[0][0], step[-1][1]
    count = 2 ** len(step)
    place = (lax.axis_index(axis) // low) % count
    return axis, sizes[axis], place, [k * low for k in range(count)]


def gather_start(x, sizes):
    return x.reshape((1,) * len(bits_of(sizes)) + x.shape)


def gather_trip(cur, step, sizes):
    axis, size, place, offsets = partners(step, sizes)
    dim = bits_of(sizes).index(step[0])
    shape = cur.shape[:dim] + (2,) * len(step) + cur.shape[dim + len(step) :]
    sends = [(cur, axis, turned(size, k)) for k in offsets[1:]]
    return Trip(cur, sends, lambda parts: jnp.concatenate(ordered(parts, place), axis=dim).reshape(shape))


def gather_end(cur, sizes):
    lead = len(bits_of(sizes))
    return cur.reshape((-1,) + cur.shape[lead + 1 :])


def scatter_start(x, sizes):
    bits = bits_of(sizes)
    return x.reshape((2,) * len(bits) + (x.shape[0] // 2 ** len(bits),) + x.shape[1:])


def scatter_trip(cur, step, sizes, kind=BF16):
    axis, size, place, offsets = partners(step, sizes)
    dim = bits_of(sizes).index(step[0])
    lead, rest = cur.shape[:dim], cur.shape[dim + len(step) :]
    merged = cur.reshape(lead + (len(offsets),) + rest)
    parts = [lax.dynamic_index_in_dim(merged, place ^ k, dim, True) for k in range(len(offsets))]
    sends = [(part, axis, turned(size, k)) for part, k in zip(parts[1:], offsets[1:])]

    def finish(parts):
        total = parts[0].astype(F32)
        for part in parts[1:]:
            total = total + part.astype(F32)
        return total.astype(kind).reshape(lead + (1,) * len(step) + rest)

    return Trip(parts[0], sends, finish)


def scatter_end(cur, sizes):
    return cur.reshape(cur.shape[len(bits_of(sizes)) :])


def dot(a, b, contract):
    return lax.dot_general(a, b, ((contract[:1], contract[1:]), ((), ())), preferred_element_type=F32)


def sine_cosine(x):
    turns = jnp.round(x * (1.0 / math.pi))
    rest = x - turns * 3.140625
    rest = rest - turns * 9.67502593994140625e-4
    rest = rest - turns * 1.50995788317e-7
    half = turns * 0.5
    odd = half - jnp.floor(half)
    sign = 1.0 - 4.0 * odd
    sq = rest * rest
    sine = sq * (-2.5052108385e-8) + 2.7557319224e-6
    sine = sine * sq - 1.9841269841e-4
    sine = sine * sq + 8.3333333333e-3
    sine = sine * sq - 1.6666666667e-1
    sine = rest + rest * (sq * sine)
    cosine = sq * 2.0876756988e-9 - 2.7557319224e-7
    cosine = cosine * sq + 2.4801587302e-5
    cosine = cosine * sq - 1.3888888889e-3
    cosine = cosine * sq + 4.1666666667e-2
    cosine = cosine * sq - 0.5
    cosine = cosine * sq + 1.0
    return sine * sign, cosine * sign


def split_rows(x):
    high = x.astype(BF16).astype(F32)
    rest = x - high
    middle = rest.astype(BF16).astype(F32)
    return high, middle, rest - middle


def outer_sum(column, row):
    width = row.shape[1]
    place = lax.broadcasted_iota(jnp.int32, (AUG, width), 0)

    def lay(parts, first):
        out = jnp.zeros((AUG, width), F32)
        for i, part in enumerate(parts):
            out = jnp.where(place == first + i, part, out)
        return jnp.where((place >= 3 - first) & (place < 6 - first), 1.0, out).astype(BF16)

    return dot(lay(split_rows(column), 0), lay(split_rows(row), 3), (0, 0))


def augmented(v, ones):
    width = v.shape[1]
    place = lax.broadcasted_iota(jnp.int32, (AUG, width), 0)
    extra = jnp.where(place == 0, ones, 0.0)
    return jnp.concatenate([v.astype(F32), extra], axis=0)


def lower_mask(c):
    return lax.broadcasted_iota(jnp.int32, (c, c), 0) <= lax.broadcasted_iota(jnp.int32, (c, c), 1)


def gate_kernel(tile, raw_ref, bias_ref, out_ref):
    logit = raw_ref[...].astype(F32) + bias_ref[...]
    heads, width = logit.shape
    small = jnp.log1p(jnp.exp(-jnp.abs(logit)))
    keep = jnp.minimum(logit, 0.0) - small
    slow = jnp.minimum(-logit, 0.0) - small
    place = lax.broadcasted_iota(jnp.int32, (heads, width), 1)

    def sums(x, within):
        at = lax.rem(place, within)
        step = 1
        while step < within:
            x = x + jnp.where(at >= step, pltpu.roll(x, step, 1), 0.0)
            step *= 2
        return x

    running = sums(keep, tile)
    whole = running
    offset = jnp.zeros((heads, 1), F32)
    for at in range(0, width, tile):
        whole = jnp.where((place >= at) & (place < at + tile), running + offset, whole)
        offset = offset + running[:, at + tile - 1 : at + tile]
    for kind, value in enumerate(
        (running, slow - running, whole, jnp.exp(slow), jnp.exp(keep), jnp.broadcast_to(offset, (heads, width)))
    ):
        for head in range(heads):
            out_ref[head, kind : kind + 1, :] = value[head : head + 1]


def first_kernel(per_row, qkv_ref, gate_ref, up_ref, *refs):
    *vectors, bias_ref, maps_ref, out_ref = refs
    shard, wide = qkv_ref.shape
    heads = gate_ref.shape[1]
    lane = lax.broadcasted_iota(jnp.int32, (shard, 128), 1)

    def column(ref, stride, first):
        n = ref.shape[0]
        value = jnp.broadcast_to(ref[...].astype(F32)[None, :], (shard, n))
        row_at = lax.broadcasted_iota(jnp.int32, (shard, n), 0)
        line_at = lax.broadcasted_iota(jnp.int32, (shard, n), 1)
        return jnp.sum(jnp.where(line_at == row_at * stride + first, value, 0.0), axis=1, keepdims=True)

    small = jnp.zeros((shard, 128), F32)
    columns = [column(up_ref, per_row, i) for i in range(per_row)] + [column(ref, 1, 0) for ref in vectors]
    for i, value in enumerate(columns):
        small = jnp.where(lane == heads + i, value, small)
    at = heads + len(columns)
    bias = jnp.broadcast_to(bias_ref[...][None, :], (shard, bias_ref.shape[0]))
    for part in split_rows(bias):
        for i in range(bias_ref.shape[0]):
            small = jnp.where(lane == at, part[:, i : i + 1], small)
            at += 1
    for i in range(heads):
        small = jnp.where(lane == i, gate_ref[:, i : i + 1].astype(F32), small)
    out_ref[:, :wide] = qkv_ref[...]
    out_ref[:, wide : wide + 128] = small.astype(BF16)
    out_ref[:, wide + 128 :] = maps_ref[...]


def rest_kernel(out_ref_w, up_ref, down_ref, out_ref):
    shard, width = out_ref_w.shape
    out_ref[:shard] = out_ref_w[...]
    blocks = up_ref.shape[1] // width
    for i in range(blocks):
        out_ref[shard * (i + 1) : shard * (i + 2)] = up_ref[:, i * width : (i + 1) * width]
    out_ref[shard * (blocks + 1) :] = down_ref[...]


def features(unit, fmt, scale):
    sine, cosine = sine_cosine(dot(fmt, unit, (1, 0)))
    return (jnp.concatenate([sine, cosine], axis=0) * scale).astype(BF16)


def forward_kernel(tile, qkv_ref, fmt_ref, rows_ref, qf_ref, kf_ref, nu_ref, state_ref):
    width = qkv_ref.shape[-1]
    fmt = fmt_ref[0]
    scale = 1.0 / math.sqrt(fmt.shape[0])
    mask = lower_mask(tile)
    state = None
    for at in range(0, width, tile):
        here = pl.ds(at, tile)
        query = qkv_ref[0, 0, :, here].astype(F32)
        key = qkv_ref[0, 1, :, here].astype(F32)
        query = (query * lax.rsqrt(jnp.sum(query * query, axis=0, keepdims=True) + 1e-06)).astype(BF16)
        key = (key * lax.rsqrt(jnp.sum(key * key, axis=0, keepdims=True) + 1e-06)).astype(BF16)
        qf = features(query, fmt, scale)
        kf = features(key, fmt, scale)
        qf_ref[0, :, here] = qf
        kf_ref[0, :, here] = kf
        running = rows_ref[0, 0:1, here]
        lead = rows_ref[0, 1:2, here]
        last = running[:, tile - 1 : tile]
        values = augmented(qkv_ref[0, 2, :, here], 1.0)
        weights = jnp.where(mask, jnp.exp(outer_sum(lead, running)), 0.0)
        scores = (dot(kf, qf, (0, 0)) * weights).astype(BF16)
        numer = dot(values.astype(BF16), scores, (1, 0))
        if state is not None:
            numer = numer + jnp.exp(running) * dot(state.astype(BF16), qf, (1, 0))
        nu_ref[0, :, here] = numer[: nu_ref.shape[1]]
        tail = (values * jnp.exp(last + lead)).astype(BF16)
        new = dot(tail, kf, (1, 1))
        state = new if state is None else jnp.exp(last) * state + new
    state_ref[0] = state


def enter_kernel(state_ref, qf_ref, rows_ref, nu_ref, mixed_ref, total_ref):
    state = state_ref[0]
    high = state.astype(BF16)
    rest = (state - high.astype(F32)).astype(BF16)
    qf = qf_ref[0]
    rows = nu_ref.shape[1]
    extra = (dot(high, qf, (1, 0)) + dot(rest, qf, (1, 0)))[:rows]
    total = nu_ref[0] + jnp.exp(rows_ref[0, 2:3, :]) * extra
    total_ref[0] = total
    size = mixed_ref.shape[1]
    denom = total[size : size + 1]
    floor = softplus(4.0 * denom) * 0.25 + 0.1
    mixed_ref[0] = (total[:size] / floor).astype(BF16)


def softplus(x):
    return jnp.maximum(x, 0.0) + jnp.log1p(jnp.exp(-jnp.abs(x)))


def leave_kernel(grad_ref, total_ref, qf_ref, rows_ref, a_ref, back_ref):
    grad = grad_ref[0].astype(F32)
    size = grad.shape[0]
    numer = total_ref[0, :size]
    denom = total_ref[0, size : size + 1]
    inverse = 1.0 / (softplus(4.0 * denom) * 0.25 + 0.1)
    inner = jnp.sum(grad * numer, axis=0, keepdims=True)
    by_denom = -inner * jax.nn.sigmoid(4.0 * denom) * inverse * inverse
    whole = augmented(grad * inverse, by_denom)
    a_ref[0] = whole.astype(BF16)
    back_ref[0] = dot((whole * jnp.exp(rows_ref[0, 2:3, :])).astype(BF16), qf_ref[0], (1, 1))


def unit_back(raw, unit_grad):
    inverse = lax.rsqrt(jnp.sum(raw * raw, axis=0, keepdims=True) + 1e-06)
    inner = jnp.sum(raw * unit_grad, axis=0, keepdims=True)
    return inverse * (unit_grad - raw * (inner * inverse * inverse))


def angle_back(feat, grad):
    half = feat.shape[0] // 2
    feat = feat.astype(F32)
    return (grad[:half] * feat[half:] - grad[half:] * feat[:half]).astype(BF16)


def backward_kernel(
    tile, qkv_ref, fm_ref, rows_ref, qf_ref, kf_ref, a_ref, state_ref, back_ref, out_ref, logit_ref
):
    width = qkv_ref.shape[-1]
    size = qkv_ref.shape[2]
    fm = fm_ref[0]
    mask = lower_mask(tile)
    spots = list(range(0, width, tile))
    states = [state_ref[0]]
    for at in spots:
        here = pl.ds(at, tile)
        last = rows_ref[0, 0:1, at + tile - 1 : at + tile]
        values = augmented(qkv_ref[0, 2, :, here], 1.0)
        tail = (values * jnp.exp(last + rows_ref[0, 1:2, here])).astype(BF16)
        states.append(jnp.exp(last) * states[-1] + dot(tail, kf_ref[0, :, here], (1, 1)))
    back = back_ref[0]
    ones = jnp.ones((AUG, tile), BF16)

    def whole_sum(x):
        return jnp.sum(jnp.sum(x, axis=0, keepdims=True), axis=1, keepdims=True)

    pieces = []
    for index in reversed(range(len(spots))):
        at = spots[index]
        here = pl.ds(at, tile)
        running = rows_ref[0, 0:1, here]
        lead = rows_ref[0, 1:2, here]
        last = running[:, tile - 1 : tile]
        decay = jnp.exp(running)
        tail = jnp.exp(last + lead)
        qf = qf_ref[0, :, here]
        kf = kf_ref[0, :, here]
        a = a_ref[0, :, here]
        values = augmented(qkv_ref[0, 2, :, here], 1.0).astype(BF16)
        state = states[index].astype(BF16)
        low_back = back.astype(BF16)
        weights = jnp.where(mask, jnp.exp(outer_sum(lead, running)), 0.0)
        alike = dot(kf, qf, (0, 0))
        scores = (alike * weights).astype(BF16)
        pairs = dot(values, a, (0, 0)) * weights
        terms = (pairs * alike).astype(BF16)
        pairs = pairs.astype(BF16)
        from_state = decay * dot(state, a, (0, 0))
        from_back = tail * dot(low_back, values, (0, 0))
        query_feat = dot(kf, pairs, (1, 0)) + from_state
        key_feat = dot(qf, pairs, (1, 1)) + from_back
        by_query = dot(ones, terms, (1, 0))[:1]
        by_key = dot(ones, terms, (1, 1))[:1]
        state_term = jnp.sum(qf.astype(F32) * from_state, axis=0, keepdims=True)
        back_term = jnp.sum(kf.astype(F32) * from_back, axis=0, keepdims=True)
        through = jnp.exp(last) * whole_sum(back * states[index])
        constant = jnp.sum(back_term, axis=1, keepdims=True) + through
        pieces.append((by_query - by_key + state_term - back_term, by_key + back_term, constant))
        value = dot(a[:size], scores, (1, 1)) + tail * dot(low_back[:size], kf, (1, 0))
        query_unit = dot(fm, angle_back(qf, query_feat), (1, 0))
        key_unit = dot(fm, angle_back(kf, key_feat), (1, 0))
        out_ref[0, 0, :, here] = unit_back(qkv_ref[0, 0, :, here].astype(F32), query_unit).astype(BF16)
        out_ref[0, 1, :, here] = unit_back(qkv_ref[0, 1, :, here].astype(F32), key_unit).astype(BF16)
        out_ref[0, 2, :, here] = value.astype(BF16)
        back = jnp.exp(last) * back + dot((a.astype(F32) * decay).astype(BF16), qf, (1, 1))
    place = lax.broadcasted_iota(jnp.int32, (ROWS, tile), 0)
    sums = jnp.zeros((ROWS, tile), F32)
    for index, piece in enumerate(pieces[::-1]):
        sums = jnp.where(place == index, piece[0], sums)
    place = lax.broadcasted_iota(jnp.int32, (ROWS, tile), 1)
    step = 1
    while step < tile:
        sums = sums + jnp.where(place < tile - step, pltpu.roll(sums, tile - step, 1), 0.0)
        step *= 2
    for index, (_, by_key, constant) in enumerate(pieces[::-1]):
        here = pl.ds(spots[index], tile)
        keep_grad = sums[index : index + 1] + constant
        logit = keep_grad * rows_ref[0, 3:4, here] - by_key * rows_ref[0, 4:5, here]
        logit_ref[0, :, here] = jnp.broadcast_to(logit, (ROWS, tile))


def per_head(kernel, outs, heads, *arrays, us):
    def spec(shape, offset):
        rest = len(shape) - 1
        return pl.BlockSpec((1,) + tuple(shape[1:]), lambda h: (h + offset,) + (0,) * rest)

    nbytes = sum(heads * math.prod(a.shape[1:]) * a.dtype.itemsize for a, _ in arrays)
    nbytes += sum(math.prod(s) * jnp.dtype(d).itemsize for s, d in outs)
    return pl.pallas_call(
        kernel,
        grid=(heads,),
        in_specs=[spec(a.shape, offset) for a, offset in arrays],
        out_specs=[spec(s, 0) for s, _ in outs],
        out_shape=[jax.ShapeDtypeStruct(s, d) for s, d in outs],
        compiler_params=pltpu.CompilerParams(vmem_limit_bytes=24 * 2**20),
        cost_estimate=pl.CostEstimate(flops=int(us * 1.1e9), bytes_accessed=int(nbytes), transcendentals=0),
    )(*[a for a, _ in arrays])


def norm_parts(x):
    average = jnp.mean(x, axis=0, keepdims=True)
    centered = x - average
    inverse = lax.rsqrt(jnp.mean(centered * centered, axis=0, keepdims=True) + 1e-05)
    return centered * inverse, inverse


def norm_back(hat, inverse, gain, grad):
    scaled = grad * gain
    first = jnp.mean(scaled, axis=0, keepdims=True)
    second = jnp.mean(scaled * hat, axis=0, keepdims=True)
    return (scaled - first - hat * second) * inverse


def product(spec, a, b):
    return jnp.einsum(spec, a, b, preferred_element_type=F32)


def local(
    tokens, w_qkv, w_gate, gate_bias, w_out, w_up, up_bias, w_down, down_bias, pre_gain, pre_shift,
    mid_gain, mid_shift, feature_map, state_init, keysum_init, out_cot, state_cot, keysum_cot,
):
    sizes = {axis: lax.axis_size(axis) for axis in ALL}
    count_hd, count_blk = sizes["hd"], sizes["blk"]
    devices = sizes["rows"] * count_blk * count_hd
    both = count_blk * count_hd
    seqs, part, width = tokens.shape
    own_heads, head_dim, rand = feature_map.shape
    heads = own_heads * count_hd
    feat = 2 * rand
    hidden_size = w_up.shape[1]
    length = seqs * part
    tile = 256 if length % 256 == 0 else 128
    shard = w_qkv.shape[0]
    aug = head_dim + AUG
    place_hd, place_blk = lax.axis_index("hd"), lax.axis_index("blk")
    place = place_blk * count_hd + place_hd
    member, chunk = place % seqs, place // seqs
    chunks = both // seqs

    def to_chunk(x):
        return pieces_trip(x, BOTH, both, seqs, member)

    def from_chunk(x):
        return pieces_trip(x.reshape(seqs, part, width), BOTH, both, seqs, member)

    per_row = hidden_size // width
    n_small = heads + per_row + 5
    shares = devices // count_hd
    maps = feature_map.reshape(shares, shard, -1)
    spot = lax.axis_index("rows") * count_blk + place_blk
    maps = lax.dynamic_index_in_dim(maps, spot, 0, False)
    first = pl.pallas_call(
        functools.partial(first_kernel, per_row),
        out_shape=jax.ShapeDtypeStruct((shard, 3 * width + 128 + maps.shape[1]), BF16),
    )(w_qkv, w_gate, up_bias, down_bias, pre_gain, pre_shift, mid_gain, mid_shift, gate_bias, maps)

    half = 3 * width // 2
    one, two = routes(sizes)
    stages = range(len(one))

    def gathers(streams, at):
        return [gather_trip(cur, route[at], sizes) for cur, route in zip(streams, (one, two))]

    whole = gather_trip(gather_start(first, sizes), one[0], sizes).land()
    first = [whole[..., :half], whole[..., half:]]
    tokens_trip = to_chunk(after(tokens, *first))
    cut = len(one) - len([b for b in bits_of(sizes) if b[0] == "rows"]) + 1
    for at in stages[1:cut]:
        first = landed(gathers(first, at))
    second = pl.pallas_call(
        rest_kernel, out_shape=jax.ShapeDtypeStruct((shard * (per_row + 1) + w_down.shape[0], width), BF16)
    )(w_out, w_up, w_down)
    second = lax.all_gather(second, ALL, axis=0)
    for at in stages[cut:]:
        first = landed(gathers(first, at))
    qkv_halves = [gather_end(f, sizes) for f in first]
    full_small = qkv_halves[1][:, half:]
    qkv_halves[1] = qkv_halves[1][:, :half]
    full_gate = full_small[:, :heads]
    full_up_bias = full_small[:, heads : heads + per_row].reshape(hidden_size, 1).astype(F32)
    vectors = [full_small[:, heads + per_row + i : heads + per_row + i + 1].astype(F32) for i in range(5)]
    full_down_bias, gain_1, shift_1, gain_2, shift_2 = vectors
    maps = full_small[:, -maps.shape[1] :].reshape(shares, count_hd, shard, -1)
    fm = maps.transpose(1, 0, 2, 3).reshape(heads, head_dim, rand)
    fmt = fm.transpose(0, 2, 1)
    bias = full_small.reshape(shares, count_hd, shard, -1)[0, :, 0, n_small : n_small + 3 * own_heads]
    bias = jnp.sum(bias.reshape(count_hd, 3, own_heads).astype(F32), axis=1).reshape(heads, 1)

    def lines(state, keysum):
        lead = state.shape[:-3]
        n = state.shape[-3]
        rows = jnp.swapaxes(state, -1, -2).reshape(lead + (n * head_dim, feat))
        return jnp.concatenate([rows, keysum], axis=-2)

    def unlines(rows, n):
        lead = rows.shape[:-2]
        return rows[..., : n * head_dim, :].reshape(lead + (n, head_dim, feat)), rows[..., n * head_dim :, :]

    def stacked(state, keysum):
        zeros = jnp.zeros((keysum.shape[0], AUG - 1, feat), F32)
        return jnp.concatenate([state.astype(F32), keysum.astype(F32)[:, None], zeros], axis=1)

    def flat(x):
        return jnp.concatenate([x[:, :head_dim].reshape(-1, feat), x[:, head_dim]], axis=0)

    def unflat(rows):
        return stacked(*unlines(rows, rows.shape[0] // (head_dim + 1)))

    begin, end = lines(state_init, keysum_init), lines(state_cot, keysum_cot)
    offers = []
    for other in range(count_hd):
        spot = place_blk * count_hd + other
        pick = lambda a: lax.dynamic_index_in_dim(a, spot % seqs, 0, False)
        offers.append(jnp.where(spot // seqs == 0, pick(begin), pick(end)))
    edge_trip = pieces_trip(after(jnp.stack(offers), *first), "hd", count_hd, count_hd, place_hd)

    at_start = chunk == 0
    at_end = chunk == chunks - 1
    own = heads // 2
    groups = [slice(0, own), slice(own, heads)]

    def hop_trip(group, added, forward):
        pairs = [(i, i + seqs) for i in range(both - seqs)]
        pairs = pairs if forward else [(b, a) for a, b in pairs]
        outer = at_start if forward else at_end
        choose = lambda parts: jnp.where(outer, edge[group], unflat(parts[1].astype(F32)))
        state = edge[group]
        for last in range(chunks - 1):
            trip = Trip(None, [(flat(added + decay[group] * state).astype(BF16), BOTH, pairs)], choose)
            if last < chunks - 2:
                state = trip.land()
        return trip

    x = tokens_trip.land().reshape(length, width).T.astype(F32)
    hat_1, inverse_1 = norm_parts(x)
    normed = (hat_1 * gain_1 + shift_1).astype(BF16)
    packed = [product("dc,dt->ct", w, normed).astype(BF16).reshape(own, 3, head_dim, length) for w in qkv_halves]
    raw = product("dh,dt->ht", full_gate, normed).astype(BF16)
    rows = pl.pallas_call(
        functools.partial(gate_kernel, tile),
        out_shape=jax.ShapeDtypeStruct((heads, ROWS, length), F32),
    )(raw, bias)
    decay = jnp.exp(rows[:, 5:6, :1])
    edge = unlines(edge_trip.land(*packed), own_heads)
    edge = stacked(edge[0].reshape(heads, head_dim, feat), edge[1].reshape(heads, feat))

    def forward(group, part_qkv):
        return per_head(
            functools.partial(forward_kernel, tile),
            [
                ((own, feat, length), BF16),
                ((own, feat, length), BF16),
                ((own, head_dim + 8, length), F32),
                ((own, aug, feat), F32),
            ],
            own, (part_qkv, 0), (fmt, group.start), (rows, group.start), us=9,
        )

    def enter(group, state, qf, partial_nu):
        return per_head(
            enter_kernel,
            [((own, head_dim, length), BF16), ((own, head_dim + 8, length), F32)],
            own, (state, 0), (qf, 0), (rows, group.start), (partial_nu, 0), us=2,
        )

    cot_trip = to_chunk(after(out_cot, *packed))
    done = [forward(groups[0], departed(packed[0], cot_trip))]
    cot = cot_trip.land(done[0]).reshape(length, width).T
    hop_one = hop_trip(groups[0], done[0][3], True)
    done.append(forward(groups[1], departed(packed[1], hop_one)))
    hop_two = hop_trip(groups[1], done[1][3], True)
    entering = [hop_one.land(done[1])]
    entered = [enter(groups[0], departed(entering[0], hop_two), done[0][0], done[0][2])]
    entering.append(hop_two.land(entered[0]))
    entered.append(enter(groups[1], entering[1], done[1][0], done[1][2]))
    second = after(second, entered[1][0])
    full_out = second[:, :shard].reshape(width, width)
    full_up = [second[:, i : i + shard].reshape(width, width) for i in range(shard, shard * (per_row + 1), shard)]
    full_up = jnp.concatenate(full_up, axis=1)
    full_down = second[:, shard * (per_row + 1) :].reshape(hidden_size, width)
    leaving = [d[3] + decay[group] * state for d, group, state in zip(done, groups, entering)]
    mixed = jnp.concatenate([e[0] for e in entered]).reshape(width, length)

    attended = x + product("io,it->ot", full_out, mixed)
    hat_2, inverse_2 = norm_parts(attended)
    hidden = (hat_2 * gain_2 + shift_2).astype(BF16)
    before = product("df,dt->ft", full_up, hidden) + full_up_bias
    cumulative = 0.5 + 0.5 * lax.erf(before * math.sqrt(0.5))
    density = jnp.exp(-0.5 * before * before) * (1.0 / math.sqrt(2.0 * math.pi))
    active = (before * cumulative).astype(BF16)
    before_grad = (product("fo,ot->ft", full_down, cot) * (cumulative + before * density)).astype(BF16)
    hidden_grad = product("df,ft->dt", full_up, before_grad)
    cot_full = cot.astype(F32)
    attended_grad = cot_full + norm_back(hat_2, inverse_2, gain_2, hidden_grad)
    attended_low = attended_grad.astype(BF16)
    mixed_grad = product("io,ot->it", full_out, attended_low).astype(BF16).reshape(heads, head_dim, length)

    def leave(group, grad, entered_part, qf):
        return per_head(
            leave_kernel,
            [((own, aug, length), BF16), ((own, aug, feat), F32)],
            own, (grad, group.start), (entered_part, 0), (qf, 0), (rows, group.start), us=2,
        )

    left = [leave(groups[0], mixed_grad, entered[0][1], done[0][0])]
    hop_one = hop_trip(groups[0], left[0][1], False)
    left.append(leave(groups[1], departed(mixed_grad, hop_one), entered[1][1], done[1][0]))
    hop_two = hop_trip(groups[1], left[1][1], False)

    held = departed(hidden, hop_two)
    up_grad = product("dt,ft->df", held, before_grad).astype(BF16)
    down_grad = product("ft,ot->fo", active, cot).astype(BF16)

    def scatters(streams, at, kind=BF16):
        return [scatter_trip(cur, route[at], sizes, kind) for cur, route in zip(streams, (one, two))]

    early = [scatter_start(up_grad, sizes), scatter_start(down_grad, sizes)]
    early_trips = scatters(early, len(one) - 1)
    result = attended + product("fo,ft->ot", departed(full_down, *early_trips), active) + full_down_bias
    result = result.astype(BF16)
    out_grad = product("it,ot->io", mixed, attended_low).astype(BF16)
    early = landed(early_trips, result)
    for at in stages[-2 : cut - 1 : -1]:
        early = landed(scatters(early, at))
    output_trip = from_chunk(result.T)
    backs = [hop_one.land(result), hop_two.land(result)]
    starting = [part[1] + decay[group] * back for part, group, back in zip(left, groups, backs)]
    down_bias_grad = jnp.sum(cot_full, axis=1)
    up_bias_grad = jnp.sum(before_grad.astype(F32), axis=1)
    gain_2_grad = jnp.sum(hidden_grad * hat_2, axis=1)
    shift_2_grad = jnp.sum(hidden_grad, axis=1)

    ends = flat(jnp.where(at_start, jnp.concatenate(starting), jnp.concatenate(leaving)))
    ends = lax.all_gather(ends.astype(BF16), BOTH, axis=0)

    def backward(i, part_qkv):
        group = groups[i]
        grad, logit = per_head(
            functools.partial(backward_kernel, tile),
            [((own, 3, head_dim, length), BF16), ((own, ROWS, length), F32)],
            own, (part_qkv, 0), (fm, group.start), (rows, group.start), (done[i][0], 0), (done[i][1], 0),
            (left[i][0], 0), (entering[i], 0), (backs[i], 0), us=10,
        )
        return grad.reshape(half, length), logit[:, 0]

    early_trips = scatters(early, cut - 1)
    grads = [backward(0, departed(packed[0], output_trip, *early_trips))]
    early = landed(early_trips, grads[0])
    output = output_trip.land(grads[0])
    for at in stages[cut - 2 : 1 : -1]:
        early = landed(scatters(early, at))
    early_trips = scatters(early, 1)
    qkv_grad = [product("dt,ct->dc", normed, grads[0][0]).astype(BF16)]
    late_one = scatter_start(jnp.concatenate([qkv_grad[0], out_grad], axis=1), sizes)
    late_trip = scatter_trip(late_one, one[-1], sizes)
    grads.append(backward(1, departed(packed[1], late_trip, *early_trips)))
    early = landed(early_trips, grads[1])
    late_one = late_trip.land(grads[1])
    late_trip = scatter_trip(late_one, one[-2], sizes)

    gate_low = jnp.concatenate([g[1] for g in grads])
    bias_grad = jnp.sum(gate_low, axis=1)
    gate_low = gate_low.astype(BF16)
    last_grad = departed(grads[1][0], late_trip)
    normed_grad = (
        product("dc,ct->dt", qkv_halves[0], grads[0][0])
        + product("dc,ct->dt", qkv_halves[1], last_grad)
        + product("dh,ht->dt", full_gate, gate_low)
    )
    qkv_grad.append(product("dt,ct->dc", normed, last_grad).astype(BF16))
    gate_grad = product("dt,ht->dh", normed, gate_low)
    gain_1_grad = jnp.sum(normed_grad * hat_1, axis=1)
    shift_1_grad = jnp.sum(normed_grad, axis=1)
    grad_small = jnp.concatenate(
        [gate_grad, up_bias_grad.reshape(width, per_row)]
        + [v[:, None] for v in (down_bias_grad, gain_1_grad, shift_1_grad, gain_2_grad, shift_2_grad)]
        + [jnp.broadcast_to(bias_grad[None], (width, heads))],
        axis=1,
    )
    grad_small = jnp.pad(grad_small, ((0, 0), (0, -grad_small.shape[1] % 128))).astype(BF16)
    late_two = scatter_start(jnp.concatenate([qkv_grad[1], grad_small], axis=1), sizes)
    other_trip = scatter_trip(late_two, two[-1], sizes)
    late_one = late_trip.land(other_trip.messages())
    late_trip = scatter_trip(late_one, one[-3], sizes, BF16 if len(one) > 3 else F32)
    early_trips = scatters(after(early, other_trip.messages()), 0, F32)
    held = departed(inverse_1, other_trip, late_trip, *early_trips)
    token_grad = (attended_grad + norm_back(hat_1, held, gain_1, normed_grad)).astype(BF16).T
    tokens_trip = from_chunk(token_grad)
    late_one = late_trip.land(token_grad)
    late_two = other_trip.land(token_grad)
    late = [late_one, late_two]
    routes_left = [one[-4::-1], two[-2::-1]]
    last_trips = []
    for i in range(2):
        for step in routes_left[i][:-1]:
            late[i] = scatter_trip(late[i], step, sizes).land()
        last_trips.append(scatter_trip(late[i], routes_left[i][-1], sizes, F32))
    up_own, down_own = (scatter_end(e, sizes) for e in landed(early_trips, *[t.messages() for t in last_trips]))
    late_one, late_two = landed(last_trips)
    late_one, late_two = scatter_end(late_one, sizes), scatter_end(late_two, sizes)
    token_grad = tokens_trip.land(*[t.messages() for t in last_trips])
    def finished(rows):
        state, keysum = unlines(rows, heads)
        state = lax.dynamic_slice_in_dim(state, place_hd * own_heads, own_heads, 1)
        keysum = lax.dynamic_slice_in_dim(keysum, place_hd * own_heads, own_heads, 1)
        return jnp.swapaxes(state.astype(F32), -1, -2), keysum.astype(F32)

    state_start, keysum_start = finished(ends[:seqs])
    state_final, keysum_final = finished(ends[both - seqs :])

    qkv_own = jnp.concatenate([late_one[:, :half], late_two[:, :half]], axis=1)
    out_own = late_one[:, half:]
    own_small = late_two[:, half:]
    gate_own = own_small[:, :heads]
    up_bias_own = own_small[:, heads : heads + per_row].reshape(-1)
    down_bias_own, gain_1_own, shift_1_own, gain_2_own, shift_2_own = (
        own_small[:, heads + per_row + i] for i in range(5)
    )
    bias_sum = own_small[0, heads + per_row + 5 : 2 * heads + per_row + 5]
    bias_own = lax.dynamic_slice_in_dim(bias_sum, place_hd * own_heads, own_heads)
    return (
        output, token_grad, qkv_own, gate_own, bias_own, out_own, up_own, up_bias_own, down_own, down_bias_own,
        gain_1_own, shift_1_own, gain_2_own, shift_2_own, state_final, keysum_final, state_start, keysum_start,
    )


def solution(mesh):
    by_tokens = P("rows", ("blk", "hd"), None)
    by_rows = P(ALL, None)
    by_entry = P(ALL)
    by_head = P("hd")
    by_state = P("rows", "hd", None, None)
    by_keysum = P("rows", "hd", None)
    in_specs = (
        by_tokens, by_rows, by_rows, by_head, by_rows, by_rows, by_entry, by_rows, by_entry, by_entry, by_entry,
        by_entry, by_entry, P("hd", None, None), by_state, by_keysum, by_tokens, by_state, by_keysum,
    )
    out_specs = (
        by_tokens, by_tokens, by_rows, by_rows, by_head, by_rows, by_rows, by_entry, by_rows, by_entry,
        by_entry, by_entry, by_entry, by_entry, by_state, by_keysum, by_state, by_keysum,
    )
    return jax.shard_map(local, mesh=mesh, in_specs=in_specs, out_specs=out_specs, check_vma=False)
```

```python
import functools
import math

import jax
import jax.numpy as jnp
from jax import lax
from jax.experimental import pallas as pl
from jax.experimental.pallas import tpu as pltpu
from jax.sharding import PartitionSpec as P

ALL = ("rows", "blk", "hd")
BOTH = ("blk", "hd")
F32 = jnp.float32
BF16 = jnp.bfloat16
AUG = 16
ROWS = 8


def after(x, *others):
    return lax.optimization_barrier((x,) + others)[0]


class Trip:
    def __init__(self, own, sends, finish):
        self.own, self.sends, self.finish = own, sends, finish

    def messages(self):
        return [send[0] for send in self.sends]

    def land(self, *others):
        got = [lax.ppermute(*send) for send in self.sends]
        if others:
            got = after(got, *others)
        return self.finish([self.own] + got)


def departed(x, *trips):
    return after(x, [trip.messages() for trip in trips])


def landed(trips, *others):
    return [trip.land(*others) for trip in trips]


def turned(size, bit):
    return [(i, i ^ bit) for i in range(size)]


def ordered(parts, me):
    parts = list(parts)
    bit = 1
    while bit < len(parts):
        there = (me & bit) != 0
        parts = [jnp.where(there, parts[i ^ bit], parts[i]) for i in range(len(parts))]
        bit *= 2
    return parts


def pieces_trip(x, axis, size, group, me):
    sends = [(lax.dynamic_index_in_dim(x, me ^ k, 0, False), axis, turned(size, k)) for k in range(1, group)]
    own = lax.dynamic_index_in_dim(x, me, 0, False)
    return Trip(own, sends, lambda parts: jnp.stack(ordered(parts, me)))


def bits_of(sizes):
    found = []
    for axis in ALL:
        bit = sizes[axis] // 2
        while bit:
            found.append((axis, bit))
            bit //= 2
    return found


def routes(sizes):
    own = lambda axis: [[b] for b in bits_of(sizes) if b[0] == axis]
    z = [[b for b in bits_of(sizes) if b[0] == "blk"]]
    y, x = own("hd"), own("rows")
    return z + y + x[:1] + x[1:], z + x[:1] + y + x[1:]


def partners(step, sizes):
    axis, low = step[0][0], step[-1][1]
    count = 2 ** len(step)
    place = (lax.axis_index(axis) // low) % count
    return axis, sizes[axis], place, [k * low for k in range(count)]


def gather_start(x, sizes):
    return x.reshape((1,) * len(bits_of(sizes)) + x.shape)


def gather_trip(cur, step, sizes):
    axis, size, place, offsets = partners(step, sizes)
    dim = bits_of(sizes).index(step[0])
    shape = cur.shape[:dim] + (2,) * len(step) + cur.shape[dim + len(step) :]
    sends = [(cur, axis, turned(size, k)) for k in offsets[1:]]
    return Trip(cur, sends, lambda parts: jnp.concatenate(ordered(parts, place), axis=dim).reshape(shape))


def gather_end(cur, sizes):
    lead = len(bits_of(sizes))
    return cur.reshape((-1,) + cur.shape[lead + 1 :])


def scatter_start(x, sizes):
    bits = bits_of(sizes)
    return x.reshape((2,) * len(bits) + (x.shape[0] // 2 ** len(bits),) + x.shape[1:])


def in_two(x):
    high = lax.reduce_precision(x, 8, 7)
    return jnp.concatenate([high, x - high], axis=-1)


def scatter_trip(cur, step, sizes, kind=BF16, fine=0):
    axis, size, place, offsets = partners(step, sizes)
    dim = bits_of(sizes).index(step[0])
    lead, rest = cur.shape[:dim], cur.shape[dim + len(step) : -1]
    merged = cur.reshape(lead + (len(offsets),) + rest + cur.shape[-1:])
    parts = [lax.dynamic_index_in_dim(merged, place ^ k, dim, True) for k in range(len(offsets))]
    sends = [(part, axis, turned(size, k)) for part, k in zip(parts[1:], offsets[1:])]

    def finish(parts):
        total = parts[0].astype(F32)
        for part in parts[1:]:
            total = total + part.astype(F32)
        if fine:
            exact = total[..., -2 * fine : -fine] + total[..., -fine:]
            exact = exact if kind == F32 else in_two(exact)
            total = jnp.concatenate([total[..., : -2 * fine], exact], axis=-1)
        return total.astype(kind).reshape(lead + (1,) * len(step) + rest + total.shape[-1:])

    return Trip(parts[0], sends, finish)


def scatter_end(cur, sizes):
    return cur.reshape(cur.shape[len(bits_of(sizes)) :])


def dot(a, b, contract):
    return lax.dot_general(a, b, ((contract[:1], contract[1:]), ((), ())), preferred_element_type=F32)


def sine_cosine(x):
    turns = jnp.round(x * (1.0 / math.pi))
    rest = x - turns * 3.140625
    rest = rest - turns * 9.67502593994140625e-4
    rest = rest - turns * 1.50995788317e-7
    half = turns * 0.5
    odd = half - jnp.floor(half)
    sign = 1.0 - 4.0 * odd
    sq = rest * rest
    sine = sq * (-2.5052108385e-8) + 2.7557319224e-6
    sine = sine * sq - 1.9841269841e-4
    sine = sine * sq + 8.3333333333e-3
    sine = sine * sq - 1.6666666667e-1
    sine = rest + rest * (sq * sine)
    cosine = sq * 2.0876756988e-9 - 2.7557319224e-7
    cosine = cosine * sq + 2.4801587302e-5
    cosine = cosine * sq - 1.3888888889e-3
    cosine = cosine * sq + 4.1666666667e-2
    cosine = cosine * sq - 0.5
    cosine = cosine * sq + 1.0
    return sine * sign, cosine * sign


def split_rows(x):
    high = x.astype(BF16).astype(F32)
    rest = x - high
    middle = rest.astype(BF16).astype(F32)
    return high, middle, rest - middle


def outer_sum(column, row):
    width = row.shape[1]
    place = lax.broadcasted_iota(jnp.int32, (AUG, width), 0)

    def lay(parts, first):
        out = jnp.zeros((AUG, width), F32)
        for i, part in enumerate(parts):
            out = jnp.where(place == first + i, part, out)
        return jnp.where((place >= 3 - first) & (place < 6 - first), 1.0, out).astype(BF16)

    return dot(lay(split_rows(column), 0), lay(split_rows(row), 3), (0, 0))


def augmented(v, ones):
    width = v.shape[1]
    place = lax.broadcasted_iota(jnp.int32, (AUG, width), 0)
    extra = jnp.where(place == 0, ones, 0.0)
    return jnp.concatenate([v.astype(F32), extra], axis=0)


def lower_mask(c):
    return lax.broadcasted_iota(jnp.int32, (c, c), 0) <= lax.broadcasted_iota(jnp.int32, (c, c), 1)


def gate_kernel(tile, heads, own_heads, shard, first_bias, small_ref, normed_ref, out_ref):
    raw = dot(small_ref[:, :128], normed_ref[...], (0, 0))[:heads].astype(BF16).astype(F32)
    groups = heads // own_heads
    block = small_ref[: groups * shard, :128].astype(F32)
    head = lax.broadcasted_iota(jnp.int32, (heads, 128), 0)
    lane = lax.broadcasted_iota(jnp.int32, (heads, 128), 1)
    bias = jnp.zeros((heads, 1), F32)
    for group in range(groups):
        wanted = False
        for part in range(3):
            wanted = wanted | (lane == first_bias + part * own_heads + head - group * own_heads)
        wanted = wanted & (head >= group * own_heads) & (head < (group + 1) * own_heads)
        bias = bias + jnp.sum(jnp.where(wanted, block[group * shard : group * shard + 1], 0.0), axis=1, keepdims=True)
    logit = raw + bias
    heads, width = logit.shape
    small = jnp.log1p(jnp.exp(-jnp.abs(logit)))
    keep = jnp.minimum(logit, 0.0) - small
    slow = jnp.minimum(-logit, 0.0) - small
    place = lax.broadcasted_iota(jnp.int32, (heads, width), 1)

    def sums(x, within):
        at = lax.rem(place, within)
        step = 1
        while step < within:
            x = x + jnp.where(at >= step, pltpu.roll(x, step, 1), 0.0)
            step *= 2
        return x

    running = sums(keep, tile)
    whole = running
    offset = jnp.zeros((heads, 1), F32)
    for at in range(0, width, tile):
        whole = jnp.where((place >= at) & (place < at + tile), running + offset, whole)
        offset = offset + running[:, at + tile - 1 : at + tile]
    for kind, value in enumerate(
        (running, slow - running, whole, jnp.exp(slow), jnp.exp(keep), jnp.broadcast_to(jnp.exp(offset), (heads, width)))
    ):
        for head in range(heads):
            out_ref[head, kind : kind + 1, :] = value[head : head + 1]


def first_kernel(per_row, qkv_ref, gate_ref, up_ref, *refs):
    *vectors, bias_ref, maps_ref, out_ref = refs
    shard, wide = qkv_ref.shape
    heads = gate_ref.shape[0]
    lane = lax.broadcasted_iota(jnp.int32, (shard, 128), 1)

    def column(ref, stride, first):
        n = ref.shape[0]
        value = jnp.broadcast_to(ref[...].astype(F32)[None, :], (shard, n))
        row_at = lax.broadcasted_iota(jnp.int32, (shard, n), 0)
        line_at = lax.broadcasted_iota(jnp.int32, (shard, n), 1)
        return jnp.sum(jnp.where(line_at == row_at * stride + first, value, 0.0), axis=1, keepdims=True)

    small = jnp.zeros((shard, 128), F32)
    columns = [column(up_ref, per_row, i) for i in range(per_row)] + [column(ref, 1, 0) for ref in vectors]
    for i, value in enumerate(columns):
        small = jnp.where(lane == heads + i, value, small)
    at = heads + len(columns)
    bias = jnp.broadcast_to(bias_ref[...][None, :], (shard, bias_ref.shape[0]))
    for part in split_rows(bias):
        for i in range(bias_ref.shape[0]):
            small = jnp.where(lane == at, part[:, i : i + 1], small)
            at += 1
    for i in range(heads):
        small = jnp.where(lane == i, column(gate_ref.at[i], 1, 0), small)
    out_ref[:, :wide] = qkv_ref[...]
    out_ref[:, wide : wide + 128] = small.astype(BF16)
    out_ref[:, wide + 128 :] = maps_ref[...]


def rest_kernel(out_ref_w, up_ref, down_ref, out_ref):
    shard, width = out_ref_w.shape
    out_ref[:shard] = out_ref_w[...]
    blocks = up_ref.shape[1] // width
    for i in range(blocks):
        out_ref[shard * (i + 1) : shard * (i + 2)] = up_ref[:, i * width : (i + 1) * width]
    out_ref[shard * (blocks + 1) :] = down_ref[...]


def features(unit, fmt, scale):
    sine, cosine = sine_cosine(dot(fmt, unit, (1, 0)))
    return (jnp.concatenate([sine, cosine], axis=0) * scale).astype(BF16)


def forward_kernel(tile, qkv_ref, fmt_ref, rows_ref, qf_ref, kf_ref, nu_ref, state_ref):
    width = qkv_ref.shape[-1]
    fmt = fmt_ref[0]
    scale = 1.0 / math.sqrt(fmt.shape[0])
    mask = lower_mask(tile)
    state = None
    for at in range(0, width, tile):
        here = pl.ds(at, tile)
        query = qkv_ref[0, 0, :, here].astype(F32)
        key = qkv_ref[0, 1, :, here].astype(F32)
        query = (query * lax.rsqrt(jnp.sum(query * query, axis=0, keepdims=True) + 1e-06)).astype(BF16)
        key = (key * lax.rsqrt(jnp.sum(key * key, axis=0, keepdims=True) + 1e-06)).astype(BF16)
        qf = features(query, fmt, scale)
        kf = features(key, fmt, scale)
        qf_ref[0, :, here] = qf
        kf_ref[0, :, here] = kf
        running = rows_ref[0, 0:1, here]
        lead = rows_ref[0, 1:2, here]
        last = running[:, tile - 1 : tile]
        values = augmented(qkv_ref[0, 2, :, here], 1.0)
        weights = jnp.where(mask, jnp.exp(outer_sum(lead, running)), 0.0)
        scores = (dot(kf, qf, (0, 0)) * weights).astype(BF16)
        numer = dot(values.astype(BF16), scores, (1, 0))
        if state is not None:
            numer = numer + jnp.exp(running) * dot(state.astype(BF16), qf, (1, 0))
        nu_ref[0, :, here] = numer[: nu_ref.shape[1]]
        tail = (values * jnp.exp(last + lead)).astype(BF16)
        new = dot(tail, kf, (1, 1))
        state = new if state is None else jnp.exp(last) * state + new
    state_ref[0] = state[: state_ref.shape[1]]


def enter_kernel(state_ref, qf_ref, rows_ref, nu_ref, mixed_ref, total_ref):
    state = padded(state_ref[0])
    high = state.astype(BF16)
    rest = (state - high.astype(F32)).astype(BF16)
    qf = qf_ref[0]
    rows = nu_ref.shape[1]
    extra = (dot(high, qf, (1, 0)) + dot(rest, qf, (1, 0)))[:rows]
    total = nu_ref[0] + jnp.exp(rows_ref[0, 2:3, :]) * extra
    total_ref[0] = total
    size = mixed_ref.shape[1]
    denom = total[size : size + 1]
    floor = softplus(4.0 * denom) * 0.25 + 0.1
    mixed_ref[0] = (total[:size] / floor).astype(BF16)


def padded(state):
    return jnp.concatenate([state, jnp.zeros((AUG - ROWS, state.shape[1]), F32)], axis=0)


def softplus(x):
    return jnp.maximum(x, 0.0) + jnp.log1p(jnp.exp(-jnp.abs(x)))


def leave_kernel(grad_ref, total_ref, qf_ref, rows_ref, a_ref, back_ref):
    grad = grad_ref[0].astype(F32)
    size = grad.shape[0]
    numer = total_ref[0, :size]
    denom = total_ref[0, size : size + 1]
    inverse = 1.0 / (softplus(4.0 * denom) * 0.25 + 0.1)
    inner = jnp.sum(grad * numer, axis=0, keepdims=True)
    by_denom = -inner * jax.nn.sigmoid(4.0 * denom) * inverse * inverse
    whole = augmented(grad * inverse, by_denom)
    a_ref[0] = whole.astype(BF16)
    back = dot((whole * jnp.exp(rows_ref[0, 2:3, :])).astype(BF16), qf_ref[0], (1, 1))
    back_ref[0] = back[: back_ref.shape[1]]


def unit_back(raw, unit_grad):
    inverse = lax.rsqrt(jnp.sum(raw * raw, axis=0, keepdims=True) + 1e-06)
    inner = jnp.sum(raw * unit_grad, axis=0, keepdims=True)
    return inverse * (unit_grad - raw * (inner * inverse * inverse))


def angle_back(feat, grad):
    half = feat.shape[0] // 2
    feat = feat.astype(F32)
    return (grad[:half] * feat[half:] - grad[half:] * feat[:half]).astype(BF16)


def backward_kernel(
    tile, qkv_ref, fm_ref, rows_ref, qf_ref, kf_ref, a_ref, state_ref, back_ref, out_ref, logit_ref
):
    width = qkv_ref.shape[-1]
    size = qkv_ref.shape[2]
    fm = fm_ref[0]
    mask = lower_mask(tile)
    spots = list(range(0, width, tile))
    states = [padded(state_ref[0])]
    for at in spots:
        here = pl.ds(at, tile)
        last = rows_ref[0, 0:1, at + tile - 1 : at + tile]
        values = augmented(qkv_ref[0, 2, :, here], 1.0)
        tail = (values * jnp.exp(last + rows_ref[0, 1:2, here])).astype(BF16)
        states.append(jnp.exp(last) * states[-1] + dot(tail, kf_ref[0, :, here], (1, 1)))
    back = padded(back_ref[0])
    ones = jnp.ones((AUG, tile), BF16)

    def whole_sum(x):
        return jnp.sum(jnp.sum(x, axis=0, keepdims=True), axis=1, keepdims=True)

    pieces = []
    for index in reversed(range(len(spots))):
        at = spots[index]
        here = pl.ds(at, tile)
        running = rows_ref[0, 0:1, here]
        lead = rows_ref[0, 1:2, here]
        last = running[:, tile - 1 : tile]
        decay = jnp.exp(running)
        tail = jnp.exp(last + lead)
        qf = qf_ref[0, :, here]
        kf = kf_ref[0, :, here]
        a = a_ref[0, :, here]
        values = augmented(qkv_ref[0, 2, :, here], 1.0).astype(BF16)
        state = states[index].astype(BF16)
        low_back = back.astype(BF16)
        weights = jnp.where(mask, jnp.exp(outer_sum(lead, running)), 0.0)
        alike = dot(kf, qf, (0, 0))
        scores = (alike * weights).astype(BF16)
        pairs = dot(values, a, (0, 0)) * weights
        terms = (pairs * alike).astype(BF16)
        pairs = pairs.astype(BF16)
        from_state = decay * dot(state, a, (0, 0))
        from_back = tail * dot(low_back, values, (0, 0))
        query_feat = dot(kf, pairs, (1, 0)) + from_state
        key_feat = dot(qf, pairs, (1, 1)) + from_back
        by_query = dot(ones, terms, (1, 0))[:1]
        by_key = dot(ones, terms, (1, 1))[:1]
        state_term = jnp.sum(qf.astype(F32) * from_state, axis=0, keepdims=True)
        back_term = jnp.sum(kf.astype(F32) * from_back, axis=0, keepdims=True)
        through = jnp.exp(last) * whole_sum(back * states[index])
        constant = jnp.sum(back_term, axis=1, keepdims=True) + through
        pieces.append((by_query - by_key + state_term - back_term, by_key + back_term, constant))
        value = dot(a[:size], scores, (1, 1)) + tail * dot(low_back[:size], kf, (1, 0))
        query_unit = dot(fm, angle_back(qf, query_feat), (1, 0))
        key_unit = dot(fm, angle_back(kf, key_feat), (1, 0))
        out_ref[0, 0, :, here] = unit_back(qkv_ref[0, 0, :, here].astype(F32), query_unit).astype(BF16)
        out_ref[0, 1, :, here] = unit_back(qkv_ref[0, 1, :, here].astype(F32), key_unit).astype(BF16)
        out_ref[0, 2, :, here] = value.astype(BF16)
        back = jnp.exp(last) * back + dot((a.astype(F32) * decay).astype(BF16), qf, (1, 1))
    place = lax.broadcasted_iota(jnp.int32, (ROWS, tile), 0)
    sums = jnp.zeros((ROWS, tile), F32)
    for index, piece in enumerate(pieces[::-1]):
        sums = jnp.where(place == index, piece[0], sums)
    place = lax.broadcasted_iota(jnp.int32, (ROWS, tile), 1)
    step = 1
    while step < tile:
        sums = sums + jnp.where(place < tile - step, pltpu.roll(sums, tile - step, 1), 0.0)
        step *= 2
    for index, (_, by_key, constant) in enumerate(pieces[::-1]):
        here = pl.ds(spots[index], tile)
        keep_grad = sums[index : index + 1] + constant
        logit = keep_grad * rows_ref[0, 3:4, here] - by_key * rows_ref[0, 4:5, here]
        logit_ref[0, :, here] = jnp.broadcast_to(logit, (ROWS, tile))


def per_head(kernel, outs, heads, *arrays, us, far=()):
    def spec(shape, offset):
        rest = len(shape) - 1
        return pl.BlockSpec((1,) + tuple(shape[1:]), lambda h: (h + offset,) + (0,) * rest)

    nbytes = sum(heads * math.prod(a.shape[1:]) * a.dtype.itemsize for a, _ in arrays)
    nbytes += sum(math.prod(s) * jnp.dtype(d).itemsize for s, d in outs)
    return pl.pallas_call(
        kernel,
        grid=(heads,),
        in_specs=[spec(a.shape, offset) for a, offset in arrays],
        out_specs=[spec(s, 0) for s, _ in outs],
        out_shape=[jax.ShapeDtypeStruct(s, d) if i not in far else pltpu.HBM(s, d) for i, (s, d) in enumerate(outs)],
        compiler_params=pltpu.CompilerParams(vmem_limit_bytes=24 * 2**20),
        cost_estimate=pl.CostEstimate(flops=int(us * 1.1e9), bytes_accessed=int(nbytes), transcendentals=0),
    )(*[a for a, _ in arrays])


def norm_parts(x):
    average = jnp.mean(x, axis=0, keepdims=True)
    centered = x - average
    inverse = lax.rsqrt(jnp.mean(centered * centered, axis=0, keepdims=True) + 1e-05)
    return centered * inverse, inverse


def norm_back(hat, inverse, gain, grad):
    scaled = grad * gain
    first = jnp.mean(scaled, axis=0, keepdims=True)
    second = jnp.mean(scaled * hat, axis=0, keepdims=True)
    return (scaled - first - hat * second) * inverse


def product(spec, a, b):
    return jnp.einsum(spec, a, b, preferred_element_type=F32)


def local(
    tokens, w_qkv, w_gate, gate_bias, w_out, w_up, up_bias, w_down, down_bias, pre_gain, pre_shift,
    mid_gain, mid_shift, feature_map, state_init, keysum_init, out_cot, state_cot, keysum_cot,
):
    sizes = {axis: lax.axis_size(axis) for axis in ALL}
    count_hd, count_blk = sizes["hd"], sizes["blk"]
    devices = sizes["rows"] * count_blk * count_hd
    both = count_blk * count_hd
    seqs, part, width = tokens.shape
    own_heads, head_dim, rand = feature_map.shape
    heads = own_heads * count_hd
    feat = 2 * rand
    hidden_size = w_up.shape[1]
    length = seqs * part
    tile = 256 if length % 256 == 0 else 128
    shard = w_qkv.shape[0]
    aug, held_rows = head_dim + AUG, head_dim + ROWS
    place_hd, place_blk = lax.axis_index("hd"), lax.axis_index("blk")
    place = place_blk * count_hd + place_hd
    member, chunk = place % seqs, place // seqs
    chunks = both // seqs

    def to_chunk(x):
        return pieces_trip(x, BOTH, both, seqs, member)

    def from_chunk(x):
        return pieces_trip(x.reshape(seqs, part, width), BOTH, both, seqs, member)

    per_row = hidden_size // width
    n_small = heads + per_row + 5
    shares = devices // count_hd
    maps = feature_map.reshape(shares, shard, -1)
    spot = lax.axis_index("rows") * count_blk + place_blk
    maps = lax.dynamic_index_in_dim(maps, spot, 0, False)
    first_packed = pl.pallas_call(
        functools.partial(first_kernel, per_row),
        out_shape=jax.ShapeDtypeStruct((shard, 3 * width + 128 + maps.shape[1]), BF16),
    )(w_qkv, w_gate.T, up_bias, down_bias, pre_gain, pre_shift, mid_gain, mid_shift, gate_bias, maps)

    half = 3 * width // 2
    one, two = routes(sizes)
    stages = range(len(one))

    def gathers(streams, at):
        return [gather_trip(cur, route[at], sizes) for cur, route in zip(streams, (one, two))]

    whole = gather_trip(gather_start(first_packed, sizes), one[0], sizes).land()
    first = [whole[..., :half], whole[..., half:]]
    tokens_trip = to_chunk(after(tokens, *first))
    second = pl.pallas_call(
        rest_kernel, out_shape=jax.ShapeDtypeStruct((shard * (per_row + 1) + w_down.shape[0], width), BF16)
    )(*after((w_out, w_up, w_down), first_packed))
    second = lax.all_gather(second, ALL, axis=0)

    at_start = chunk == 0
    at_end = chunk == chunks - 1
    offers = []
    for other in range(count_hd):
        spot = place_blk * count_hd + other
        pick = lambda a: lax.dynamic_index_in_dim(a, spot % seqs, 0, False)
        state = jnp.where(spot // seqs == 0, pick(state_init), pick(state_cot))
        keysum = jnp.where(spot // seqs == 0, pick(keysum_init), pick(keysum_cot))
        keysum = jnp.pad(keysum[:, None], ((0, 0), (0, ROWS - 1), (0, 0)))
        offers.append(jnp.concatenate([jnp.swapaxes(state, -1, -2), keysum], axis=1))
    offers = after(jnp.stack(offers), *first)

    cut = len(one) - len([b for b in bits_of(sizes) if b[0] == "rows"]) + 1
    for at in stages[1:]:
        first = landed(gathers(first, at))
        if at == cut - 1:
            edge_trip = pieces_trip(after(offers, *first), "hd", count_hd, count_hd, place_hd)
    qkv_halves = [gather_end(f, sizes) for f in first]
    full_small = qkv_halves[1][:, half:]
    qkv_halves[1] = qkv_halves[1][:, :half]
    full_gate = full_small[:, :heads]
    full_up_bias = full_small[:, heads : heads + per_row].reshape(hidden_size, 1).astype(F32)
    vectors = [full_small[:, heads + per_row + i : heads + per_row + i + 1].astype(F32) for i in range(5)]
    full_down_bias, gain_1, shift_1, gain_2, shift_2 = vectors
    maps = full_small[:, -maps.shape[1] :].reshape(shares, count_hd, shard, -1)
    fm = maps.transpose(1, 0, 2, 3).reshape(heads, head_dim, rand)
    fmt = fm.transpose(0, 2, 1)

    def hop_trip(added, forward):
        pairs = [(i, i + seqs) for i in range(both - seqs)]
        pairs = pairs if forward else [(b, a) for a, b in pairs]
        outer = at_start if forward else at_end
        choose = lambda parts: jnp.where(outer, edge, parts[1].astype(F32))
        state = edge
        for last in range(chunks - 1):
            trip = Trip(None, [((added + decay * state).astype(BF16), BOTH, pairs)], choose)
            if last < chunks - 2:
                state = trip.land()
        return trip

    x = tokens_trip.land().reshape(length, width).T.astype(F32)
    hat_1, inverse_1 = norm_parts(x)
    normed = (hat_1 * gain_1 + shift_1).astype(BF16)
    rows = pl.pallas_call(
        functools.partial(gate_kernel, tile, heads, own_heads, shard, n_small),
        out_shape=jax.ShapeDtypeStruct((heads, ROWS, length), F32),
        compiler_params=pltpu.CompilerParams(vmem_limit_bytes=24 * 2**20),
    )(full_small, normed)
    packed = product("dc,dt->ct", jnp.concatenate(qkv_halves, axis=1), normed)
    packed = packed.astype(BF16).reshape(heads, 3, head_dim, length)
    decay = rows[:, 5:6, :1]

    cot_trip = to_chunk(after(out_cot, normed))
    qf, kf, partial_nu, chunk_state = per_head(
        functools.partial(forward_kernel, tile),
        [
            ((heads, feat, length), BF16),
            ((heads, feat, length), BF16),
            ((heads, held_rows, length), F32),
            ((heads, held_rows, feat), F32),
        ],
        heads, (departed(packed, cot_trip, edge_trip), 0), (fmt, 0), (rows, 0), us=18, far=(1,),
    )
    edge = edge_trip.land(chunk_state).reshape(heads, held_rows, feat)
    hop = hop_trip(chunk_state, True)
    cot = cot_trip.land(hop.messages()).reshape(length, width).T
    second = after(second, hop.messages())
    full_out = second[:, :shard].reshape(width, width)
    full_up = [second[:, i : i + shard].reshape(width, width) for i in range(shard, shard * (per_row + 1), shard)]
    full_up = jnp.concatenate(full_up, axis=1)
    full_down = second[:, shard * (per_row + 1) :].reshape(hidden_size, width)
    entering = hop.land(cot, full_out, full_up, full_down)
    mixed, total_nu = per_head(
        enter_kernel,
        [((heads, head_dim, length), BF16), ((heads, held_rows, length), F32)],
        heads, (entering, 0), (qf, 0), (rows, 0), (partial_nu, 0), us=3,
    )
    mixed = mixed.reshape(width, length)

    attended = x + product("io,it->ot", full_out, mixed)
    hat_2, inverse_2 = norm_parts(attended)
    hidden = (hat_2 * gain_2 + shift_2).astype(BF16)
    before = product("df,dt->ft", full_up, hidden) + full_up_bias
    cumulative = 0.5 + 0.5 * lax.erf(before * math.sqrt(0.5))
    density = jnp.exp(-0.5 * before * before) * (1.0 / math.sqrt(2.0 * math.pi))
    active = (before * cumulative).astype(BF16)
    before_grad = (product("fo,ot->ft", full_down, cot) * (cumulative + before * density)).astype(BF16)
    hidden_grad = product("df,ft->dt", full_up, before_grad)
    cot_full = cot.astype(F32)
    attended_grad = cot_full + norm_back(hat_2, inverse_2, gain_2, hidden_grad)
    attended_low = attended_grad.astype(BF16)
    mixed_grad = product("io,ot->it", full_out, attended_low).astype(BF16).reshape(heads, head_dim, length)

    a, chunk_back = per_head(
        leave_kernel,
        [((heads, aug, length), BF16), ((heads, held_rows, feat), F32)],
        heads, (mixed_grad, 0), (total_nu, 0), (qf, 0), (rows, 0), us=3,
    )
    hop = hop_trip(chunk_back, False)

    def scatters(streams, at, kind=BF16):
        return [scatter_trip(cur, route[at], sizes, kind) for cur, route in zip(streams, (one, two))]

    held = departed(hidden, hop)
    up_grad = product("dt,ft->df", held, before_grad).astype(BF16)
    down_grad = product("ft,ot->fo", active, cot).astype(BF16)
    early = [scatter_start(up_grad, sizes), scatter_start(down_grad, sizes)]
    early_trips = scatters(early, len(one) - 1)
    result = attended + product("fo,ft->ot", departed(full_down, *early_trips), active) + full_down_bias
    result = result.astype(BF16)
    out_grad = product("it,ot->io", mixed, attended_low).astype(BF16)
    early = landed(early_trips, result)
    for at in stages[-2 : cut - 1 : -1]:
        early = landed(scatters(early, at))
    output_trip = from_chunk(result.T)
    back = hop.land(result)
    down_bias_grad = jnp.sum(cot_full, axis=1)
    up_bias_grad = jnp.sum(before_grad.astype(F32), axis=1)
    gain_2_grad = jnp.sum(hidden_grad * hat_2, axis=1)
    shift_2_grad = jnp.sum(hidden_grad, axis=1)

    added = jnp.where(at_start, chunk_back, chunk_state)
    ends = (added + decay * jnp.where(at_start, back, entering)).astype(BF16)
    ends = lax.all_gather(ends, BOTH, axis=0)

    own = heads // 2

    def backward(i, part_qkv):
        grad, logit = per_head(
            functools.partial(backward_kernel, tile),
            [((own, 3, head_dim, length), BF16), ((own, ROWS, length), F32)],
            own, (part_qkv, i * own), (fm, i * own), (rows, i * own), (qf, i * own), (kf, i * own),
            (a, i * own), (entering, i * own), (back, i * own), us=9,
        )
        return grad.reshape(half, length), logit[:, 0]

    early_trips = scatters(early, cut - 1)
    grads = [backward(0, departed(packed, output_trip, *early_trips))]
    early = landed(early_trips, grads[0])
    output = output_trip.land(grads[0])
    for at in stages[cut - 2 : 1 : -1]:
        early = landed(scatters(early, at))
    early_trips = scatters(early, 1)
    qkv_grad = [product("dt,ct->dc", normed, grads[0][0]).astype(BF16)]
    late_one = scatter_start(jnp.concatenate([qkv_grad[0], out_grad], axis=1), sizes)
    late_trip = scatter_trip(late_one, one[-1], sizes)
    grads.append(backward(1, departed(packed, late_trip, *early_trips)))
    late_one = late_trip.land(grads[1])
    late_trip = scatter_trip(late_one, one[-2], sizes)

    gate_low = jnp.concatenate([g[1] for g in grads])
    bias_grad = jnp.sum(gate_low, axis=1)
    gate_low = gate_low.astype(BF16)
    last_grad = departed(grads[1][0], late_trip)
    normed_grad = (
        product("dc,ct->dt", qkv_halves[0], grads[0][0])
        + product("dc,ct->dt", qkv_halves[1], last_grad)
        + product("dh,ht->dt", full_gate, gate_low)
    )
    qkv_grad.append(product("dt,ct->dc", normed, last_grad).astype(BF16))
    gate_grad = product("dt,ht->dh", normed, gate_low)
    gain_1_grad = jnp.sum(normed_grad * hat_1, axis=1)
    shift_1_grad = jnp.sum(normed_grad, axis=1)
    grad_small = jnp.concatenate(
        [gate_grad, up_bias_grad.reshape(width, per_row)]
        + [v[:, None] for v in (down_bias_grad, gain_1_grad, shift_1_grad, gain_2_grad, shift_2_grad)]
        + [jnp.broadcast_to(bias_grad[None], (width, heads))],
        axis=1,
    )
    fine = grad_small.shape[1] + -grad_small.shape[1] % 128
    grad_small = in_two(jnp.pad(grad_small, ((0, 0), (0, fine - grad_small.shape[1])))).astype(BF16)
    late_two = scatter_start(jnp.concatenate([qkv_grad[1], grad_small], axis=1), sizes)
    other_trip = scatter_trip(late_two, two[-1], sizes, fine=fine)
    late_one = late_trip.land(other_trip.messages())
    late_trip = scatter_trip(late_one, one[-3], sizes)
    late_two = other_trip.land(late_trip.messages())
    other_trip = scatter_trip(late_two, two[-2], sizes, fine=fine)
    early = landed(early_trips, other_trip.messages())
    held = departed(inverse_1, other_trip, late_trip)
    token_grad = (attended_grad + norm_back(hat_1, held, gain_1, normed_grad)).astype(BF16).T
    late_one = late_trip.land(token_grad)
    late_two = other_trip.land(token_grad)
    for step in one[-4:0:-1]:
        late_one = scatter_trip(late_one, step, sizes).land()
    for step in two[-3:1:-1]:
        late_two = scatter_trip(late_two, step, sizes, fine=fine).land()
    late_trip = scatter_trip(late_one, one[0], sizes, F32)
    other_trip = scatter_trip(late_two, two[1], sizes, fine=fine)
    tokens_trip = from_chunk(departed(token_grad, late_trip, other_trip))
    early = after(early, tokens_trip.messages())
    early_trips = scatters(early, 0, F32)
    late_two = other_trip.land(tokens_trip.messages())
    other_trip = scatter_trip(late_two, two[0], sizes, F32, fine=fine)

    def finished(rows):
        state = lax.dynamic_slice_in_dim(rows, place_hd * own_heads, own_heads, 1).astype(F32)
        return jnp.swapaxes(state[:, :, :head_dim], -1, -2), state[:, :, head_dim]

    ends = after(ends, other_trip.messages())
    state_start, keysum_start = finished(ends[:seqs])
    state_final, keysum_final = finished(ends[both - seqs :])
    states = (state_start, state_final)
    up_own, down_own = (scatter_end(e, sizes) for e in landed(early_trips, *states))
    late_one, late_two = (scatter_end(e, sizes) for e in landed([late_trip, other_trip], *states))
    token_grad = tokens_trip.land(*states)

    qkv_own = jnp.concatenate([late_one[:, :half], late_two[:, :half]], axis=1)
    out_own = late_one[:, half:]
    own_small = late_two[:, half:]
    gate_own = own_small[:, :heads]
    up_bias_own = own_small[:, heads : heads + per_row].reshape(-1)
    down_bias_own, gain_1_own, shift_1_own, gain_2_own, shift_2_own = (
        own_small[:, heads + per_row + i] for i in range(5)
    )
    bias_sum = own_small[0, heads + per_row + 5 : 2 * heads + per_row + 5]
    bias_own = lax.dynamic_slice_in_dim(bias_sum, place_hd * own_heads, own_heads)
    return (
        output, token_grad, qkv_own, gate_own, bias_own, out_own, up_own, up_bias_own, down_own, down_bias_own,
        gain_1_own, shift_1_own, gain_2_own, shift_2_own, state_final, keysum_final, state_start, keysum_start,
    )


def solution(mesh):
    by_tokens = P("rows", ("blk", "hd"), None)
    by_rows = P(ALL, None)
    by_entry = P(ALL)
    by_head = P("hd")
    by_state = P("rows", "hd", None, None)
    by_keysum = P("rows", "hd", None)
    in_specs = (
        by_tokens, by_rows, by_rows, by_head, by_rows, by_rows, by_entry, by_rows, by_entry, by_entry, by_entry,
        by_entry, by_entry, P("hd", None, None), by_state, by_keysum, by_tokens, by_state, by_keysum,
    )
    out_specs = (
        by_tokens, by_tokens, by_rows, by_rows, by_head, by_rows, by_rows, by_entry, by_rows, by_entry,
        by_entry, by_entry, by_entry, by_entry, by_state, by_keysum, by_state, by_keysum,
    )
    return jax.shard_map(local, mesh=mesh, in_specs=in_specs, out_specs=out_specs, check_vma=False)
```

```python
import functools
import math

import jax
import jax.numpy as jnp
from jax import lax
from jax.experimental import pallas as pl
from jax.experimental.pallas import tpu as pltpu
from jax.sharding import PartitionSpec as P

ALL = ("rows", "blk", "hd")
BOTH = ("blk", "hd")
F32 = jnp.float32
BF16 = jnp.bfloat16
AUG = 16
ROWS = 8


def after(x, *others):
    return lax.optimization_barrier((x,) + others)[0]


class Trip:
    def __init__(self, own, sends, finish):
        self.own, self.sends, self.finish = own, sends, finish

    def messages(self):
        return [send[0] for send in self.sends]

    def land(self, *others):
        got = [lax.ppermute(*send) for send in self.sends]
        if others:
            got = after(got, *others)
        return self.finish([self.own] + got)


def departed(x, *trips):
    return after(x, [trip.messages() for trip in trips])


def landed(trips, *others):
    return [trip.land(*others) for trip in trips]


def turned(size, bit):
    return [(i, i ^ bit) for i in range(size)]


def ordered(parts, me):
    parts = list(parts)
    bit = 1
    while bit < len(parts):
        there = (me & bit) != 0
        parts = [jnp.where(there, parts[i ^ bit], parts[i]) for i in range(len(parts))]
        bit *= 2
    return parts


def pieces_trip(x, axis, size, group, me):
    sends = [(lax.dynamic_index_in_dim(x, me ^ k, 0, False), axis, turned(size, k)) for k in range(1, group)]
    own = lax.dynamic_index_in_dim(x, me, 0, False)
    return Trip(own, sends, lambda parts: jnp.stack(ordered(parts, me)))


def bits_of(sizes):
    found = []
    for axis in ALL:
        bit = sizes[axis] // 2
        while bit:
            found.append((axis, bit))
            bit //= 2
    return found


def routes(sizes):
    own = lambda axis: [[b] for b in bits_of(sizes) if b[0] == axis]
    z = [[b for b in bits_of(sizes) if b[0] == "blk"]]
    y, x = own("hd"), own("rows")
    return z + y + x[:1] + x[1:], z + x[:1] + y + x[1:]


def partners(step, sizes):
    axis, low = step[0][0], step[-1][1]
    count = 2 ** len(step)
    place = (lax.axis_index(axis) // low) % count
    return axis, sizes[axis], place, [k * low for k in range(count)]


def gather_start(x, sizes):
    return x.reshape((1,) * len(bits_of(sizes)) + x.shape)


def gather_trip(cur, step, sizes):
    axis, size, place, offsets = partners(step, sizes)
    dim = bits_of(sizes).index(step[0])
    shape = cur.shape[:dim] + (2,) * len(step) + cur.shape[dim + len(step) :]
    sends = [(cur, axis, turned(size, k)) for k in offsets[1:]]
    return Trip(cur, sends, lambda parts: jnp.concatenate(ordered(parts, place), axis=dim).reshape(shape))


def gather_end(cur, sizes):
    lead = len(bits_of(sizes))
    return cur.reshape((-1,) + cur.shape[lead + 1 :])


def scatter_start(x, sizes):
    bits = bits_of(sizes)
    return [x.reshape((2,) * len(bits) + (x.shape[0] // 2 ** len(bits),) + x.shape[1:])]


def in_two(x):
    high = lax.reduce_precision(x, 8, 7)
    return jnp.concatenate([high, x - high], axis=-1)


def term_sum(terms, fine):
    total = terms[0].astype(F32)
    for term in terms[1:]:
        total = total + term.astype(F32)
    if fine:
        total = [total[..., : -2 * fine], total[..., -2 * fine : -fine] + total[..., -fine:]]
    return total


def scatter_trip(terms, step, sizes, fine=0):
    axis, size, place, offsets = partners(step, sizes)
    dim = bits_of(sizes).index(step[0])
    shape = terms[0].shape
    lead, rest = shape[:dim], shape[dim + len(step) :]
    merged = [term.reshape(lead + (len(offsets),) + rest) for term in terms]

    def part(k):
        picked = [lax.dynamic_index_in_dim(term, place ^ k, dim, True) for term in merged]
        if len(picked) == 1:
            return picked[0]
        total = term_sum(picked, fine)
        return (jnp.concatenate([total[0], in_two(total[1])], axis=-1) if fine else total).astype(BF16)

    sends = [(part(k), axis, turned(size, offset)) for k, offset in enumerate(offsets) if k]
    here = lead + (1,) * len(step) + rest
    return Trip(part(0), sends, lambda parts: [p.reshape(here) for p in parts])


def scatter_end(terms, sizes):
    return [term.reshape(term.shape[len(bits_of(sizes)) :]) for term in terms]


def dot(a, b, contract):
    return lax.dot_general(a, b, ((contract[:1], contract[1:]), ((), ())), preferred_element_type=F32)


def sine_cosine(x, scale):
    turns = jnp.round(x * (1.0 / math.pi))
    rest = (x - turns * 3.140625) - turns * 9.67653589793e-4
    half = turns * 0.5
    sign = scale - (4.0 * scale) * (half - jnp.floor(half))
    sq = rest * rest
    sine = sq * 2.600052801290691e-06 - 0.0001980661418962755
    sine = sine * sq + 0.008333017275116794
    sine = sine * sq - 0.16666657095676896
    sine = rest + rest * (sq * sine)
    cosine = sq * 2.319437094031874e-05 - 0.001385592644003374
    cosine = cosine * sq + 0.04166398934467621
    cosine = cosine * sq - 0.4999993228818705
    cosine = cosine * sq + 1.0
    return sine * sign, cosine * sign


def split_rows(x):
    high = x.astype(BF16).astype(F32)
    rest = x - high
    middle = rest.astype(BF16).astype(F32)
    return high, middle, rest - middle


def outer_sum(column, row):
    width = row.shape[1]
    place = lax.broadcasted_iota(jnp.int32, (AUG, width), 0)

    def lay(parts, first):
        out = jnp.zeros((AUG, width), F32)
        for i, part in enumerate(parts):
            out = jnp.where(place == first + i, part, out)
        return jnp.where((place >= 3 - first) & (place < 6 - first), 1.0, out).astype(BF16)

    return dot(lay(split_rows(column), 0), lay(split_rows(row), 3), (0, 0))


def augmented(v, ones):
    width = v.shape[1]
    place = lax.broadcasted_iota(jnp.int32, (AUG, width), 0)
    extra = jnp.where(place == 0, ones, 0.0)
    return jnp.concatenate([v.astype(F32), extra], axis=0)


def lower_mask(c):
    return lax.broadcasted_iota(jnp.int32, (c, c), 0) <= lax.broadcasted_iota(jnp.int32, (c, c), 1)


def gate_kernel(tile, heads, own_heads, shard, first_bias, small_ref, normed_ref, out_ref):
    raw = dot(small_ref[:, :128], normed_ref[...], (0, 0))[:heads].astype(BF16).astype(F32)
    groups = heads // own_heads
    block = small_ref[: groups * shard, :128].astype(F32)
    head = lax.broadcasted_iota(jnp.int32, (heads, 128), 0)
    lane = lax.broadcasted_iota(jnp.int32, (heads, 128), 1)
    bias = jnp.zeros((heads, 1), F32)
    for group in range(groups):
        wanted = False
        for part in range(3):
            wanted = wanted | (lane == first_bias + part * own_heads + head - group * own_heads)
        wanted = wanted & (head >= group * own_heads) & (head < (group + 1) * own_heads)
        bias = bias + jnp.sum(jnp.where(wanted, block[group * shard : group * shard + 1], 0.0), axis=1, keepdims=True)
    logit = raw + bias
    heads, width = logit.shape
    small = jnp.log1p(jnp.exp(-jnp.abs(logit)))
    keep = jnp.minimum(logit, 0.0) - small
    slow = jnp.minimum(-logit, 0.0) - small
    place = lax.broadcasted_iota(jnp.int32, (heads, width), 1)

    def sums(x, within):
        at = lax.rem(place, within)
        step = 1
        while step < within:
            x = x + jnp.where(at >= step, pltpu.roll(x, step, 1), 0.0)
            step *= 2
        return x

    running = sums(keep, tile)
    whole = running
    offset = jnp.zeros((heads, 1), F32)
    for at in range(0, width, tile):
        whole = jnp.where((place >= at) & (place < at + tile), running + offset, whole)
        offset = offset + running[:, at + tile - 1 : at + tile]
    for kind, value in enumerate(
        (running, slow - running, whole, jnp.exp(slow), jnp.exp(keep), jnp.broadcast_to(jnp.exp(offset), (heads, width)))
    ):
        for head in range(heads):
            out_ref[head, kind : kind + 1, :] = value[head : head + 1]


def first_kernel(per_row, qkv_ref, gate_ref, up_ref, *refs):
    *vectors, bias_ref, maps_ref, out_ref = refs
    shard, wide = qkv_ref.shape
    heads = gate_ref.shape[0]
    lane = lax.broadcasted_iota(jnp.int32, (shard, 128), 1)

    def column(ref, stride, first):
        n = ref.shape[0]
        value = jnp.broadcast_to(ref[...].astype(F32)[None, :], (shard, n))
        row_at = lax.broadcasted_iota(jnp.int32, (shard, n), 0)
        line_at = lax.broadcasted_iota(jnp.int32, (shard, n), 1)
        return jnp.sum(jnp.where(line_at == row_at * stride + first, value, 0.0), axis=1, keepdims=True)

    small = jnp.zeros((shard, 128), F32)
    columns = [column(up_ref, per_row, i) for i in range(per_row)] + [column(ref, 1, 0) for ref in vectors]
    for i, value in enumerate(columns):
        small = jnp.where(lane == heads + i, value, small)
    at = heads + len(columns)
    bias = jnp.broadcast_to(bias_ref[...][None, :], (shard, bias_ref.shape[0]))
    for part in split_rows(bias):
        for i in range(bias_ref.shape[0]):
            small = jnp.where(lane == at, part[:, i : i + 1], small)
            at += 1
    for i in range(heads):
        small = jnp.where(lane == i, column(gate_ref.at[i], 1, 0), small)
    out_ref[:, :wide] = qkv_ref[...]
    out_ref[:, wide : wide + 128] = small.astype(BF16)
    out_ref[:, wide + 128 :] = maps_ref[...]


def rest_kernel(out_ref_w, up_ref, down_ref, out_ref):
    shard, width = out_ref_w.shape
    out_ref[:shard] = out_ref_w[...]
    blocks = up_ref.shape[1] // width
    for i in range(blocks):
        out_ref[shard * (i + 1) : shard * (i + 2)] = up_ref[:, i * width : (i + 1) * width]
    out_ref[shard * (blocks + 1) :] = down_ref[...]


def last_kernel(per_row, heads, n_one, hd_ref, *refs):
    ones, twos, outs = refs[:n_one], refs[n_one : -10], refs[-10:]
    qkv_ref, gate_ref, bias_ref, out_ref, up_ref = outs[:5]
    half = qkv_ref.shape[1] // 2
    shard = qkv_ref.shape[0]
    one = sum(ref[...].astype(F32) for ref in ones)
    two = sum(ref[...].astype(F32) for ref in twos)
    fine = (two.shape[1] - half) // 2
    small = two[:, half : half + fine] + two[:, half + fine :]
    qkv_ref[:, :half] = one[:, :half]
    qkv_ref[:, half:] = two[:, :half]
    out_ref[...] = one[:, half:]
    gate_ref[...] = small[:, :heads]
    row_at = lax.broadcasted_iota(jnp.int32, (shard, fine), 0)
    lane_at = lax.broadcasted_iota(jnp.int32, (shard, fine), 1)

    def line(n, stride, columns):
        row_at = lax.broadcasted_iota(jnp.int32, (shard, n), 0)
        line_at = lax.broadcasted_iota(jnp.int32, (shard, n), 1)
        value = jnp.zeros((shard, n), F32)
        for j, column in enumerate(columns):
            value = jnp.where(line_at == row_at * stride + j, column, value)
        return jnp.sum(value, axis=0)

    up_ref[...] = line(shard * per_row, per_row, [small[:, heads + j : heads + j + 1] for j in range(per_row)])
    for i, ref in enumerate(outs[5:]):
        at = heads + per_row + i
        ref[...] = line(shard, 1, [small[:, at : at + 1]])
    own = bias_ref.shape[0]
    first = heads + per_row + 5 + hd_ref[0] * own
    column = jnp.sum(jnp.where(lane_at == first + row_at, small, 0.0), axis=1, keepdims=True)
    bias_ref[...] = line(own, 1, [column])


def ends_kernel(hd_ref, start_ref, final_ref, *outs):
    size = outs[0].shape[2]
    for ref, state_ref, key_ref in ((start_ref, *outs[:2]), (final_ref, *outs[2:])):
        for head in range(ref.shape[1]):
            rows = ref[0, head].astype(F32)
            state_ref[0, head] = rows[:size]
            key_ref[0, head : head + 1] = rows[size : size + 1]


def features(unit, fmt, scale):
    sine, cosine = sine_cosine(dot(fmt, unit, (1, 0)), scale)
    return jnp.concatenate([sine, cosine], axis=0).astype(BF16)


def forward_kernel(tile, qkv_ref, fmt_ref, rows_ref, qf_ref, kf_ref, nu_ref, state_ref):
    width = qkv_ref.shape[-1]
    fmt = fmt_ref[0]
    scale = 1.0 / math.sqrt(fmt.shape[0])
    mask = lower_mask(tile)
    state = None
    for at in range(0, width, tile):
        here = pl.ds(at, tile)
        query = qkv_ref[0, 0, :, here].astype(F32)
        key = qkv_ref[0, 1, :, here].astype(F32)
        query = (query * lax.rsqrt(jnp.sum(query * query, axis=0, keepdims=True) + 1e-06)).astype(BF16)
        key = (key * lax.rsqrt(jnp.sum(key * key, axis=0, keepdims=True) + 1e-06)).astype(BF16)
        qf = features(query, fmt, scale)
        kf = features(key, fmt, scale)
        qf_ref[0, :, here] = qf
        kf_ref[0, :, here] = kf
        running = rows_ref[0, 0:1, here]
        lead = rows_ref[0, 1:2, here]
        last = running[:, tile - 1 : tile]
        values = augmented(qkv_ref[0, 2, :, here], 1.0)
        weights = jnp.where(mask, jnp.exp(outer_sum(lead, running)), 0.0)
        scores = (dot(kf, qf, (0, 0)) * weights).astype(BF16)
        numer = dot(values.astype(BF16), scores, (1, 0))
        if state is not None:
            numer = numer + jnp.exp(running) * dot(state.astype(BF16), qf, (1, 0))
        nu_ref[0, :, here] = numer[: nu_ref.shape[1]]
        tail = (values * jnp.exp(last + lead)).astype(BF16)
        new = dot(tail, kf, (1, 1))
        state = new if state is None else jnp.exp(last) * state + new
    state_ref[0] = state[: state_ref.shape[1]]


def enter_kernel(state_ref, qf_ref, rows_ref, nu_ref, mixed_ref, total_ref):
    state = padded(state_ref[0])
    high = state.astype(BF16)
    rest = (state - high.astype(F32)).astype(BF16)
    qf = qf_ref[0]
    rows = nu_ref.shape[1]
    extra = (dot(high, qf, (1, 0)) + dot(rest, qf, (1, 0)))[:rows]
    total = nu_ref[0] + jnp.exp(rows_ref[0, 2:3, :]) * extra
    total_ref[0] = total
    size = mixed_ref.shape[1]
    denom = total[size : size + 1]
    floor = softplus(4.0 * denom) * 0.25 + 0.1
    mixed_ref[0] = (total[:size] / floor).astype(BF16)


def padded(state):
    return jnp.concatenate([state, jnp.zeros((AUG - ROWS, state.shape[1]), F32)], axis=0)


def softplus(x):
    return jnp.maximum(x, 0.0) + jnp.log1p(jnp.exp(-jnp.abs(x)))


def leave_kernel(grad_ref, total_ref, qf_ref, rows_ref, a_ref, back_ref):
    grad = grad_ref[0].astype(F32)
    size = grad.shape[0]
    numer = total_ref[0, :size]
    denom = total_ref[0, size : size + 1]
    inverse = 1.0 / (softplus(4.0 * denom) * 0.25 + 0.1)
    inner = jnp.sum(grad * numer, axis=0, keepdims=True)
    by_denom = -inner * jax.nn.sigmoid(4.0 * denom) * inverse * inverse
    whole = augmented(grad * inverse, by_denom)
    a_ref[0] = whole.astype(BF16)
    back = dot((whole * jnp.exp(rows_ref[0, 2:3, :])).astype(BF16), qf_ref[0], (1, 1))
    back_ref[0] = back[: back_ref.shape[1]]


def unit_back(raw, unit_grad):
    inverse = lax.rsqrt(jnp.sum(raw * raw, axis=0, keepdims=True) + 1e-06)
    inner = jnp.sum(raw * unit_grad, axis=0, keepdims=True)
    return inverse * (unit_grad - raw * (inner * inverse * inverse))


def angle_back(feat, grad):
    half = feat.shape[0] // 2
    feat = feat.astype(F32)
    return (grad[:half] * feat[half:] - grad[half:] * feat[:half]).astype(BF16)


def backward_kernel(
    tile, qkv_ref, fm_ref, rows_ref, qf_ref, kf_ref, a_ref, state_ref, back_ref, out_ref, logit_ref
):
    width = qkv_ref.shape[-1]
    size = qkv_ref.shape[2]
    fm = fm_ref[0]
    mask = lower_mask(tile)
    spots = list(range(0, width, tile))
    states = [padded(state_ref[0])]
    for at in spots:
        here = pl.ds(at, tile)
        last = rows_ref[0, 0:1, at + tile - 1 : at + tile]
        values = augmented(qkv_ref[0, 2, :, here], 1.0)
        tail = (values * jnp.exp(last + rows_ref[0, 1:2, here])).astype(BF16)
        states.append(jnp.exp(last) * states[-1] + dot(tail, kf_ref[0, :, here], (1, 1)))
    back = padded(back_ref[0])
    ones = jnp.ones((AUG, tile), BF16)

    def whole_sum(x):
        return jnp.sum(jnp.sum(x, axis=0, keepdims=True), axis=1, keepdims=True)

    pieces = []
    for index in reversed(range(len(spots))):
        at = spots[index]
        here = pl.ds(at, tile)
        running = rows_ref[0, 0:1, here]
        lead = rows_ref[0, 1:2, here]
        last = running[:, tile - 1 : tile]
        decay = jnp.exp(running)
        tail = jnp.exp(last + lead)
        qf = qf_ref[0, :, here]
        kf = kf_ref[0, :, here]
        a = a_ref[0, :, here]
        values = augmented(qkv_ref[0, 2, :, here], 1.0).astype(BF16)
        state = states[index].astype(BF16)
        low_back = back.astype(BF16)
        weights = jnp.where(mask, jnp.exp(outer_sum(lead, running)), 0.0)
        alike = dot(kf, qf, (0, 0))
        scores = (alike * weights).astype(BF16)
        pairs = dot(values, a, (0, 0)) * weights
        terms = (pairs * alike).astype(BF16)
        pairs = pairs.astype(BF16)
        from_state = decay * dot(state, a, (0, 0))
        from_back = tail * dot(low_back, values, (0, 0))
        query_feat = dot(kf, pairs, (1, 0)) + from_state
        key_feat = dot(qf, pairs, (1, 1)) + from_back
        by_query = dot(ones, terms, (1, 0))[:1]
        by_key = dot(ones, terms, (1, 1))[:1]
        state_term = jnp.sum(qf.astype(F32) * from_state, axis=0, keepdims=True)
        back_term = jnp.sum(kf.astype(F32) * from_back, axis=0, keepdims=True)
        through = jnp.exp(last) * whole_sum(back * states[index])
        constant = jnp.sum(back_term, axis=1, keepdims=True) + through
        pieces.append((by_query - by_key + state_term - back_term, by_key + back_term, constant))
        value = dot(a[:size], scores, (1, 1)) + tail * dot(low_back[:size], kf, (1, 0))
        query_unit = dot(fm, angle_back(qf, query_feat), (1, 0))
        key_unit = dot(fm, angle_back(kf, key_feat), (1, 0))
        out_ref[0, 0, :, here] = unit_back(qkv_ref[0, 0, :, here].astype(F32), query_unit).astype(BF16)
        out_ref[0, 1, :, here] = unit_back(qkv_ref[0, 1, :, here].astype(F32), key_unit).astype(BF16)
        out_ref[0, 2, :, here] = value.astype(BF16)
        back = jnp.exp(last) * back + dot((a.astype(F32) * decay).astype(BF16), qf, (1, 1))
    place = lax.broadcasted_iota(jnp.int32, (ROWS, tile), 0)
    sums = jnp.zeros((ROWS, tile), F32)
    for index, piece in enumerate(pieces[::-1]):
        sums = jnp.where(place == index, piece[0], sums)
    place = lax.broadcasted_iota(jnp.int32, (ROWS, tile), 1)
    step = 1
    while step < tile:
        sums = sums + jnp.where(place < tile - step, pltpu.roll(sums, tile - step, 1), 0.0)
        step *= 2
    for index, (_, by_key, constant) in enumerate(pieces[::-1]):
        here = pl.ds(spots[index], tile)
        keep_grad = sums[index : index + 1] + constant
        logit = keep_grad * rows_ref[0, 3:4, here] - by_key * rows_ref[0, 4:5, here]
        logit_ref[0, :, here] = jnp.broadcast_to(logit, (ROWS, tile))


def per_head(kernel, outs, heads, *arrays, us, far=()):
    group = 4

    def spec(shape, offset):
        rest = len(shape) - 1
        return pl.BlockSpec((group,) + tuple(shape[1:]), lambda h: (h + offset // group,) + (0,) * rest)

    def grouped(*refs):
        for i in range(group):
            kernel(*[ref.at[pl.ds(i, 1)] for ref in refs])

    nbytes = sum(heads * math.prod(a.shape[1:]) * a.dtype.itemsize for a, _ in arrays)
    nbytes += sum(math.prod(s) * jnp.dtype(d).itemsize for s, d in outs)
    return pl.pallas_call(
        grouped,
        grid=(heads // group,),
        in_specs=[spec(a.shape, offset) for a, offset in arrays],
        out_specs=[spec(s, 0) for s, _ in outs],
        out_shape=[jax.ShapeDtypeStruct(s, d) if i not in far else pltpu.HBM(s, d) for i, (s, d) in enumerate(outs)],
        compiler_params=pltpu.CompilerParams(vmem_limit_bytes=24 * 2**20),
        cost_estimate=pl.CostEstimate(flops=int(us * 1.1e9), bytes_accessed=int(nbytes), transcendentals=0),
    )(*[a for a, _ in arrays])


def norm_parts(x):
    average = jnp.mean(x, axis=0, keepdims=True)
    centered = x - average
    inverse = lax.rsqrt(jnp.mean(centered * centered, axis=0, keepdims=True) + 1e-05)
    return centered * inverse, inverse


def norm_back(hat, inverse, gain, grad):
    scaled = grad * gain
    first = jnp.mean(scaled, axis=0, keepdims=True)
    second = jnp.mean(scaled * hat, axis=0, keepdims=True)
    return (scaled - first - hat * second) * inverse


def product(spec, a, b):
    return jnp.einsum(spec, a, b, preferred_element_type=F32)


def local(
    tokens, w_qkv, w_gate, gate_bias, w_out, w_up, up_bias, w_down, down_bias, pre_gain, pre_shift,
    mid_gain, mid_shift, feature_map, state_init, keysum_init, out_cot, state_cot, keysum_cot,
):
    sizes = {axis: lax.axis_size(axis) for axis in ALL}
    count_hd, count_blk = sizes["hd"], sizes["blk"]
    devices = sizes["rows"] * count_blk * count_hd
    both = count_blk * count_hd
    seqs, part, width = tokens.shape
    own_heads, head_dim, rand = feature_map.shape
    heads = own_heads * count_hd
    feat = 2 * rand
    hidden_size = w_up.shape[1]
    length = seqs * part
    tile = 256 if length % 256 == 0 else 128
    shard = w_qkv.shape[0]
    aug, held_rows = head_dim + AUG, head_dim + ROWS
    place_hd, place_blk = lax.axis_index("hd"), lax.axis_index("blk")
    place = place_blk * count_hd + place_hd
    member, chunk = place % seqs, place // seqs
    chunks = both // seqs

    def to_chunk(x):
        return pieces_trip(x, BOTH, both, seqs, member)

    def from_chunk(x):
        return pieces_trip(x.reshape(seqs, part, width), BOTH, both, seqs, member)

    per_row = hidden_size // width
    n_small = heads + per_row + 5
    shares = devices // count_hd
    maps = feature_map.reshape(shares, shard, -1)
    spot = lax.axis_index("rows") * count_blk + place_blk
    maps = lax.dynamic_index_in_dim(maps, spot, 0, False)
    first_packed = pl.pallas_call(
        functools.partial(first_kernel, per_row),
        out_shape=jax.ShapeDtypeStruct((shard, 3 * width + 128 + maps.shape[1]), BF16),
    )(w_qkv, w_gate.T, up_bias, down_bias, pre_gain, pre_shift, mid_gain, mid_shift, gate_bias, maps)

    half = 3 * width // 2
    one, two = routes(sizes)
    stages = range(len(one))

    def gathers(streams, at):
        return [gather_trip(cur, route[at], sizes) for cur, route in zip(streams, (one, two))]

    whole = gather_trip(gather_start(first_packed, sizes), one[0], sizes).land()
    first = [whole[..., :half], whole[..., half:]]
    tokens_trip = to_chunk(after(tokens, *first))
    second = pl.pallas_call(
        rest_kernel, out_shape=jax.ShapeDtypeStruct((shard * (per_row + 1) + w_down.shape[0], width), BF16)
    )(*after((w_out, w_up, w_down), first_packed))
    second = lax.all_gather(second, ALL, axis=0)

    at_start = chunk == 0
    at_end = chunk == chunks - 1
    offers = []
    for other in range(count_hd):
        spot = place_blk * count_hd + other
        pick = lambda a: lax.dynamic_index_in_dim(a, spot % seqs, 0, False)
        state = jnp.where(spot // seqs == 0, pick(state_init), pick(state_cot))
        keysum = jnp.where(spot // seqs == 0, pick(keysum_init), pick(keysum_cot))
        keysum = jnp.pad(keysum[:, None], ((0, 0), (0, ROWS - 1), (0, 0)))
        offers.append(jnp.concatenate([jnp.swapaxes(state, -1, -2), keysum], axis=1))
    offers = after(jnp.stack(offers), *first)

    cut = len(one) - len([b for b in bits_of(sizes) if b[0] == "rows"]) + 1
    for at in stages[1:]:
        first = landed(gathers(first, at))
        if at == cut - 1:
            edge_trip = pieces_trip(after(offers, *first), "hd", count_hd, count_hd, place_hd)
    qkv_halves = [gather_end(f, sizes) for f in first]
    full_small = qkv_halves[1][:, half:]
    qkv_halves[1] = qkv_halves[1][:, :half]
    full_gate = full_small[:, :heads]
    full_up_bias = full_small[:, heads : heads + per_row].reshape(hidden_size, 1).astype(F32)
    vectors = [full_small[:, heads + per_row + i : heads + per_row + i + 1].astype(F32) for i in range(5)]
    full_down_bias, gain_1, shift_1, gain_2, shift_2 = vectors
    maps = full_small[:, -maps.shape[1] :].reshape(shares, count_hd, shard, -1)
    fm = maps.transpose(1, 0, 2, 3).reshape(heads, head_dim, rand)
    fmt = fm.transpose(0, 2, 1)

    def hop_trip(added, forward):
        pairs = [(i, i + seqs) for i in range(both - seqs)]
        pairs = pairs if forward else [(b, a) for a, b in pairs]
        outer = at_start if forward else at_end
        choose = lambda parts: jnp.where(outer, edge, parts[1].astype(F32))
        state = edge
        for last in range(chunks - 1):
            trip = Trip(None, [((added + decay * state).astype(BF16), BOTH, pairs)], choose)
            if last < chunks - 2:
                state = trip.land()
        return trip

    x = tokens_trip.land().reshape(length, width).T.astype(F32)
    hat_1, inverse_1 = norm_parts(x)
    normed = (hat_1 * gain_1 + shift_1).astype(BF16)
    rows = pl.pallas_call(
        functools.partial(gate_kernel, tile, heads, own_heads, shard, n_small),
        out_shape=jax.ShapeDtypeStruct((heads, ROWS, length), F32),
        compiler_params=pltpu.CompilerParams(vmem_limit_bytes=24 * 2**20),
    )(full_small, normed)
    packed = product("dc,dt->ct", jnp.concatenate(qkv_halves, axis=1), normed)
    packed = packed.astype(BF16).reshape(heads, 3, head_dim, length)
    decay = rows[:, 5:6, :1]

    cot_trip = to_chunk(after(out_cot, normed))
    qf, kf, partial_nu, chunk_state = per_head(
        functools.partial(forward_kernel, tile),
        [
            ((heads, feat, length), BF16),
            ((heads, feat, length), BF16),
            ((heads, held_rows, length), F32),
            ((heads, held_rows, feat), F32),
        ],
        heads, (departed(packed, cot_trip, edge_trip), 0), (fmt, 0), (rows, 0), us=18, far=(1,),
    )
    edge = edge_trip.land(chunk_state).reshape(heads, held_rows, feat)
    hop = hop_trip(chunk_state, True)
    cot = cot_trip.land(hop.messages()).reshape(length, width).T
    second = after(second, hop.messages())
    full_out = second[:, :shard].reshape(width, width)
    full_up = [second[:, i : i + shard].reshape(width, width) for i in range(shard, shard * (per_row + 1), shard)]
    full_up = jnp.concatenate(full_up, axis=1)
    full_down = second[:, shard * (per_row + 1) :].reshape(hidden_size, width)
    entering = hop.land(cot, full_out, full_up, full_down)
    mixed, total_nu = per_head(
        enter_kernel,
        [((heads, head_dim, length), BF16), ((heads, held_rows, length), F32)],
        heads, (entering, 0), (qf, 0), (rows, 0), (partial_nu, 0), us=3,
    )
    mixed = mixed.reshape(width, length)

    attended = x + product("io,it->ot", full_out, mixed)
    hat_2, inverse_2 = norm_parts(attended)
    hidden = (hat_2 * gain_2 + shift_2).astype(BF16)
    before = product("df,dt->ft", full_up, hidden) + full_up_bias
    cumulative = 0.5 + 0.5 * lax.erf(before * math.sqrt(0.5))
    density = jnp.exp(-0.5 * before * before) * (1.0 / math.sqrt(2.0 * math.pi))
    active = (before * cumulative).astype(BF16)
    before_grad = (product("fo,ot->ft", full_down, cot) * (cumulative + before * density)).astype(BF16)
    hidden_grad = product("df,ft->dt", full_up, before_grad)
    cot_full = cot.astype(F32)
    attended_grad = cot_full + norm_back(hat_2, inverse_2, gain_2, hidden_grad)
    attended_low = attended_grad.astype(BF16)
    mixed_grad = product("io,ot->it", full_out, attended_low).astype(BF16).reshape(heads, head_dim, length)

    a, chunk_back = per_head(
        leave_kernel,
        [((heads, aug, length), BF16), ((heads, held_rows, feat), F32)],
        heads, (mixed_grad, 0), (total_nu, 0), (qf, 0), (rows, 0), us=3,
    )
    hop = hop_trip(chunk_back, False)

    def scatters(streams, at):
        return [scatter_trip(cur, route[at], sizes) for cur, route in zip(streams, (one, two))]

    held = departed(hidden, hop)
    up_grad = product("dt,ft->df", held, before_grad).astype(BF16)
    down_grad = product("ft,ot->fo", active, cot).astype(BF16)
    early = [scatter_start(up_grad, sizes), scatter_start(down_grad, sizes)]
    early_trips = scatters(early, len(one) - 1)
    result = attended + product("fo,ft->ot", departed(full_down, *early_trips), active) + full_down_bias
    result = result.astype(BF16)
    out_grad = product("it,ot->io", mixed, attended_low).astype(BF16)
    early = landed(early_trips, result)
    for at in stages[-2 : cut - 1 : -1]:
        early = landed(scatters(early, at))
    output_trip = from_chunk(result.T)
    back = hop.land(result)
    down_bias_grad = jnp.sum(cot_full, axis=1)
    up_bias_grad = jnp.sum(before_grad.astype(F32), axis=1)
    gain_2_grad = jnp.sum(hidden_grad * hat_2, axis=1)
    shift_2_grad = jnp.sum(hidden_grad, axis=1)

    added = jnp.where(at_start, chunk_back, chunk_state)
    ends = (added + decay * jnp.where(at_start, back, entering)).astype(BF16)
    ends = lax.all_gather(ends, BOTH, axis=0)

    own = heads // 2

    def backward(i, part_qkv):
        grad, logit = per_head(
            functools.partial(backward_kernel, tile),
            [((own, 3, head_dim, length), BF16), ((own, ROWS, length), F32)],
            own, (part_qkv, i * own), (fm, i * own), (rows, i * own), (qf, i * own), (kf, i * own),
            (a, i * own), (entering, i * own), (back, i * own), us=9,
        )
        return grad.reshape(half, length), logit[:, 0]

    early_trips = scatters(early, cut - 1)
    grads = [backward(0, departed(packed, output_trip, *early_trips))]
    early = landed(early_trips, grads[0])
    output = output_trip.land(grads[0])
    for at in stages[cut - 2 : 1 : -1]:
        early = landed(scatters(early, at))
    early_trips = scatters(early, 1)
    qkv_grad = [product("dt,ct->dc", normed, grads[0][0]).astype(BF16)]
    late_one = scatter_start(jnp.concatenate([qkv_grad[0], out_grad], axis=1), sizes)
    late_trip = scatter_trip(late_one, one[-1], sizes)
    grads.append(backward(1, departed(packed, late_trip, *early_trips)))
    late_one = late_trip.land(grads[1])
    late_trip = scatter_trip(late_one, one[-2], sizes)

    gate_low = jnp.concatenate([g[1] for g in grads])
    bias_grad = jnp.sum(gate_low, axis=1)
    gate_low = gate_low.astype(BF16)
    last_grad = departed(grads[1][0], late_trip)
    normed_grad = (
        product("dc,ct->dt", qkv_halves[0], grads[0][0])
        + product("dc,ct->dt", qkv_halves[1], last_grad)
        + product("dh,ht->dt", full_gate, gate_low)
    )
    qkv_grad.append(product("dt,ct->dc", normed, last_grad).astype(BF16))
    gate_grad = product("dt,ht->dh", normed, gate_low)
    gain_1_grad = jnp.sum(normed_grad * hat_1, axis=1)
    shift_1_grad = jnp.sum(normed_grad, axis=1)
    grad_small = jnp.concatenate(
        [gate_grad, up_bias_grad.reshape(width, per_row)]
        + [v[:, None] for v in (down_bias_grad, gain_1_grad, shift_1_grad, gain_2_grad, shift_2_grad)]
        + [jnp.broadcast_to(bias_grad[None], (width, heads))],
        axis=1,
    )
    fine = grad_small.shape[1] + -grad_small.shape[1] % 128
    grad_small = in_two(jnp.pad(grad_small, ((0, 0), (0, fine - grad_small.shape[1])))).astype(BF16)
    late_two = scatter_start(jnp.concatenate([qkv_grad[1], grad_small], axis=1), sizes)
    other_trip = scatter_trip(late_two, two[-1], sizes, fine=fine)
    early_trips = scatters(landed(early_trips, other_trip.messages()), 0)
    held = departed(inverse_1, other_trip, *early_trips)
    token_grad = (attended_grad + norm_back(hat_1, held, gain_1, normed_grad)).astype(BF16)
    late_two = other_trip.land(token_grad)
    other_trip = scatter_trip(late_two, two[-2], sizes, fine=fine)
    late_one = late_trip.land(other_trip.messages())
    late_trip = scatter_trip(late_one, one[-3], sizes)
    early = landed(early_trips, late_trip.messages())
    up_own, down_own = (term_sum(scatter_end(e, sizes), 0) for e in early)
    token_grad = departed(token_grad, late_trip).T
    late_two = other_trip.land(up_own, down_own)
    for step in two[-3:1:-1]:
        late_two = scatter_trip(late_two, step, sizes, fine=fine).land()
    other_trip = scatter_trip(late_two, two[1], sizes, fine=fine)
    late_one = late_trip.land(other_trip.messages())
    for step in one[-4:0:-1]:
        late_one = scatter_trip(late_one, step, sizes).land()
    late_trip = scatter_trip(late_one, one[0], sizes)
    tokens_trip = from_chunk(departed(token_grad, late_trip))
    late_two = other_trip.land(tokens_trip.messages())
    other_trip = scatter_trip(late_two, two[0], sizes, fine=fine)
    ends = after(ends, tokens_trip.messages())
    index = lax.convert_element_type(place_hd, jnp.int32).reshape(1)
    shapes = [(seqs, own_heads, head_dim, feat), (seqs, own_heads, feat)]
    out_specs = [
        pl.BlockSpec((1,) + shapes[0][1:], lambda m, hd: (m, 0, 0, 0)), pl.BlockSpec((1,) + shapes[1][1:], lambda m, hd: (m, 0, 0))
    ]
    block = (1, own_heads, held_rows, feat)
    states = pl.pallas_call(
        ends_kernel,
        grid_spec=pltpu.PrefetchScalarGridSpec(
            num_scalar_prefetch=1,
            grid=(seqs,),
            in_specs=[
                pl.BlockSpec(block, lambda m, hd: (m, hd[0], 0, 0)),
                pl.BlockSpec(block, lambda m, hd: (m + both - seqs, hd[0], 0, 0)),
            ],
            out_specs=out_specs * 2,
        ),
        out_shape=[jax.ShapeDtypeStruct(shape, F32) for shape in shapes * 2],
        compiler_params=pltpu.CompilerParams(vmem_limit_bytes=24 * 2**20),
    )(index, ends, ends)
    state_start, keysum_start, state_final, keysum_final = states
    state_start, state_final = jnp.swapaxes(state_start, -1, -2), jnp.swapaxes(state_final, -1, -2)
    late_one, late_two = (scatter_end(e, sizes) for e in landed([late_trip, other_trip], *states))
    token_grad = tokens_trip.land(*states)
    shapes = [
        (shard, 3 * width), (shard, heads), (own_heads,), (shard, width), (shard * per_row,),
        *[(shard,)] * 5,
    ]
    in_vmem = [pl.BlockSpec(memory_space=pltpu.VMEM)]
    qkv_own, gate_own, bias_own, out_own, up_bias_own, down_bias_own, gain_1_own, shift_1_own, gain_2_own, shift_2_own = (
        pl.pallas_call(
            functools.partial(last_kernel, per_row, heads, len(late_one)),
            in_specs=[pl.BlockSpec(memory_space=pltpu.SMEM)] + in_vmem * (len(late_one) + len(late_two)),
            out_specs=in_vmem * len(shapes),
            out_shape=[jax.ShapeDtypeStruct(shape, F32) for shape in shapes],
        )(index, *late_one, *late_two)
    )
    return (
        output, token_grad, qkv_own, gate_own, bias_own, out_own, up_own, up_bias_own, down_own, down_bias_own,
        gain_1_own, shift_1_own, gain_2_own, shift_2_own, state_final, keysum_final, state_start, keysum_start,
    )


def solution(mesh):
    by_tokens = P("rows", ("blk", "hd"), None)
    by_rows = P(ALL, None)
    by_entry = P(ALL)
    by_head = P("hd")
    by_state = P("rows", "hd", None, None)
    by_keysum = P("rows", "hd", None)
    in_specs = (
        by_tokens, by_rows, by_rows, by_head, by_rows, by_rows, by_entry, by_rows, by_entry, by_entry, by_entry,
        by_entry, by_entry, P("hd", None, None), by_state, by_keysum, by_tokens, by_state, by_keysum,
    )
    out_specs = (
        by_tokens, by_tokens, by_rows, by_rows, by_head, by_rows, by_rows, by_entry, by_rows, by_entry,
        by_entry, by_entry, by_entry, by_entry, by_state, by_keysum, by_state, by_keysum,
    )
    return jax.shard_map(local, mesh=mesh, in_specs=in_specs, out_specs=out_specs, check_vma=False)
```

```python
import functools
import math

import jax
import jax.numpy as jnp
from jax import lax
from jax.experimental import pallas as pl
from jax.experimental.pallas import tpu as pltpu
from jax.sharding import PartitionSpec as P

ALL = ("rows", "blk", "hd")
BOTH = ("blk", "hd")
F32 = jnp.float32
BF16 = jnp.bfloat16
AUG = 16
ROWS = 8


def after(x, *others):
    return lax.optimization_barrier((x,) + others)[0]


class Trip:
    def __init__(self, own, sends, finish):
        self.own, self.sends, self.finish = own, sends, finish

    def messages(self):
        return [send[0] for send in self.sends]

    def land(self, *others):
        got = [lax.ppermute(*send) for send in self.sends]
        if others:
            got = after(got, *others)
        return self.finish([self.own] + got)


def departed(x, *trips):
    return after(x, [trip.messages() for trip in trips])


def landed(trips, *others):
    return [trip.land(*others) for trip in trips]


def turned(size, bit):
    return [(i, i ^ bit) for i in range(size)]


def ordered(parts, me):
    parts = list(parts)
    bit = 1
    while bit < len(parts):
        there = (me & bit) != 0
        parts = [jnp.where(there, parts[i ^ bit], parts[i]) for i in range(len(parts))]
        bit *= 2
    return parts


def pieces_trip(x, axis, size, group, me):
    sends = [(lax.dynamic_index_in_dim(x, me ^ k, 0, False), axis, turned(size, k)) for k in range(1, group)]
    own = lax.dynamic_index_in_dim(x, me, 0, False)
    return Trip(own, sends, lambda parts: jnp.stack(ordered(parts, me)))


def bits_of(sizes):
    found = []
    for axis in ALL:
        bit = sizes[axis] // 2
        while bit:
            found.append((axis, bit))
            bit //= 2
    return found


def routes(sizes):
    own = lambda axis: [[b] for b in bits_of(sizes) if b[0] == axis]
    z = [[b for b in bits_of(sizes) if b[0] == "blk"]]
    y, x = own("hd"), own("rows")
    return z + y + x[:1] + x[1:], z + x[:1] + y + x[1:]


def partners(step, sizes):
    axis, low = step[0][0], step[-1][1]
    count = 2 ** len(step)
    place = (lax.axis_index(axis) // low) % count
    return axis, sizes[axis], place, [k * low for k in range(count)]


def gather_start(x, sizes):
    return x.reshape((1,) * len(bits_of(sizes)) + x.shape)


def gather_trip(cur, step, sizes):
    axis, size, place, offsets = partners(step, sizes)
    dim = bits_of(sizes).index(step[0])
    shape = cur.shape[:dim] + (2,) * len(step) + cur.shape[dim + len(step) :]
    sends = [(cur, axis, turned(size, k)) for k in offsets[1:]]
    return Trip(cur, sends, lambda parts: jnp.concatenate(ordered(parts, place), axis=dim).reshape(shape))


def gather_end(cur, sizes):
    lead = len(bits_of(sizes))
    return cur.reshape((-1,) + cur.shape[lead + 1 :])


def scatter_start(x, sizes):
    bits = bits_of(sizes)
    return [x.reshape((2,) * len(bits) + (x.shape[0] // 2 ** len(bits),) + x.shape[1:])]


def in_two(x):
    high = lax.reduce_precision(x, 8, 7)
    return jnp.concatenate([high, x - high], axis=-1)


def term_sum(terms, fine):
    total = terms[0].astype(F32)
    for term in terms[1:]:
        total = total + term.astype(F32)
    if fine:
        total = [total[..., : -2 * fine], total[..., -2 * fine : -fine] + total[..., -fine:]]
    return total


def scatter_trip(terms, step, sizes, fine=0):
    axis, size, place, offsets = partners(step, sizes)
    dim = bits_of(sizes).index(step[0])
    shape = terms[0].shape
    lead, rest = shape[:dim], shape[dim + len(step) :]
    merged = [term.reshape(lead + (len(offsets),) + rest) for term in terms]

    def part(k):
        picked = [lax.dynamic_index_in_dim(term, place ^ k, dim, True) for term in merged]
        if len(picked) == 1:
            return picked[0]
        total = term_sum(picked, fine)
        return (jnp.concatenate([total[0], in_two(total[1])], axis=-1) if fine else total).astype(BF16)

    sends = [(part(k), axis, turned(size, offset)) for k, offset in enumerate(offsets) if k]
    here = lead + (1,) * len(step) + rest
    return Trip(part(0), sends, lambda parts: [p.reshape(here) for p in parts])


def scatter_end(terms, sizes):
    return [term.reshape(term.shape[len(bits_of(sizes)) :]) for term in terms]


def dot(a, b, contract):
    return lax.dot_general(a, b, ((contract[:1], contract[1:]), ((), ())), preferred_element_type=F32)


def sine_cosine(x, scale):
    turns = jnp.round(x * (1.0 / math.pi))
    rest = (x - turns * 3.140625) - turns * 9.67653589793e-4
    half = turns * 0.5
    sign = scale - (4.0 * scale) * (half - jnp.floor(half))
    sq = rest * rest
    sine = sq * 2.600052801290691e-06 - 0.0001980661418962755
    sine = sine * sq + 0.008333017275116794
    sine = sine * sq - 0.16666657095676896
    sine = rest + rest * (sq * sine)
    cosine = sq * 2.319437094031874e-05 - 0.001385592644003374
    cosine = cosine * sq + 0.04166398934467621
    cosine = cosine * sq - 0.4999993228818705
    cosine = cosine * sq + 1.0
    return sine * sign, cosine * sign


def split_rows(x):
    high = x.astype(BF16).astype(F32)
    rest = x - high
    middle = rest.astype(BF16).astype(F32)
    return high, middle, rest - middle


def outer_sum(column, row):
    width = row.shape[1]
    place = lax.broadcasted_iota(jnp.int32, (AUG, width), 0)

    def lay(parts, first):
        out = jnp.zeros((AUG, width), F32)
        for i, part in enumerate(parts):
            out = jnp.where(place == first + i, part, out)
        return jnp.where((place >= 3 - first) & (place < 6 - first), 1.0, out).astype(BF16)

    return dot(lay(split_rows(column), 0), lay(split_rows(row), 3), (0, 0))


def augmented(v, ones):
    width = v.shape[1]
    place = lax.broadcasted_iota(jnp.int32, (AUG, width), 0)
    extra = jnp.where(place == 0, ones, 0.0)
    return jnp.concatenate([v.astype(F32), extra], axis=0)


def lower_mask(c):
    return lax.broadcasted_iota(jnp.int32, (c, c), 0) <= lax.broadcasted_iota(jnp.int32, (c, c), 1)


def gate_kernel(tile, heads, own_heads, shard, first_bias, small_ref, normed_ref, out_ref):
    raw = dot(small_ref[:, :128], normed_ref[...], (0, 0))[:heads].astype(BF16).astype(F32)
    groups = heads // own_heads
    block = small_ref[: groups * shard, :128].astype(F32)
    head = lax.broadcasted_iota(jnp.int32, (heads, 128), 0)
    lane = lax.broadcasted_iota(jnp.int32, (heads, 128), 1)
    bias = jnp.zeros((heads, 1), F32)
    for group in range(groups):
        wanted = False
        for part in range(3):
            wanted = wanted | (lane == first_bias + part * own_heads + head - group * own_heads)
        wanted = wanted & (head >= group * own_heads) & (head < (group + 1) * own_heads)
        bias = bias + jnp.sum(jnp.where(wanted, block[group * shard : group * shard + 1], 0.0), axis=1, keepdims=True)
    logit = raw + bias
    heads, width = logit.shape
    small = jnp.log1p(jnp.exp(-jnp.abs(logit)))
    keep = jnp.minimum(logit, 0.0) - small
    slow = jnp.minimum(-logit, 0.0) - small
    place = lax.broadcasted_iota(jnp.int32, (heads, width), 1)

    def sums(x, within):
        at = lax.rem(place, within)
        step = 1
        while step < within:
            x = x + jnp.where(at >= step, pltpu.roll(x, step, 1), 0.0)
            step *= 2
        return x

    running = sums(keep, tile)
    whole = running
    offset = jnp.zeros((heads, 1), F32)
    for at in range(0, width, tile):
        whole = jnp.where((place >= at) & (place < at + tile), running + offset, whole)
        offset = offset + running[:, at + tile - 1 : at + tile]
    for kind, value in enumerate(
        (running, slow - running, whole, jnp.exp(slow), jnp.exp(keep), jnp.broadcast_to(jnp.exp(offset), (heads, width)))
    ):
        for head in range(heads):
            out_ref[head, kind : kind + 1, :] = value[head : head + 1]


def first_kernel(per_row, qkv_ref, gate_ref, up_ref, *refs):
    *vectors, bias_ref, maps_ref, out_ref = refs
    shard, wide = qkv_ref.shape
    heads = gate_ref.shape[0]
    lane = lax.broadcasted_iota(jnp.int32, (shard, 128), 1)

    def column(ref, stride, first):
        n = ref.shape[0]
        value = jnp.broadcast_to(ref[...].astype(F32)[None, :], (shard, n))
        row_at = lax.broadcasted_iota(jnp.int32, (shard, n), 0)
        line_at = lax.broadcasted_iota(jnp.int32, (shard, n), 1)
        return jnp.sum(jnp.where(line_at == row_at * stride + first, value, 0.0), axis=1, keepdims=True)

    small = jnp.zeros((shard, 128), F32)
    columns = [column(up_ref, per_row, i) for i in range(per_row)] + [column(ref, 1, 0) for ref in vectors]
    for i, value in enumerate(columns):
        small = jnp.where(lane == heads + i, value, small)
    at = heads + len(columns)
    bias = jnp.broadcast_to(bias_ref[...][None, :], (shard, bias_ref.shape[0]))
    for part in split_rows(bias):
        for i in range(bias_ref.shape[0]):
            small = jnp.where(lane == at, part[:, i : i + 1], small)
            at += 1
    for i in range(heads):
        small = jnp.where(lane == i, column(gate_ref.at[i], 1, 0), small)
    out_ref[:, :wide] = qkv_ref[...]
    out_ref[:, wide : wide + 128] = small.astype(BF16)
    out_ref[:, wide + 128 :] = maps_ref[...]


def rest_kernel(out_ref_w, up_ref, down_ref, out_ref):
    shard, width = out_ref_w.shape
    out_ref[:shard] = out_ref_w[...]
    blocks = up_ref.shape[1] // width
    for i in range(blocks):
        out_ref[shard * (i + 1) : shard * (i + 2)] = up_ref[:, i * width : (i + 1) * width]
    out_ref[shard * (blocks + 1) :] = down_ref[...]


def last_kernel(per_row, heads, n_one, hd_ref, *refs):
    ones, twos, outs = refs[:n_one], refs[n_one : -10], refs[-10:]
    qkv_ref, gate_ref, bias_ref, out_ref, up_ref = outs[:5]
    half = qkv_ref.shape[1] // 2
    shard = qkv_ref.shape[0]
    one = sum(ref[...].astype(F32) for ref in ones)
    two = sum(ref[...].astype(F32) for ref in twos)
    fine = (two.shape[1] - half) // 2
    small = two[:, half : half + fine] + two[:, half + fine :]
    qkv_ref[:, :half] = one[:, :half]
    qkv_ref[:, half:] = two[:, :half]
    out_ref[...] = one[:, half:]
    row_at = lax.broadcasted_iota(jnp.int32, (shard, fine), 0)
    lane_at = lax.broadcasted_iota(jnp.int32, (shard, fine), 1)

    def line(n, stride, columns):
        row_at = lax.broadcasted_iota(jnp.int32, (shard, n), 0)
        line_at = lax.broadcasted_iota(jnp.int32, (shard, n), 1)
        value = jnp.zeros((shard, n), F32)
        for j, column in enumerate(columns):
            value = jnp.where(line_at == row_at * stride + j, column, value)
        return jnp.sum(value, axis=0)

    up_ref[...] = line(shard * per_row, per_row, [small[:, heads + j : heads + j + 1] for j in range(per_row)])
    for i, ref in enumerate(outs[5:]):
        at = heads + per_row + i
        ref[...] = line(shard, 1, [small[:, at : at + 1]])
    for i in range(heads):
        gate_ref[i] = line(shard, 1, [small[:, i : i + 1]])
    own = bias_ref.shape[0]
    first = heads + per_row + 5 + hd_ref[0] * own
    column = jnp.sum(jnp.where(lane_at == first + row_at, small, 0.0), axis=1, keepdims=True)
    bias_ref[...] = line(own, 1, [column])


def ends_kernel(hd_ref, start_ref, final_ref, *outs):
    size = outs[0].shape[2]
    for ref, state_ref, key_ref in ((start_ref, *outs[:2]), (final_ref, *outs[2:])):
        for head in range(ref.shape[1]):
            rows = ref[0, head].astype(F32)
            state_ref[0, head] = rows[:size]
            key_ref[0, head : head + 1] = rows[size : size + 1]


def features(unit, fmt, scale):
    sine, cosine = sine_cosine(dot(fmt, unit, (1, 0)), scale)
    return jnp.concatenate([sine, cosine], axis=0).astype(BF16)


def forward_kernel(tile, qkv_ref, fmt_ref, rows_ref, qf_ref, kf_ref, nu_ref, state_ref):
    width = qkv_ref.shape[-1]
    fmt = fmt_ref[0]
    scale = 1.0 / math.sqrt(fmt.shape[0])
    mask = lower_mask(tile)
    state = None
    for at in range(0, width, tile):
        here = pl.ds(at, tile)
        query = qkv_ref[0, 0, :, here].astype(F32)
        key = qkv_ref[0, 1, :, here].astype(F32)
        query = (query * lax.rsqrt(jnp.sum(query * query, axis=0, keepdims=True) + 1e-06)).astype(BF16)
        key = (key * lax.rsqrt(jnp.sum(key * key, axis=0, keepdims=True) + 1e-06)).astype(BF16)
        qf = features(query, fmt, scale)
        kf = features(key, fmt, scale)
        qf_ref[0, :, here] = qf
        kf_ref[0, :, here] = kf
        running = rows_ref[0, 0:1, here]
        lead = rows_ref[0, 1:2, here]
        last = running[:, tile - 1 : tile]
        values = augmented(qkv_ref[0, 2, :, here], 1.0)
        weights = jnp.where(mask, jnp.exp(outer_sum(lead, running)), 0.0)
        scores = (dot(kf, qf, (0, 0)) * weights).astype(BF16)
        numer = dot(values.astype(BF16), scores, (1, 0))
        if state is not None:
            numer = numer + jnp.exp(running) * dot(state.astype(BF16), qf, (1, 0))
        nu_ref[0, :, here] = numer[: nu_ref.shape[1]]
        tail = (values * jnp.exp(last + lead)).astype(BF16)
        new = dot(tail, kf, (1, 1))
        state = new if state is None else jnp.exp(last) * state + new
    state_ref[0] = state[: state_ref.shape[1]]


def enter_kernel(state_ref, qf_ref, rows_ref, nu_ref, mixed_ref, total_ref):
    state = padded(state_ref[0])
    high = state.astype(BF16)
    rest = (state - high.astype(F32)).astype(BF16)
    qf = qf_ref[0]
    rows = nu_ref.shape[1]
    extra = (dot(high, qf, (1, 0)) + dot(rest, qf, (1, 0)))[:rows]
    total = nu_ref[0] + jnp.exp(rows_ref[0, 2:3, :]) * extra
    total_ref[0] = total
    size = mixed_ref.shape[1]
    denom = total[size : size + 1]
    floor = softplus(4.0 * denom) * 0.25 + 0.1
    mixed_ref[0] = (total[:size] / floor).astype(BF16)


def padded(state):
    return jnp.concatenate([state, jnp.zeros((AUG - ROWS, state.shape[1]), F32)], axis=0)


def softplus(x):
    return jnp.maximum(x, 0.0) + jnp.log1p(jnp.exp(-jnp.abs(x)))


def leave_kernel(grad_ref, total_ref, qf_ref, rows_ref, a_ref, back_ref):
    grad = grad_ref[0].astype(F32)
    size = grad.shape[0]
    numer = total_ref[0, :size]
    denom = total_ref[0, size : size + 1]
    inverse = 1.0 / (softplus(4.0 * denom) * 0.25 + 0.1)
    inner = jnp.sum(grad * numer, axis=0, keepdims=True)
    by_denom = -inner * jax.nn.sigmoid(4.0 * denom) * inverse * inverse
    whole = augmented(grad * inverse, by_denom)
    a_ref[0] = whole.astype(BF16)
    back = dot((whole * jnp.exp(rows_ref[0, 2:3, :])).astype(BF16), qf_ref[0], (1, 1))
    back_ref[0] = back[: back_ref.shape[1]]


def unit_back(raw, unit_grad):
    inverse = lax.rsqrt(jnp.sum(raw * raw, axis=0, keepdims=True) + 1e-06)
    inner = jnp.sum(raw * unit_grad, axis=0, keepdims=True)
    return inverse * (unit_grad - raw * (inner * inverse * inverse))


def angle_back(feat, grad):
    half = feat.shape[0] // 2
    feat = feat.astype(F32)
    return (grad[:half] * feat[half:] - grad[half:] * feat[:half]).astype(BF16)


def backward_kernel(
    tile, qkv_ref, fm_ref, rows_ref, qf_ref, kf_ref, a_ref, state_ref, back_ref, out_ref, logit_ref
):
    width = qkv_ref.shape[-1]
    size = qkv_ref.shape[2]
    fm = fm_ref[0]
    mask = lower_mask(tile)
    spots = list(range(0, width, tile))
    states = [padded(state_ref[0])]
    for at in spots:
        here = pl.ds(at, tile)
        last = rows_ref[0, 0:1, at + tile - 1 : at + tile]
        values = augmented(qkv_ref[0, 2, :, here], 1.0)
        tail = (values * jnp.exp(last + rows_ref[0, 1:2, here])).astype(BF16)
        states.append(jnp.exp(last) * states[-1] + dot(tail, kf_ref[0, :, here], (1, 1)))
    back = padded(back_ref[0])
    ones = jnp.ones((AUG, tile), BF16)

    def whole_sum(x):
        return jnp.sum(jnp.sum(x, axis=0, keepdims=True), axis=1, keepdims=True)

    pieces = []
    for index in reversed(range(len(spots))):
        at = spots[index]
        here = pl.ds(at, tile)
        running = rows_ref[0, 0:1, here]
        lead = rows_ref[0, 1:2, here]
        last = running[:, tile - 1 : tile]
        decay = jnp.exp(running)
        tail = jnp.exp(last + lead)
        qf = qf_ref[0, :, here]
        kf = kf_ref[0, :, here]
        a = a_ref[0, :, here]
        values = augmented(qkv_ref[0, 2, :, here], 1.0).astype(BF16)
        state = states[index].astype(BF16)
        low_back = back.astype(BF16)
        weights = jnp.where(mask, jnp.exp(outer_sum(lead, running)), 0.0)
        alike = dot(kf, qf, (0, 0))
        scores = (alike * weights).astype(BF16)
        pairs = dot(values, a, (0, 0)) * weights
        terms = (pairs * alike).astype(BF16)
        pairs = pairs.astype(BF16)
        from_state = decay * dot(state, a, (0, 0))
        from_back = tail * dot(low_back, values, (0, 0))
        query_feat = dot(kf, pairs, (1, 0)) + from_state
        key_feat = dot(qf, pairs, (1, 1)) + from_back
        by_query = dot(ones, terms, (1, 0))[:1]
        by_key = dot(ones, terms, (1, 1))[:1]
        state_term = jnp.sum(qf.astype(F32) * from_state, axis=0, keepdims=True)
        back_term = jnp.sum(kf.astype(F32) * from_back, axis=0, keepdims=True)
        through = jnp.exp(last) * whole_sum(back * states[index])
        constant = jnp.sum(back_term, axis=1, keepdims=True) + through
        pieces.append((by_query - by_key + state_term - back_term, by_key + back_term, constant))
        value = dot(a[:size], scores, (1, 1)) + tail * dot(low_back[:size], kf, (1, 0))
        query_unit = dot(fm, angle_back(qf, query_feat), (1, 0))
        key_unit = dot(fm, angle_back(kf, key_feat), (1, 0))
        out_ref[0, 0, :, here] = unit_back(qkv_ref[0, 0, :, here].astype(F32), query_unit).astype(BF16)
        out_ref[0, 1, :, here] = unit_back(qkv_ref[0, 1, :, here].astype(F32), key_unit).astype(BF16)
        out_ref[0, 2, :, here] = value.astype(BF16)
        back = jnp.exp(last) * back + dot((a.astype(F32) * decay).astype(BF16), qf, (1, 1))
    place = lax.broadcasted_iota(jnp.int32, (ROWS, tile), 0)
    sums = jnp.zeros((ROWS, tile), F32)
    for index, piece in enumerate(pieces[::-1]):
        sums = jnp.where(place == index, piece[0], sums)
    place = lax.broadcasted_iota(jnp.int32, (ROWS, tile), 1)
    step = 1
    while step < tile:
        sums = sums + jnp.where(place < tile - step, pltpu.roll(sums, tile - step, 1), 0.0)
        step *= 2
    for index, (_, by_key, constant) in enumerate(pieces[::-1]):
        here = pl.ds(spots[index], tile)
        keep_grad = sums[index : index + 1] + constant
        logit = keep_grad * rows_ref[0, 3:4, here] - by_key * rows_ref[0, 4:5, here]
        logit_ref[0, :, here] = jnp.broadcast_to(logit, (ROWS, tile))


def per_head(kernel, outs, heads, *arrays, us, far=()):
    group = 4

    def spec(shape, offset):
        rest = len(shape) - 1
        return pl.BlockSpec((group,) + tuple(shape[1:]), lambda h: (h + offset // group,) + (0,) * rest)

    def grouped(*refs):
        for i in range(group):
            kernel(*[ref.at[pl.ds(i, 1)] for ref in refs])

    nbytes = sum(heads * math.prod(a.shape[1:]) * a.dtype.itemsize for a, _ in arrays)
    nbytes += sum(math.prod(s) * jnp.dtype(d).itemsize for s, d in outs)
    return pl.pallas_call(
        grouped,
        grid=(heads // group,),
        in_specs=[spec(a.shape, offset) for a, offset in arrays],
        out_specs=[spec(s, 0) for s, _ in outs],
        out_shape=[jax.ShapeDtypeStruct(s, d) if i not in far else pltpu.HBM(s, d) for i, (s, d) in enumerate(outs)],
        compiler_params=pltpu.CompilerParams(vmem_limit_bytes=24 * 2**20),
        cost_estimate=pl.CostEstimate(flops=int(us * 1.1e9), bytes_accessed=int(nbytes), transcendentals=0),
    )(*[a for a, _ in arrays])


def norm_parts(x):
    average = jnp.mean(x, axis=0, keepdims=True)
    centered = x - average
    inverse = lax.rsqrt(jnp.mean(centered * centered, axis=0, keepdims=True) + 1e-05)
    return centered * inverse, inverse


def norm_back(hat, inverse, gain, grad):
    scaled = grad * gain
    first = jnp.mean(scaled, axis=0, keepdims=True)
    second = jnp.mean(scaled * hat, axis=0, keepdims=True)
    return (scaled - first - hat * second) * inverse


def product(spec, a, b):
    return jnp.einsum(spec, a, b, preferred_element_type=F32)


def local(
    tokens, w_qkv, w_gate, gate_bias, w_out, w_up, up_bias, w_down, down_bias, pre_gain, pre_shift,
    mid_gain, mid_shift, feature_map, state_init, keysum_init, out_cot, state_cot, keysum_cot,
):
    sizes = {axis: lax.axis_size(axis) for axis in ALL}
    count_hd, count_blk = sizes["hd"], sizes["blk"]
    devices = sizes["rows"] * count_blk * count_hd
    both = count_blk * count_hd
    seqs, part, width = tokens.shape
    own_heads, head_dim, rand = feature_map.shape
    heads = own_heads * count_hd
    feat = 2 * rand
    hidden_size = w_up.shape[1]
    length = seqs * part
    tile = 256 if length % 256 == 0 else 128
    shard = w_qkv.shape[0]
    aug, held_rows = head_dim + AUG, head_dim + ROWS
    place_hd, place_blk = lax.axis_index("hd"), lax.axis_index("blk")
    place = place_blk * count_hd + place_hd
    member, chunk = place % seqs, place // seqs
    chunks = both // seqs

    def to_chunk(x):
        return pieces_trip(x, BOTH, both, seqs, member)

    def from_chunk(x):
        return pieces_trip(x.reshape(seqs, part, width), BOTH, both, seqs, member)

    per_row = hidden_size // width
    n_small = heads + per_row + 5
    shares = devices // count_hd
    maps = feature_map.reshape(shares, shard, -1)
    spot = lax.axis_index("rows") * count_blk + place_blk
    maps = lax.dynamic_index_in_dim(maps, spot, 0, False)
    first_packed = pl.pallas_call(
        functools.partial(first_kernel, per_row),
        out_shape=jax.ShapeDtypeStruct((shard, 3 * width + 128 + maps.shape[1]), BF16),
    )(w_qkv, w_gate.T, up_bias, down_bias, pre_gain, pre_shift, mid_gain, mid_shift, gate_bias, maps)

    half = 3 * width // 2
    one, two = routes(sizes)
    stages = range(len(one))

    def gathers(streams, at):
        return [gather_trip(cur, route[at], sizes) for cur, route in zip(streams, (one, two))]

    whole = gather_trip(gather_start(first_packed, sizes), one[0], sizes).land()
    first = [whole[..., :half], whole[..., half:]]
    tokens_trip = to_chunk(after(tokens, *first))
    second = pl.pallas_call(
        rest_kernel, out_shape=jax.ShapeDtypeStruct((shard * (per_row + 1) + w_down.shape[0], width), BF16)
    )(*after((w_out, w_up, w_down), first_packed))
    second = lax.all_gather(second, ALL, axis=0)

    at_start = chunk == 0
    at_end = chunk == chunks - 1
    offers = []
    for other in range(count_hd):
        spot = place_blk * count_hd + other
        pick = lambda a: lax.dynamic_index_in_dim(a, spot % seqs, 0, False)
        state = jnp.where(spot // seqs == 0, pick(state_init), pick(state_cot))
        keysum = jnp.where(spot // seqs == 0, pick(keysum_init), pick(keysum_cot))
        keysum = jnp.pad(keysum[:, None], ((0, 0), (0, ROWS - 1), (0, 0)))
        offers.append(jnp.concatenate([jnp.swapaxes(state, -1, -2), keysum], axis=1))
    offers = after(jnp.stack(offers), *first)

    cut = len(one) - len([b for b in bits_of(sizes) if b[0] == "rows"]) + 1
    for at in stages[1:]:
        first = landed(gathers(first, at))
        if at == cut - 1:
            edge_trip = pieces_trip(after(offers, *first), "hd", count_hd, count_hd, place_hd)
    qkv_halves = [gather_end(f, sizes) for f in first]
    full_small = qkv_halves[1][:, half:]
    qkv_halves[1] = qkv_halves[1][:, :half]
    full_gate = full_small[:, :heads]
    full_up_bias = full_small[:, heads : heads + per_row].reshape(hidden_size, 1).astype(F32)
    vectors = [full_small[:, heads + per_row + i : heads + per_row + i + 1].astype(F32) for i in range(5)]
    full_down_bias, gain_1, shift_1, gain_2, shift_2 = vectors
    maps = full_small[:, -maps.shape[1] :].reshape(shares, count_hd, shard, -1)
    fm = maps.transpose(1, 0, 2, 3).reshape(heads, head_dim, rand)
    fmt = fm.transpose(0, 2, 1)

    def hop_trip(added, forward):
        pairs = [(i, i + seqs) for i in range(both - seqs)]
        pairs = pairs if forward else [(b, a) for a, b in pairs]
        outer = at_start if forward else at_end
        choose = lambda parts: jnp.where(outer, edge, parts[1].astype(F32))
        state = edge
        for last in range(chunks - 1):
            trip = Trip(None, [((added + decay * state).astype(BF16), BOTH, pairs)], choose)
            if last < chunks - 2:
                state = trip.land()
        return trip

    x = tokens_trip.land().reshape(length, width).T.astype(F32)
    hat_1, inverse_1 = norm_parts(x)
    normed = (hat_1 * gain_1 + shift_1).astype(BF16)
    rows = pl.pallas_call(
        functools.partial(gate_kernel, tile, heads, own_heads, shard, n_small),
        out_shape=jax.ShapeDtypeStruct((heads, ROWS, length), F32),
        compiler_params=pltpu.CompilerParams(vmem_limit_bytes=24 * 2**20),
    )(full_small, normed)
    packed = product("dc,dt->ct", jnp.concatenate(qkv_halves, axis=1), normed)
    packed = packed.astype(BF16).reshape(heads, 3, head_dim, length)
    decay = rows[:, 5:6, :1]

    cot_trip = to_chunk(after(out_cot, normed))
    qf, kf, partial_nu, chunk_state = per_head(
        functools.partial(forward_kernel, tile),
        [
            ((heads, feat, length), BF16),
            ((heads, feat, length), BF16),
            ((heads, held_rows, length), F32),
            ((heads, held_rows, feat), F32),
        ],
        heads, (packed, 0), (departed(fmt, cot_trip, edge_trip), 0), (rows, 0), us=18, far=(0, 1),
    )
    edge = edge_trip.land(chunk_state).reshape(heads, held_rows, feat)
    hop = hop_trip(chunk_state, True)
    cot = cot_trip.land(hop.messages()).reshape(length, width).T
    second = after(second, hop.messages())
    full_out = second[:, :shard].reshape(width, width)
    full_up = [second[:, i : i + shard].reshape(width, width) for i in range(shard, shard * (per_row + 1), shard)]
    full_up = jnp.concatenate(full_up, axis=1)
    full_down = second[:, shard * (per_row + 1) :].reshape(hidden_size, width)
    entering = hop.land(cot, full_out, full_up, full_down)
    mixed, total_nu = per_head(
        enter_kernel,
        [((heads, head_dim, length), BF16), ((heads, held_rows, length), F32)],
        heads, (entering, 0), (qf, 0), (rows, 0), (partial_nu, 0), us=3,
    )
    mixed = mixed.reshape(width, length)

    attended = x + product("io,it->ot", full_out, mixed)
    hat_2, inverse_2 = norm_parts(attended)
    hidden = (hat_2 * gain_2 + shift_2).astype(BF16)
    before = product("df,dt->ft", full_up, hidden) + full_up_bias
    cumulative = 0.5 + 0.5 * lax.erf(before * math.sqrt(0.5))
    density = jnp.exp(-0.5 * before * before) * (1.0 / math.sqrt(2.0 * math.pi))
    active = (before * cumulative).astype(BF16)
    before_grad = (product("fo,ot->ft", full_down, cot) * (cumulative + before * density)).astype(BF16)
    hidden_grad = product("df,ft->dt", full_up, before_grad)
    cot_full = cot.astype(F32)
    attended_grad = cot_full + norm_back(hat_2, inverse_2, gain_2, hidden_grad)
    attended_low = attended_grad.astype(BF16)
    mixed_grad = product("io,ot->it", full_out, attended_low).astype(BF16).reshape(heads, head_dim, length)

    a, chunk_back = per_head(
        leave_kernel,
        [((heads, aug, length), BF16), ((heads, held_rows, feat), F32)],
        heads, (mixed_grad, 0), (total_nu, 0), (qf, 0), (rows, 0), us=3,
    )
    hop = hop_trip(chunk_back, False)

    def scatters(streams, at):
        return [scatter_trip(cur, route[at], sizes) for cur, route in zip(streams, (one, two))]

    held = departed(hidden, hop)
    up_grad = product("dt,ft->df", held, before_grad).astype(BF16)
    down_grad = product("ft,ot->fo", active, cot).astype(BF16)
    early = [scatter_start(up_grad, sizes), scatter_start(down_grad, sizes)]
    early_trips = scatters(early, len(one) - 1)
    result = attended + product("fo,ft->ot", departed(full_down, *early_trips), active) + full_down_bias
    result = result.astype(BF16)
    out_grad = product("it,ot->io", mixed, attended_low).astype(BF16)
    early = landed(early_trips, result)
    for at in stages[-2 : cut - 1 : -1]:
        early = landed(scatters(early, at))
    output_trip = from_chunk(result.T)
    back = hop.land(result)
    down_bias_grad = jnp.sum(cot_full, axis=1)
    up_bias_grad = jnp.sum(before_grad.astype(F32), axis=1)
    gain_2_grad = jnp.sum(hidden_grad * hat_2, axis=1)
    shift_2_grad = jnp.sum(hidden_grad, axis=1)

    added = jnp.where(at_start, chunk_back, chunk_state)
    ends = (added + decay * jnp.where(at_start, back, entering)).astype(BF16)
    ends = lax.all_gather(ends, BOTH, axis=0)

    own = heads // 2

    def backward(i, fm):
        grad, logit = per_head(
            functools.partial(backward_kernel, tile),
            [((own, 3, head_dim, length), BF16), ((own, ROWS, length), F32)],
            own, (packed, i * own), (fm, i * own), (rows, i * own), (qf, i * own), (kf, i * own),
            (a, i * own), (entering, i * own), (back, i * own), us=9,
        )
        return grad.reshape(half, length), logit[:, 0]

    early_trips = scatters(early, cut - 1)
    grads = [backward(0, departed(fm, output_trip, *early_trips))]
    early = landed(early_trips, grads[0])
    output = output_trip.land(grads[0])
    for at in stages[cut - 2 : 1 : -1]:
        early = landed(scatters(early, at))
    early_trips = scatters(early, 1)
    qkv_grad = [product("dt,ct->dc", normed, grads[0][0]).astype(BF16)]
    late_one = scatter_start(jnp.concatenate([qkv_grad[0], out_grad], axis=1), sizes)
    late_trip = scatter_trip(late_one, one[-1], sizes)
    grads.append(backward(1, departed(fm, late_trip, *early_trips)))
    late_one = late_trip.land(grads[1])
    late_trip = scatter_trip(late_one, one[-2], sizes)

    gate_low = jnp.concatenate([g[1] for g in grads])
    bias_grad = jnp.sum(gate_low, axis=1)
    gate_low = gate_low.astype(BF16)
    last_grad = departed(grads[1][0], late_trip)
    normed_grad = (
        product("dc,ct->dt", qkv_halves[0], grads[0][0])
        + product("dc,ct->dt", qkv_halves[1], last_grad)
        + product("dh,ht->dt", full_gate, gate_low)
    )
    qkv_grad.append(product("dt,ct->dc", normed, last_grad).astype(BF16))
    gate_grad = product("dt,ht->dh", normed, gate_low)
    gain_1_grad = jnp.sum(normed_grad * hat_1, axis=1)
    shift_1_grad = jnp.sum(normed_grad, axis=1)
    grad_small = jnp.concatenate(
        [gate_grad, up_bias_grad.reshape(width, per_row)]
        + [v[:, None] for v in (down_bias_grad, gain_1_grad, shift_1_grad, gain_2_grad, shift_2_grad)]
        + [jnp.broadcast_to(bias_grad[None], (width, heads))],
        axis=1,
    )
    fine = grad_small.shape[1] + -grad_small.shape[1] % 128
    grad_small = in_two(jnp.pad(grad_small, ((0, 0), (0, fine - grad_small.shape[1])))).astype(BF16)
    late_two = scatter_start(jnp.concatenate([qkv_grad[1], grad_small], axis=1), sizes)
    other_trip = scatter_trip(late_two, two[-1], sizes, fine=fine)
    early_trips = scatters(landed(early_trips, other_trip.messages()), 0)
    held = departed(inverse_1, other_trip, *early_trips)
    token_grad = (attended_grad + norm_back(hat_1, held, gain_1, normed_grad)).astype(BF16)
    late_two = other_trip.land(token_grad)
    other_trip = scatter_trip(late_two, two[-2], sizes, fine=fine)
    late_one = late_trip.land(other_trip.messages())
    late_trip = scatter_trip(late_one, one[-3], sizes)
    early = landed(early_trips, late_trip.messages())
    up_own, down_own = (term_sum(scatter_end(e, sizes), 0) for e in early)
    token_grad = departed(token_grad, late_trip).T
    late_two = other_trip.land(up_own, down_own)
    for step in two[-3:1:-1]:
        late_two = scatter_trip(late_two, step, sizes, fine=fine).land()
    other_trip = scatter_trip(late_two, two[1], sizes, fine=fine)
    late_one = late_trip.land(other_trip.messages())
    for step in one[-4:0:-1]:
        late_one = scatter_trip(late_one, step, sizes).land()
    late_trip = scatter_trip(late_one, one[0], sizes)
    tokens_trip = from_chunk(departed(token_grad, late_trip))
    late_two = other_trip.land(tokens_trip.messages())
    other_trip = scatter_trip(late_two, two[0], sizes, fine=fine)
    ends = after(ends, tokens_trip.messages())
    index = lax.convert_element_type(place_hd, jnp.int32).reshape(1)
    shapes = [(seqs, own_heads, head_dim, feat), (seqs, own_heads, feat)]
    out_specs = [
        pl.BlockSpec((1,) + shapes[0][1:], lambda m, hd: (m, 0, 0, 0)), pl.BlockSpec((1,) + shapes[1][1:], lambda m, hd: (m, 0, 0))
    ]
    block = (1, own_heads, held_rows, feat)
    states = pl.pallas_call(
        ends_kernel,
        grid_spec=pltpu.PrefetchScalarGridSpec(
            num_scalar_prefetch=1,
            grid=(seqs,),
            in_specs=[
                pl.BlockSpec(block, lambda m, hd: (m, hd[0], 0, 0)),
                pl.BlockSpec(block, lambda m, hd: (m + both - seqs, hd[0], 0, 0)),
            ],
            out_specs=out_specs * 2,
        ),
        out_shape=[jax.ShapeDtypeStruct(shape, F32) for shape in shapes * 2],
        compiler_params=pltpu.CompilerParams(vmem_limit_bytes=24 * 2**20),
    )(index, ends, ends)
    state_start, keysum_start, state_final, keysum_final = states
    state_start, state_final = jnp.swapaxes(state_start, -1, -2), jnp.swapaxes(state_final, -1, -2)
    late_one, late_two = (scatter_end(e, sizes) for e in landed([late_trip, other_trip], *states))
    token_grad = tokens_trip.land(*states)
    shapes = [
        (shard, 3 * width), (heads, shard), (own_heads,), (shard, width), (shard * per_row,),
        *[(shard,)] * 5,
    ]
    in_vmem = [pl.BlockSpec(memory_space=pltpu.VMEM)]
    qkv_own, gate_own, bias_own, out_own, up_bias_own, down_bias_own, gain_1_own, shift_1_own, gain_2_own, shift_2_own = (
        pl.pallas_call(
            functools.partial(last_kernel, per_row, heads, len(late_one)),
            in_specs=[pl.BlockSpec(memory_space=pltpu.SMEM)] + in_vmem * (len(late_one) + len(late_two)),
            out_specs=in_vmem * len(shapes),
            out_shape=[jax.ShapeDtypeStruct(shape, F32) for shape in shapes],
        )(index, *late_one, *late_two)
    )
    return (
        output, token_grad, qkv_own, gate_own.T, bias_own, out_own, up_own, up_bias_own, down_own, down_bias_own,
        gain_1_own, shift_1_own, gain_2_own, shift_2_own, state_final, keysum_final, state_start, keysum_start,
    )


def solution(mesh):
    by_tokens = P("rows", ("blk", "hd"), None)
    by_rows = P(ALL, None)
    by_entry = P(ALL)
    by_head = P("hd")
    by_state = P("rows", "hd", None, None)
    by_keysum = P("rows", "hd", None)
    in_specs = (
        by_tokens, by_rows, by_rows, by_head, by_rows, by_rows, by_entry, by_rows, by_entry, by_entry, by_entry,
        by_entry, by_entry, P("hd", None, None), by_state, by_keysum, by_tokens, by_state, by_keysum,
    )
    out_specs = (
        by_tokens, by_tokens, by_rows, by_rows, by_head, by_rows, by_rows, by_entry, by_rows, by_entry,
        by_entry, by_entry, by_entry, by_entry, by_state, by_keysum, by_state, by_keysum,
    )
    return jax.shard_map(local, mesh=mesh, in_specs=in_specs, out_specs=out_specs, check_vma=False)
```

```python
import functools
import math

import jax
import jax.numpy as jnp
from jax import lax
from jax.experimental import pallas as pl
from jax.experimental.pallas import tpu as pltpu
from jax.sharding import PartitionSpec as P

ALL = ("rows", "blk", "hd")
BOTH = ("blk", "hd")
F32 = jnp.float32
BF16 = jnp.bfloat16
AUG = 16
ROWS = 8


def after(x, *others):
    return lax.optimization_barrier((x,) + others)[0]


class Trip:
    def __init__(self, own, sends, finish):
        self.own, self.sends, self.finish = own, sends, finish

    def messages(self):
        return [send[0] for send in self.sends]

    def land(self, *others):
        got = [lax.ppermute(*send) for send in self.sends]
        if others:
            got = after(got, *others)
        return self.finish([self.own] + got)


def departed(x, *trips):
    return after(x, [trip.messages() for trip in trips])


def landed(trips, *others):
    return [trip.land(*others) for trip in trips]


def turned(size, bit):
    return [(i, i ^ bit) for i in range(size)]


def ordered(parts, me):
    parts = list(parts)
    bit = 1
    while bit < len(parts):
        there = (me & bit) != 0
        parts = [jnp.where(there, parts[i ^ bit], parts[i]) for i in range(len(parts))]
        bit *= 2
    return parts


def pieces_trip(x, axis, size, group, me):
    sends = [(lax.dynamic_index_in_dim(x, me ^ k, 0, False), axis, turned(size, k)) for k in range(1, group)]
    own = lax.dynamic_index_in_dim(x, me, 0, False)
    return Trip(own, sends, lambda parts: jnp.stack(ordered(parts, me)))


def bits_of(sizes):
    found = []
    for axis in ALL:
        bit = sizes[axis] // 2
        while bit:
            found.append((axis, bit))
            bit //= 2
    return found


def routes(sizes):
    own = lambda axis: [[b] for b in bits_of(sizes) if b[0] == axis]
    z = [[b for b in bits_of(sizes) if b[0] == "blk"]]
    y, x = own("hd"), own("rows")
    return z + y + x[:1] + x[1:], z + x[:1] + y + x[1:]


def partners(step, sizes):
    axis, low = step[0][0], step[-1][1]
    count = 2 ** len(step)
    place = (lax.axis_index(axis) // low) % count
    return axis, sizes[axis], place, [k * low for k in range(count)]


def gather_start(x, sizes):
    return x.reshape((1,) * len(bits_of(sizes)) + x.shape)


def gather_trip(cur, step, sizes):
    axis, size, place, offsets = partners(step, sizes)
    dim = bits_of(sizes).index(step[0])
    shape = cur.shape[:dim] + (2,) * len(step) + cur.shape[dim + len(step) :]
    sends = [(cur, axis, turned(size, k)) for k in offsets[1:]]
    return Trip(cur, sends, lambda parts: jnp.concatenate(ordered(parts, place), axis=dim).reshape(shape))


def gather_end(cur, sizes):
    lead = len(bits_of(sizes))
    return cur.reshape((-1,) + cur.shape[lead + 1 :])


def scatter_start(x, sizes):
    bits = bits_of(sizes)
    return [x.reshape((2,) * len(bits) + (x.shape[0] // 2 ** len(bits),) + x.shape[1:])]


def in_two(x):
    high = lax.reduce_precision(x, 8, 7)
    return jnp.concatenate([high, x - high], axis=-1)


def term_sum(terms, fine):
    total = terms[0].astype(F32)
    for term in terms[1:]:
        total = total + term.astype(F32)
    if fine:
        total = [total[..., : -2 * fine], total[..., -2 * fine : -fine] + total[..., -fine:]]
    return total


def scatter_trip(terms, step, sizes, fine=0):
    axis, size, place, offsets = partners(step, sizes)
    dim = bits_of(sizes).index(step[0])
    shape = terms[0].shape
    lead, rest = shape[:dim], shape[dim + len(step) :]
    merged = [term.reshape(lead + (len(offsets),) + rest) for term in terms]

    def part(k):
        picked = [lax.dynamic_index_in_dim(term, place ^ k, dim, True) for term in merged]
        if len(picked) == 1:
            return picked[0]
        total = term_sum(picked, fine)
        return (jnp.concatenate([total[0], in_two(total[1])], axis=-1) if fine else total).astype(BF16)

    sends = [(part(k), axis, turned(size, offset)) for k, offset in enumerate(offsets) if k]
    here = lead + (1,) * len(step) + rest
    return Trip(part(0), sends, lambda parts: [p.reshape(here) for p in parts])


def scatter_end(terms, sizes):
    return [term.reshape(term.shape[len(bits_of(sizes)) :]) for term in terms]


def dot(a, b, contract):
    return lax.dot_general(a, b, ((contract[:1], contract[1:]), ((), ())), preferred_element_type=F32)


def sine_cosine(x, scale):
    turns = jnp.round(x * (1.0 / math.pi))
    rest = (x - turns * 3.140625) - turns * 9.67653589793e-4
    half = turns * 0.5
    sign = scale - (4.0 * scale) * (half - jnp.floor(half))
    sq = rest * rest
    sine = sq * 2.600052801290691e-06 - 0.0001980661418962755
    sine = sine * sq + 0.008333017275116794
    sine = sine * sq - 0.16666657095676896
    sine = rest + rest * (sq * sine)
    cosine = sq * 2.319437094031874e-05 - 0.001385592644003374
    cosine = cosine * sq + 0.04166398934467621
    cosine = cosine * sq - 0.4999993228818705
    cosine = cosine * sq + 1.0
    return sine * sign, cosine * sign


def split_rows(x):
    high = x.astype(BF16).astype(F32)
    rest = x - high
    middle = rest.astype(BF16).astype(F32)
    return high, middle, rest - middle


def outer_sum(column, row):
    width = row.shape[1]
    place = lax.broadcasted_iota(jnp.int32, (AUG, width), 0)

    def lay(parts, first):
        out = jnp.zeros((AUG, width), F32)
        for i, part in enumerate(parts):
            out = jnp.where(place == first + i, part, out)
        return jnp.where((place >= 3 - first) & (place < 6 - first), 1.0, out).astype(BF16)

    return dot(lay(split_rows(column), 0), lay(split_rows(row), 3), (0, 0))


def augmented(v, ones):
    width = v.shape[1]
    place = lax.broadcasted_iota(jnp.int32, (AUG, width), 0)
    extra = jnp.where(place == 0, ones, 0.0)
    return jnp.concatenate([v.astype(F32), extra], axis=0)


def lower_mask(c):
    return lax.broadcasted_iota(jnp.int32, (c, c), 0) <= lax.broadcasted_iota(jnp.int32, (c, c), 1)


def gate_kernel(tile, heads, own_heads, shard, first_bias, small_ref, normed_ref, out_ref):
    raw = dot(small_ref[:, :128], normed_ref[...], (0, 0))[:heads].astype(BF16).astype(F32)
    groups = heads // own_heads
    block = small_ref[: groups * shard, :128].astype(F32)
    head = lax.broadcasted_iota(jnp.int32, (heads, 128), 0)
    lane = lax.broadcasted_iota(jnp.int32, (heads, 128), 1)
    bias = jnp.zeros((heads, 1), F32)
    for group in range(groups):
        wanted = False
        for part in range(3):
            wanted = wanted | (lane == first_bias + part * own_heads + head - group * own_heads)
        wanted = wanted & (head >= group * own_heads) & (head < (group + 1) * own_heads)
        bias = bias + jnp.sum(jnp.where(wanted, block[group * shard : group * shard + 1], 0.0), axis=1, keepdims=True)
    logit = raw + bias
    heads, width = logit.shape
    small = jnp.log1p(jnp.exp(-jnp.abs(logit)))
    keep = jnp.minimum(logit, 0.0) - small
    slow = jnp.minimum(-logit, 0.0) - small
    place = lax.broadcasted_iota(jnp.int32, (heads, width), 1)

    def sums(x, within):
        at = lax.rem(place, within)
        step = 1
        while step < within:
            x = x + jnp.where(at >= step, pltpu.roll(x, step, 1), 0.0)
            step *= 2
        return x

    running = sums(keep, tile)
    whole = running
    offset = jnp.zeros((heads, 1), F32)
    for at in range(0, width, tile):
        whole = jnp.where((place >= at) & (place < at + tile), running + offset, whole)
        offset = offset + running[:, at + tile - 1 : at + tile]
    for kind, value in enumerate(
        (running, slow - running, whole, jnp.exp(slow), jnp.exp(keep), jnp.broadcast_to(jnp.exp(offset), (heads, width)))
    ):
        for head in range(heads):
            out_ref[head, kind : kind + 1, :] = value[head : head + 1]


def first_kernel(per_row, qkv_ref, gate_ref, up_ref, *refs):
    *vectors, bias_ref, maps_ref, out_ref = refs
    shard, wide = qkv_ref.shape
    heads = gate_ref.shape[0]
    lane = lax.broadcasted_iota(jnp.int32, (shard, 128), 1)

    def column(ref, stride, first):
        n = ref.shape[0]
        value = jnp.broadcast_to(ref[...].astype(F32)[None, :], (shard, n))
        row_at = lax.broadcasted_iota(jnp.int32, (shard, n), 0)
        line_at = lax.broadcasted_iota(jnp.int32, (shard, n), 1)
        return jnp.sum(jnp.where(line_at == row_at * stride + first, value, 0.0), axis=1, keepdims=True)

    small = jnp.zeros((shard, 128), F32)
    columns = [column(up_ref, per_row, i) for i in range(per_row)] + [column(ref, 1, 0) for ref in vectors]
    for i, value in enumerate(columns):
        small = jnp.where(lane == heads + i, value, small)
    at = heads + len(columns)
    bias = jnp.broadcast_to(bias_ref[...][None, :], (shard, bias_ref.shape[0]))
    for part in split_rows(bias):
        for i in range(bias_ref.shape[0]):
            small = jnp.where(lane == at, part[:, i : i + 1], small)
            at += 1
    for i in range(heads):
        small = jnp.where(lane == i, column(gate_ref.at[i], 1, 0), small)
    out_ref[:, :wide] = qkv_ref[...]
    out_ref[:, wide : wide + 128] = small.astype(BF16)
    out_ref[:, wide + 128 :] = maps_ref[...]


def rest_kernel(out_ref_w, up_ref, down_ref, out_ref):
    shard, width = out_ref_w.shape
    out_ref[:shard] = out_ref_w[...]
    blocks = up_ref.shape[1] // width
    for i in range(blocks):
        out_ref[shard * (i + 1) : shard * (i + 2)] = up_ref[:, i * width : (i + 1) * width]
    out_ref[shard * (blocks + 1) :] = down_ref[...]


def last_kernel(per_row, heads, n_one, hd_ref, *refs):
    ones, twos, outs = refs[:n_one], refs[n_one : -10], refs[-10:]
    qkv_ref, gate_ref, bias_ref, out_ref, up_ref = outs[:5]
    half = qkv_ref.shape[1] // 2
    shard = qkv_ref.shape[0]
    one = sum(ref[...].astype(F32) for ref in ones)
    two = sum(ref[...].astype(F32) for ref in twos)
    fine = (two.shape[1] - half) // 2
    small = two[:, half : half + fine] + two[:, half + fine :]
    qkv_ref[:, :half] = one[:, :half]
    qkv_ref[:, half:] = two[:, :half]
    out_ref[...] = one[:, half:]
    row_at = lax.broadcasted_iota(jnp.int32, (shard, fine), 0)
    lane_at = lax.broadcasted_iota(jnp.int32, (shard, fine), 1)

    def line(n, stride, columns):
        row_at = lax.broadcasted_iota(jnp.int32, (shard, n), 0)
        line_at = lax.broadcasted_iota(jnp.int32, (shard, n), 1)
        value = jnp.zeros((shard, n), F32)
        for j, column in enumerate(columns):
            value = jnp.where(line_at == row_at * stride + j, column, value)
        return jnp.sum(value, axis=0)

    up_ref[...] = line(shard * per_row, per_row, [small[:, heads + j : heads + j + 1] for j in range(per_row)])
    for i, ref in enumerate(outs[5:]):
        at = heads + per_row + i
        ref[...] = line(shard, 1, [small[:, at : at + 1]])
    for i in range(heads):
        gate_ref[i] = line(shard, 1, [small[:, i : i + 1]])
    own = bias_ref.shape[0]
    first = heads + per_row + 5 + hd_ref[0] * own
    column = jnp.sum(jnp.where(lane_at == first + row_at, small, 0.0), axis=1, keepdims=True)
    bias_ref[...] = line(own, 1, [column])


def ends_kernel(hd_ref, start_ref, final_ref, *outs):
    size = outs[0].shape[2]
    for ref, state_ref, key_ref in ((start_ref, *outs[:2]), (final_ref, *outs[2:])):
        for head in range(ref.shape[1]):
            rows = ref[0, head].astype(F32)
            state_ref[0, head] = rows[:size]
            key_ref[0, head : head + 1] = rows[size : size + 1]


def features(unit, fmt, scale):
    sine, cosine = sine_cosine(dot(fmt, unit, (1, 0)), scale)
    return jnp.concatenate([sine, cosine], axis=0).astype(BF16)


def forward_kernel(tile, qkv_ref, fmt_ref, rows_ref, qf_ref, kf_ref, nu_ref, state_ref):
    width = qkv_ref.shape[-1]
    fmt = fmt_ref[0]
    scale = 1.0 / math.sqrt(fmt.shape[0])
    mask = lower_mask(tile)
    state = None
    for at in range(0, width, tile):
        here = pl.ds(at, tile)
        query = qkv_ref[0, 0, :, here].astype(F32)
        key = qkv_ref[0, 1, :, here].astype(F32)
        query = (query * lax.rsqrt(jnp.sum(query * query, axis=0, keepdims=True) + 1e-06)).astype(BF16)
        key = (key * lax.rsqrt(jnp.sum(key * key, axis=0, keepdims=True) + 1e-06)).astype(BF16)
        qf = features(query, fmt, scale)
        kf = features(key, fmt, scale)
        qf_ref[0, :, here] = qf
        kf_ref[0, :, here] = kf
        running = rows_ref[0, 0:1, here]
        lead = rows_ref[0, 1:2, here]
        last = running[:, tile - 1 : tile]
        values = augmented(qkv_ref[0, 2, :, here], 1.0)
        weights = jnp.where(mask, jnp.exp(outer_sum(lead, running)), 0.0)
        scores = (dot(kf, qf, (0, 0)) * weights).astype(BF16)
        numer = dot(values.astype(BF16), scores, (1, 0))
        if state is not None:
            numer = numer + jnp.exp(running) * dot(state.astype(BF16), qf, (1, 0))
        nu_ref[0, :, here] = numer[: nu_ref.shape[1]]
        tail = (values * jnp.exp(last + lead)).astype(BF16)
        new = dot(tail, kf, (1, 1))
        state = new if state is None else jnp.exp(last) * state + new
    state_ref[0] = state[: state_ref.shape[1]]


def enter_kernel(state_ref, qf_ref, rows_ref, nu_ref, mixed_ref, total_ref):
    state = padded(state_ref[0])
    high = state.astype(BF16)
    rest = (state - high.astype(F32)).astype(BF16)
    qf = qf_ref[0]
    rows = nu_ref.shape[1]
    extra = (dot(high, qf, (1, 0)) + dot(rest, qf, (1, 0)))[:rows]
    total = nu_ref[0] + jnp.exp(rows_ref[0, 2:3, :]) * extra
    total_ref[0] = total
    size = mixed_ref.shape[1]
    denom = total[size : size + 1]
    floor = softplus(4.0 * denom) * 0.25 + 0.1
    mixed_ref[0] = (total[:size] / floor).astype(BF16)


def padded(state):
    return jnp.concatenate([state, jnp.zeros((AUG - ROWS, state.shape[1]), F32)], axis=0)


def softplus(x):
    return jnp.maximum(x, 0.0) + jnp.log1p(jnp.exp(-jnp.abs(x)))


def leave_kernel(grad_ref, total_ref, qf_ref, rows_ref, a_ref, back_ref):
    grad = grad_ref[0].astype(F32)
    size = grad.shape[0]
    numer = total_ref[0, :size]
    denom = total_ref[0, size : size + 1]
    inverse = 1.0 / (softplus(4.0 * denom) * 0.25 + 0.1)
    inner = jnp.sum(grad * numer, axis=0, keepdims=True)
    by_denom = -inner * jax.nn.sigmoid(4.0 * denom) * inverse * inverse
    whole = augmented(grad * inverse, by_denom)
    a_ref[0] = whole.astype(BF16)
    back = dot((whole * jnp.exp(rows_ref[0, 2:3, :])).astype(BF16), qf_ref[0], (1, 1))
    back_ref[0] = back[: back_ref.shape[1]]


def unit_back(raw, unit_grad):
    inverse = lax.rsqrt(jnp.sum(raw * raw, axis=0, keepdims=True) + 1e-06)
    inner = jnp.sum(raw * unit_grad, axis=0, keepdims=True)
    return inverse * (unit_grad - raw * (inner * inverse * inverse))


def angle_back(feat, grad):
    half = feat.shape[0] // 2
    feat = feat.astype(F32)
    return (grad[:half] * feat[half:] - grad[half:] * feat[:half]).astype(BF16)


def backward_kernel(
    tile, qkv_ref, fm_ref, rows_ref, qf_ref, kf_ref, a_ref, state_ref, back_ref, out_ref, logit_ref
):
    width = qkv_ref.shape[-1]
    size = qkv_ref.shape[2]
    fm = fm_ref[0]
    mask = lower_mask(tile)
    spots = list(range(0, width, tile))
    states = [padded(state_ref[0])]
    for at in spots:
        here = pl.ds(at, tile)
        last = rows_ref[0, 0:1, at + tile - 1 : at + tile]
        values = augmented(qkv_ref[0, 2, :, here], 1.0)
        tail = (values * jnp.exp(last + rows_ref[0, 1:2, here])).astype(BF16)
        states.append(jnp.exp(last) * states[-1] + dot(tail, kf_ref[0, :, here], (1, 1)))
    back = padded(back_ref[0])
    ones = jnp.ones((AUG, tile), BF16)

    def whole_sum(x):
        return jnp.sum(jnp.sum(x, axis=0, keepdims=True), axis=1, keepdims=True)

    pieces = []
    for index in reversed(range(len(spots))):
        at = spots[index]
        here = pl.ds(at, tile)
        running = rows_ref[0, 0:1, here]
        lead = rows_ref[0, 1:2, here]
        last = running[:, tile - 1 : tile]
        decay = jnp.exp(running)
        tail = jnp.exp(last + lead)
        qf = qf_ref[0, :, here]
        kf = kf_ref[0, :, here]
        a = a_ref[0, :, here]
        values = augmented(qkv_ref[0, 2, :, here], 1.0).astype(BF16)
        state = states[index].astype(BF16)
        low_back = back.astype(BF16)
        weights = jnp.where(mask, jnp.exp(outer_sum(lead, running)), 0.0)
        alike = dot(kf, qf, (0, 0))
        scores = (alike * weights).astype(BF16)
        pairs = dot(values, a, (0, 0)) * weights
        terms = (pairs * alike).astype(BF16)
        pairs = pairs.astype(BF16)
        from_state = decay * dot(state, a, (0, 0))
        from_back = tail * dot(low_back, values, (0, 0))
        query_feat = dot(kf, pairs, (1, 0)) + from_state
        key_feat = dot(qf, pairs, (1, 1)) + from_back
        by_query = dot(ones, terms, (1, 0))[:1]
        by_key = dot(ones, terms, (1, 1))[:1]
        state_term = jnp.sum(qf.astype(F32) * from_state, axis=0, keepdims=True)
        back_term = jnp.sum(kf.astype(F32) * from_back, axis=0, keepdims=True)
        through = jnp.exp(last) * whole_sum(back * states[index])
        constant = jnp.sum(back_term, axis=1, keepdims=True) + through
        pieces.append((by_query - by_key + state_term - back_term, by_key + back_term, constant))
        value = dot(a[:size], scores, (1, 1)) + tail * dot(low_back[:size], kf, (1, 0))
        query_unit = dot(fm, angle_back(qf, query_feat), (1, 0))
        key_unit = dot(fm, angle_back(kf, key_feat), (1, 0))
        out_ref[0, 0, :, here] = unit_back(qkv_ref[0, 0, :, here].astype(F32), query_unit).astype(BF16)
        out_ref[0, 1, :, here] = unit_back(qkv_ref[0, 1, :, here].astype(F32), key_unit).astype(BF16)
        out_ref[0, 2, :, here] = value.astype(BF16)
        back = jnp.exp(last) * back + dot((a.astype(F32) * decay).astype(BF16), qf, (1, 1))
    place = lax.broadcasted_iota(jnp.int32, (ROWS, tile), 0)
    sums = jnp.zeros((ROWS, tile), F32)
    for index, piece in enumerate(pieces[::-1]):
        sums = jnp.where(place == index, piece[0], sums)
    place = lax.broadcasted_iota(jnp.int32, (ROWS, tile), 1)
    step = 1
    while step < tile:
        sums = sums + jnp.where(place < tile - step, pltpu.roll(sums, tile - step, 1), 0.0)
        step *= 2
    for index, (_, by_key, constant) in enumerate(pieces[::-1]):
        here = pl.ds(spots[index], tile)
        keep_grad = sums[index : index + 1] + constant
        logit = keep_grad * rows_ref[0, 3:4, here] - by_key * rows_ref[0, 4:5, here]
        logit_ref[0, :, here] = jnp.broadcast_to(logit, (ROWS, tile))


def per_head(kernel, outs, heads, *arrays, us, far=(), group=4):
    def spec(shape, offset):
        rest = len(shape) - 1
        return pl.BlockSpec((group,) + tuple(shape[1:]), lambda h: (h + offset // group,) + (0,) * rest)

    def grouped(*refs):
        for i in range(group):
            kernel(*[ref.at[pl.ds(i, 1)] for ref in refs])

    nbytes = sum(heads * math.prod(a.shape[1:]) * a.dtype.itemsize for a, _ in arrays)
    nbytes += sum(math.prod(s) * jnp.dtype(d).itemsize for s, d in outs)
    return pl.pallas_call(
        grouped,
        grid=(heads // group,),
        in_specs=[spec(a.shape, offset) for a, offset in arrays],
        out_specs=[spec(s, 0) for s, _ in outs],
        out_shape=[jax.ShapeDtypeStruct(s, d) if i not in far else pltpu.HBM(s, d) for i, (s, d) in enumerate(outs)],
        compiler_params=pltpu.CompilerParams(vmem_limit_bytes=24 * 2**20),
        cost_estimate=pl.CostEstimate(flops=int(us * 1.1e9), bytes_accessed=int(nbytes), transcendentals=0),
    )(*[a for a, _ in arrays])


def norm_parts(x):
    average = jnp.mean(x, axis=0, keepdims=True)
    centered = x - average
    inverse = lax.rsqrt(jnp.mean(centered * centered, axis=0, keepdims=True) + 1e-05)
    return centered * inverse, inverse


def norm_back(hat, inverse, gain, grad):
    scaled = grad * gain
    first = jnp.mean(scaled, axis=0, keepdims=True)
    second = jnp.mean(scaled * hat, axis=0, keepdims=True)
    return (scaled - first - hat * second) * inverse


def product(spec, a, b):
    return jnp.einsum(spec, a, b, preferred_element_type=F32)


def local(
    tokens, w_qkv, w_gate, gate_bias, w_out, w_up, up_bias, w_down, down_bias, pre_gain, pre_shift,
    mid_gain, mid_shift, feature_map, state_init, keysum_init, out_cot, state_cot, keysum_cot,
):
    sizes = {axis: lax.axis_size(axis) for axis in ALL}
    count_hd, count_blk = sizes["hd"], sizes["blk"]
    devices = sizes["rows"] * count_blk * count_hd
    both = count_blk * count_hd
    seqs, part, width = tokens.shape
    own_heads, head_dim, rand = feature_map.shape
    heads = own_heads * count_hd
    feat = 2 * rand
    hidden_size = w_up.shape[1]
    length = seqs * part
    tile = 256 if length % 256 == 0 else 128
    shard = w_qkv.shape[0]
    aug, held_rows = head_dim + AUG, head_dim + ROWS
    place_hd, place_blk = lax.axis_index("hd"), lax.axis_index("blk")
    place = place_blk * count_hd + place_hd
    member, chunk = place % seqs, place // seqs
    chunks = both // seqs

    def to_chunk(x):
        return pieces_trip(x, BOTH, both, seqs, member)

    def from_chunk(x):
        return pieces_trip(x.reshape(seqs, part, width), BOTH, both, seqs, member)

    per_row = hidden_size // width
    n_small = heads + per_row + 5
    shares = devices // count_hd
    maps = feature_map.reshape(shares, shard, -1)
    spot = lax.axis_index("rows") * count_blk + place_blk
    maps = lax.dynamic_index_in_dim(maps, spot, 0, False)
    first_packed = pl.pallas_call(
        functools.partial(first_kernel, per_row),
        out_shape=jax.ShapeDtypeStruct((shard, 3 * width + 128 + maps.shape[1]), BF16),
    )(w_qkv, w_gate.T, up_bias, down_bias, pre_gain, pre_shift, mid_gain, mid_shift, gate_bias, maps)

    half = 3 * width // 2
    one, two = routes(sizes)
    stages = range(len(one))

    def gathers(streams, at):
        return [gather_trip(cur, route[at], sizes) for cur, route in zip(streams, (one, two))]

    whole = gather_trip(gather_start(first_packed, sizes), one[0], sizes).land()
    first = [whole[..., :half], whole[..., half:]]
    tokens_trip = to_chunk(after(tokens, *first))
    second = pl.pallas_call(
        rest_kernel, out_shape=jax.ShapeDtypeStruct((shard * (per_row + 1) + w_down.shape[0], width), BF16)
    )(*after((w_out, w_up, w_down), first_packed))
    second = lax.all_gather(second, ALL, axis=0)

    at_start = chunk == 0
    at_end = chunk == chunks - 1
    offers = []
    for other in range(count_hd):
        spot = place_blk * count_hd + other
        pick = lambda a: lax.dynamic_index_in_dim(a, spot % seqs, 0, False)
        state = jnp.where(spot // seqs == 0, pick(state_init), pick(state_cot))
        keysum = jnp.where(spot // seqs == 0, pick(keysum_init), pick(keysum_cot))
        keysum = jnp.pad(keysum[:, None], ((0, 0), (0, ROWS - 1), (0, 0)))
        offers.append(jnp.concatenate([jnp.swapaxes(state, -1, -2), keysum], axis=1))
    offers = after(jnp.stack(offers), *first)

    cut = len(one) - len([b for b in bits_of(sizes) if b[0] == "rows"]) + 1
    for at in stages[1:]:
        first = landed(gathers(first, at))
        if at == cut - 1:
            edge_trip = pieces_trip(after(offers, *first), "hd", count_hd, count_hd, place_hd)
    qkv_halves = [gather_end(f, sizes) for f in first]
    full_small = qkv_halves[1][:, half:]
    qkv_halves[1] = qkv_halves[1][:, :half]
    full_gate = full_small[:, :heads]
    full_up_bias = full_small[:, heads : heads + per_row].reshape(hidden_size, 1).astype(F32)
    vectors = [full_small[:, heads + per_row + i : heads + per_row + i + 1].astype(F32) for i in range(5)]
    full_down_bias, gain_1, shift_1, gain_2, shift_2 = vectors
    maps = full_small[:, -maps.shape[1] :].reshape(shares, count_hd, shard, -1)
    fm = maps.transpose(1, 0, 2, 3).reshape(heads, head_dim, rand)
    fmt = fm.transpose(0, 2, 1)

    def hop_trip(added, forward):
        pairs = [(i, i + seqs) for i in range(both - seqs)]
        pairs = pairs if forward else [(b, a) for a, b in pairs]
        outer = at_start if forward else at_end
        choose = lambda parts: jnp.where(outer, edge, parts[1].astype(F32))
        state = edge
        for last in range(chunks - 1):
            trip = Trip(None, [((added + decay * state).astype(BF16), BOTH, pairs)], choose)
            if last < chunks - 2:
                state = trip.land()
        return trip

    x = tokens_trip.land().reshape(length, width).T.astype(F32)
    hat_1, inverse_1 = norm_parts(x)
    normed = (hat_1 * gain_1 + shift_1).astype(BF16)
    rows = pl.pallas_call(
        functools.partial(gate_kernel, tile, heads, own_heads, shard, n_small),
        out_shape=jax.ShapeDtypeStruct((heads, ROWS, length), F32),
        compiler_params=pltpu.CompilerParams(vmem_limit_bytes=24 * 2**20),
    )(full_small, normed)
    packed = product("dc,dt->ct", jnp.concatenate(qkv_halves, axis=1), normed)
    packed = packed.astype(BF16).reshape(heads, 3, head_dim, length)
    decay = rows[:, 5:6, :1]

    cot_trip = to_chunk(after(out_cot, normed))
    qf, kf, partial_nu, chunk_state = per_head(
        functools.partial(forward_kernel, tile),
        [
            ((heads, feat, length), BF16),
            ((heads, feat, length), BF16),
            ((heads, held_rows, length), F32),
            ((heads, held_rows, feat), F32),
        ],
        heads, (packed, 0), (departed(fmt, cot_trip, edge_trip), 0), (rows, 0), us=18, far=(0, 1),
    )
    edge = edge_trip.land(chunk_state).reshape(heads, held_rows, feat)
    hop = hop_trip(chunk_state, True)
    cot = cot_trip.land(hop.messages()).reshape(length, width).T
    second = after(second, hop.messages())
    full_out = second[:, :shard].reshape(width, width)
    full_up = [second[:, i : i + shard].reshape(width, width) for i in range(shard, shard * (per_row + 1), shard)]
    full_up = jnp.concatenate(full_up, axis=1)
    full_down = second[:, shard * (per_row + 1) :].reshape(hidden_size, width)
    entering = hop.land(cot, full_out, full_up, full_down)
    mixed, total_nu = per_head(
        enter_kernel,
        [((heads, head_dim, length), BF16), ((heads, held_rows, length), F32)],
        heads, (entering, 0), (qf, 0), (rows, 0), (partial_nu, 0), us=3, group=heads,
    )
    mixed = mixed.reshape(width, length)

    attended = x + product("io,it->ot", full_out, mixed)
    hat_2, inverse_2 = norm_parts(attended)
    hidden = (hat_2 * gain_2 + shift_2).astype(BF16)
    before = product("df,dt->ft", full_up, hidden) + full_up_bias
    cumulative = 0.5 + 0.5 * lax.erf(before * math.sqrt(0.5))
    density = jnp.exp(-0.5 * before * before) * (1.0 / math.sqrt(2.0 * math.pi))
    active = (before * cumulative).astype(BF16)
    before_grad = (product("fo,ot->ft", full_down, cot) * (cumulative + before * density)).astype(BF16)
    hidden_grad = product("df,ft->dt", full_up, before_grad)
    cot_full = cot.astype(F32)
    attended_grad = cot_full + norm_back(hat_2, inverse_2, gain_2, hidden_grad)
    attended_low = attended_grad.astype(BF16)
    mixed_grad = product("io,ot->it", full_out, attended_low).astype(BF16).reshape(heads, head_dim, length)

    a, chunk_back = per_head(
        leave_kernel,
        [((heads, aug, length), BF16), ((heads, held_rows, feat), F32)],
        heads, (mixed_grad, 0), (total_nu, 0), (qf, 0), (rows, 0), us=3, group=heads,
    )
    hop = hop_trip(chunk_back, False)

    def scatters(streams, at):
        return [scatter_trip(cur, route[at], sizes) for cur, route in zip(streams, (one, two))]

    held = departed(hidden, hop)
    up_grad = product("dt,ft->df", held, before_grad).astype(BF16)
    down_grad = product("ft,ot->fo", active, cot).astype(BF16)
    early = [scatter_start(up_grad, sizes), scatter_start(down_grad, sizes)]
    early_trips = scatters(early, len(one) - 1)
    result = attended + product("fo,ft->ot", departed(full_down, *early_trips), active) + full_down_bias
    result = result.astype(BF16)
    out_grad = product("it,ot->io", mixed, attended_low).astype(BF16)
    early = landed(early_trips, result)
    for at in stages[-2 : cut - 1 : -1]:
        early = landed(scatters(early, at))
    output_trip = from_chunk(result.T)
    back = hop.land(result)
    ones = jnp.ones((length, 128), BF16)
    down_bias_grad = product("ot,tn->on", cot, ones)[:, :1]
    up_bias_grad = product("ft,tn->fn", before_grad, ones)[:, 0]
    gain_2_grad = jnp.sum(hidden_grad * hat_2, axis=1, keepdims=True)
    shift_2_grad = jnp.sum(hidden_grad, axis=1, keepdims=True)

    added = jnp.where(at_start, chunk_back, chunk_state)
    ends = (added + decay * jnp.where(at_start, back, entering)).astype(BF16)
    ends = lax.all_gather(ends, BOTH, axis=0)

    own = heads // 2

    def backward(i, fm):
        grad, logit = per_head(
            functools.partial(backward_kernel, tile),
            [((own, 3, head_dim, length), BF16), ((own, ROWS, length), F32)],
            own, (packed, i * own), (fm, i * own), (rows, i * own), (qf, i * own), (kf, i * own),
            (a, i * own), (entering, i * own), (back, i * own), us=9,
        )
        return grad.reshape(half, length), logit[:, 0]

    early_trips = scatters(early, cut - 1)
    grads = [backward(0, departed(fm, output_trip, *early_trips))]
    early = landed(early_trips, grads[0])
    output = output_trip.land(grads[0])
    for at in stages[cut - 2 : 1 : -1]:
        early = landed(scatters(early, at))
    early_trips = scatters(early, 1)
    qkv_grad = [product("dt,ct->dc", normed, grads[0][0]).astype(BF16)]
    late_one = scatter_start(jnp.concatenate([qkv_grad[0], out_grad], axis=1), sizes)
    late_trip = scatter_trip(late_one, one[-1], sizes)
    grads.append(backward(1, departed(fm, late_trip, *early_trips)))
    late_one = late_trip.land(grads[1])
    late_trip = scatter_trip(late_one, one[-2], sizes)

    gate_low = jnp.concatenate([g[1] for g in grads])
    bias_grad = jnp.sum(gate_low, axis=1)
    gate_low = gate_low.astype(BF16)
    last_grad = departed(grads[1][0], late_trip)
    normed_grad = (
        product("dc,ct->dt", qkv_halves[0], grads[0][0])
        + product("dc,ct->dt", qkv_halves[1], last_grad)
        + product("dh,ht->dt", full_gate, gate_low)
    )
    qkv_grad.append(product("dt,ct->dc", normed, last_grad).astype(BF16))
    gate_grad = product("dt,ht->dh", normed, gate_low)
    gain_1_grad = jnp.sum(normed_grad * hat_1, axis=1, keepdims=True)
    shift_1_grad = jnp.sum(normed_grad, axis=1, keepdims=True)
    grad_small = jnp.concatenate(
        [gate_grad, up_bias_grad.reshape(width, per_row)]
        + [down_bias_grad, gain_1_grad, shift_1_grad, gain_2_grad, shift_2_grad]
        + [jnp.broadcast_to(bias_grad[None], (width, heads))],
        axis=1,
    )
    fine = grad_small.shape[1] + -grad_small.shape[1] % 128
    grad_small = in_two(jnp.pad(grad_small, ((0, 0), (0, fine - grad_small.shape[1])))).astype(BF16)
    late_two = scatter_start(jnp.concatenate([qkv_grad[1], grad_small], axis=1), sizes)
    other_trip = scatter_trip(late_two, two[-1], sizes, fine=fine)
    early_trips = scatters(landed(early_trips, other_trip.messages()), 0)
    held = departed(inverse_1, other_trip, *early_trips)
    token_grad = (attended_grad + norm_back(hat_1, held, gain_1, normed_grad)).astype(BF16)
    late_two = other_trip.land(token_grad)
    other_trip = scatter_trip(late_two, two[-2], sizes, fine=fine)
    late_one = late_trip.land(other_trip.messages())
    late_trip = scatter_trip(late_one, one[-3], sizes)
    early = landed(early_trips, late_trip.messages())
    up_own, down_own = (term_sum(scatter_end(e, sizes), 0) for e in early)
    token_grad = departed(token_grad, late_trip).T
    late_two = other_trip.land(up_own, down_own)
    for step in two[-3:1:-1]:
        late_two = scatter_trip(late_two, step, sizes, fine=fine).land()
    other_trip = scatter_trip(late_two, two[1], sizes, fine=fine)
    late_one = late_trip.land(other_trip.messages())
    for step in one[-4:0:-1]:
        late_one = scatter_trip(late_one, step, sizes).land()
    late_trip = scatter_trip(late_one, one[0], sizes)
    tokens_trip = from_chunk(departed(token_grad, late_trip))
    late_two = other_trip.land(tokens_trip.messages())
    other_trip = scatter_trip(late_two, two[0], sizes, fine=fine)
    ends = after(ends, tokens_trip.messages())
    index = lax.convert_element_type(place_hd, jnp.int32).reshape(1)
    shapes = [(seqs, own_heads, head_dim, feat), (seqs, own_heads, feat)]
    out_specs = [
        pl.BlockSpec((1,) + shapes[0][1:], lambda m, hd: (m, 0, 0, 0)), pl.BlockSpec((1,) + shapes[1][1:], lambda m, hd: (m, 0, 0))
    ]
    block = (1, own_heads, held_rows, feat)
    states = pl.pallas_call(
        ends_kernel,
        grid_spec=pltpu.PrefetchScalarGridSpec(
            num_scalar_prefetch=1,
            grid=(seqs,),
            in_specs=[
                pl.BlockSpec(block, lambda m, hd: (m, hd[0], 0, 0)),
                pl.BlockSpec(block, lambda m, hd: (m + both - seqs, hd[0], 0, 0)),
            ],
            out_specs=out_specs * 2,
        ),
        out_shape=[jax.ShapeDtypeStruct(shape, F32) for shape in shapes * 2],
        compiler_params=pltpu.CompilerParams(vmem_limit_bytes=24 * 2**20),
    )(index, ends, ends)
    state_start, keysum_start, state_final, keysum_final = states
    state_start, state_final = jnp.swapaxes(state_start, -1, -2), jnp.swapaxes(state_final, -1, -2)
    late_one, late_two = (scatter_end(e, sizes) for e in landed([late_trip, other_trip], *states))
    token_grad = tokens_trip.land(*states)
    shapes = [
        (shard, 3 * width), (heads, shard), (own_heads,), (shard, width), (shard * per_row,),
        *[(shard,)] * 5,
    ]
    in_vmem = [pl.BlockSpec(memory_space=pltpu.VMEM)]
    qkv_own, gate_own, bias_own, out_own, up_bias_own, down_bias_own, gain_1_own, shift_1_own, gain_2_own, shift_2_own = (
        pl.pallas_call(
            functools.partial(last_kernel, per_row, heads, len(late_one)),
            in_specs=[pl.BlockSpec(memory_space=pltpu.SMEM)] + in_vmem * (len(late_one) + len(late_two)),
            out_specs=in_vmem * len(shapes),
            out_shape=[jax.ShapeDtypeStruct(shape, F32) for shape in shapes],
        )(index, *late_one, *late_two)
    )
    return (
        output, token_grad, qkv_own, gate_own.T, bias_own, out_own, up_own, up_bias_own, down_own, down_bias_own,
        gain_1_own, shift_1_own, gain_2_own, shift_2_own, state_final, keysum_final, state_start, keysum_start,
    )


def solution(mesh):
    by_tokens = P("rows", ("blk", "hd"), None)
    by_rows = P(ALL, None)
    by_entry = P(ALL)
    by_head = P("hd")
    by_state = P("rows", "hd", None, None)
    by_keysum = P("rows", "hd", None)
    in_specs = (
        by_tokens, by_rows, by_rows, by_head, by_rows, by_rows, by_entry, by_rows, by_entry, by_entry, by_entry,
        by_entry, by_entry, P("hd", None, None), by_state, by_keysum, by_tokens, by_state, by_keysum,
    )
    out_specs = (
        by_tokens, by_tokens, by_rows, by_rows, by_head, by_rows, by_rows, by_entry, by_rows, by_entry,
        by_entry, by_entry, by_entry, by_entry, by_state, by_keysum, by_state, by_keysum,
    )
    return jax.shard_map(local, mesh=mesh, in_specs=in_specs, out_specs=out_specs, check_vma=False)
```
